32 devices in a mesh: sec: 2 (over x), sp: 8 (over z, y), dp: 2 (over core).
Axes of the slice: x: 2, y: 2, z: 4, core: 2. Of those that a mesh axis runs over, the one named last changes fastest.
Arguments:
- block_data: bfloat16 [2, 2, 5, 8, 32, 512], P('sec', 'dp', None, 'sp'), may hold values from -6 to 6
- code_index: int32 [2, 6, 5, 8, 32], P('dp', None, None, 'sp'), may hold values from 0 to 7, as said below
- levels: int32 [6], replicated, may hold values from 3 to 8, as said below
- w_space: bfloat16 [2, 9, 512, 512], P('sec', None, 'sp'), may hold values from -0.09375 to 0.09375
- w_time: bfloat16 [2, 3, 512, 512], P('sec', None, 'sp'), may hold values from -0.15625 to 0.15625
- enc_proj: bfloat16 [6, 512], replicated, may hold values from -0.25 to 0.25
- dec_proj: bfloat16 [6, 512], replicated, may hold values from -2.5 to 2.5
Outputs:
- space_grad: float32 [2, 9, 512, 512], P('sec', None, 'sp')
- time_grad: float32 [2, 3, 512, 512], P('sec', None, 'sp')
- proj_grad: float32 [2, 6, 512], P('sec')
The draws below stay inside these ranges and needn't reach their ends.
Inputs may be any that keep to these rules, and one draw needn't show every extreme that they name: levels[l] is the number of code levels of latent dimension l; 3 and 8 both occur. code_index[b, l, t, r, c] is below levels[l].
All inputs are finite; a program needn't handle non-finite values.
Results may differ from the reference program's by a relative error of at most 0.0055.
Values may be sent and summed in bfloat16 or wider, within the bound.
No kernel may reach another device: no remote copies, remote signals or barrier semaphores. Data moves between devices by JAX's collectives and lax.ppermute only.
A program may use at most 128 MiB of HBM per device.

```python
import jax
import jax.numpy as jnp
from jax import lax

C = 512
LAT = 6
FR = 5
COLS = 32
H = 8
CLIPS = 2


def level_table(key):
    base_key = jax.random.fold_in(key, 7)
    others = jax.random.randint(jax.random.fold_in(base_key, 1), (LAT - 2,), 3, 9).astype(jnp.int32)
    ordered = jnp.concatenate([jnp.array([3, 8], jnp.int32), others])
    shuffle = jax.random.permutation(jax.random.fold_in(base_key, 2), LAT)
    return ordered[shuffle]


def draw_levels(key, part):
    return level_table(key)


def draw_code_index(key, part):
    level_row = level_table(key)
    upper = level_row[None, :, None, None, None]
    return jax.random.randint(jax.random.fold_in(key, 11), (CLIPS, LAT, FR, H, COLS), 0, upper).astype(jnp.int32)


def with_spikes(values, key, source, target, blocks, factor):
    def block_of(position):
        return (jnp.arange(values.shape[position]) // (values.shape[position] // blocks)).reshape((-1,) + (1,) * (values.ndim - 1 - position))

    first = jax.random.permutation(key, blocks)[block_of(target)]
    other_side = (block_of(target) + blocks // 2) % blocks
    return jnp.where((block_of(source) == first) | (block_of(source) == other_side), factor * values, values)


def level_of(stream_key, shape, cuts, low, largest):
    loudness, own = 1.0, jax.random.fold_in(stream_key, 6)
    for axis_at, blocks in cuts:
        heights = jnp.exp(jax.random.uniform(jax.random.fold_in(own, axis_at), (blocks,), jnp.float32, low / len(cuts), largest / len(cuts)))
        loudness = loudness * jnp.repeat(heights, shape[axis_at] // blocks).reshape([-1 if axis == axis_at else 1 for axis in range(len(shape))])
    return loudness


def scatter_about(key, dims, scale, reach, cuts=(), dtype=jnp.bfloat16):
    values = scale * jax.random.normal(key, dims, jnp.float32)
    if cuts:
        values = values * level_of(key, dims, cuts, -0.22, 0.18)
    return jnp.clip(values, -reach, reach).astype(dtype)


def noise_with(rng, extent, spread, limit, cuts, heavy, kind=jnp.bfloat16):
    values = spread * jax.random.normal(rng, extent, jnp.float32)
    if cuts:
        values = values * level_of(rng, extent, cuts, -0.22, 0.18)
    return jnp.clip(with_spikes(values, jax.random.fold_in(rng, 3), *heavy), -limit, limit).astype(kind)


def setup_inputs(seed: int = 0) -> dict:
    streams_of = jax.random.split(jax.random.key(seed), 8)
    return {
        "block_data": noise_with(streams_of[0], (2, CLIPS, FR, H, COLS, C), 1.0, 6.0, ((0, 2), (1, 2), (3, 8)), (3, 5, 8, 2.0)),
        "code_index": draw_code_index(jax.random.fold_in(streams_of[7], 71), 0),
        "levels": draw_levels(jax.random.fold_in(streams_of[7], 71), 0),
        "w_space": scatter_about(streams_of[3], (2, 9, C, C), (9 * C) ** -0.5, 0.09375, ((0, 2), (2, 8))),
        "w_time": scatter_about(streams_of[4], (2, 3, C, C), (3 * C) ** -0.5, 0.15625, ((0, 2), (2, 8))),
        "enc_proj": scatter_about(streams_of[5], (LAT, C), C ** -0.5, 0.25),
        "dec_proj": scatter_about(streams_of[6], (LAT, C), LAT ** -0.5, 2.5),
    }


HIGH = lax.Precision.HIGHEST

def latent_values(code_index, levels):
    half_width = (levels.astype(jnp.float32) - 1.0) * 0.5
    half_width = half_width[None, :, None, None, None]
    return jnp.moveaxis((code_index.astype(jnp.float32) - half_width) / half_width, 1, -1)

def silu_slope(inputs):
    logistic = jax.nn.sigmoid(inputs)
    return logistic * (1.0 + inputs * (1.0 - logistic))

def flat_dot(operand, matrix):
    leading = operand.shape[:-1]
    flat = jnp.dot(operand.reshape(-1, operand.shape[-1]), matrix, preferred_element_type=jnp.float32)
    return flat.reshape(leading + (matrix.shape[-1],))

def high_dot(operand, matrix):
    leading = operand.shape[:-1]
    flat = jnp.dot(operand.reshape(-1, operand.shape[-1]), matrix, precision=HIGH, preferred_element_type=jnp.float32)
    return flat.reshape(leading + (matrix.shape[-1],))

def space_apply(padded, kernel, row_count, col_count):
    summed = jnp.zeros(padded.shape[:2] + (row_count, col_count, kernel.shape[2]), jnp.float32)
    for tap_index in range(9):
        row_off, col_off = (tap_index // 3, tap_index % 3)
        window = padded[:, :, row_off:row_off + row_count, col_off:col_off + col_count]
        summed = summed + flat_dot(window, kernel[tap_index])
    return summed

def space_transpose(padded, kernel, row_count, col_count):
    summed = jnp.zeros(padded.shape[:2] + (row_count, col_count, kernel.shape[1]), jnp.float32)
    for tap_index in range(9):
        row_off, col_off = (tap_index // 3, tap_index % 3)
        window = padded[:, :, 2 - row_off:2 - row_off + row_count, 2 - col_off:2 - col_off + col_count]
        summed = summed + flat_dot(window, kernel[tap_index].T)
    return summed

def time_apply(inputs, kernel):
    frame_count = inputs.shape[1]
    padded = jnp.pad(inputs, ((0, 0), (2, 0), (0, 0), (0, 0), (0, 0)))
    summed = jnp.zeros(inputs.shape[:-1] + (kernel.shape[2],), jnp.float32)
    for lag_index in range(3):
        summed = summed + flat_dot(padded[:, 2 - lag_index:2 - lag_index + frame_count], kernel[lag_index])
    return summed

def time_transpose(gradient, kernel):
    frame_count = gradient.shape[1]
    padded = jnp.pad(gradient, ((0, 0), (0, 2), (0, 0), (0, 0), (0, 0)))
    summed = jnp.zeros(gradient.shape[:-1] + (kernel.shape[1],), jnp.float32)
    for lag_index in range(3):
        summed = summed + flat_dot(padded[:, lag_index:lag_index + frame_count], kernel[lag_index].T)
    return summed

def space_kernel_grad(padded, gradient, row_count, col_count):
    flat_grad = gradient.reshape(-1, gradient.shape[-1])
    pieces = []
    for tap_index in range(9):
        row_off, col_off = (tap_index // 3, tap_index % 3)
        window = padded[:, :, row_off:row_off + row_count, col_off:col_off + col_count]
        pieces.append(jnp.dot(window.reshape(-1, window.shape[-1]).T, flat_grad, preferred_element_type=jnp.float32))
    return pieces

def time_kernel_grad(front_padded, gradient, frame_count):
    flat_grad = gradient.reshape(-1, gradient.shape[-1])
    pieces = []
    for lag_index in range(3):
        window = front_padded[:, 2 - lag_index:2 - lag_index + frame_count]
        pieces.append(jnp.dot(window.reshape(-1, window.shape[-1]).T, flat_grad, preferred_element_type=jnp.float32))
    return pieces

def pad_space(inputs):
    return jnp.pad(inputs, ((0, 0), (0, 0), (1, 1), (1, 1), (0, 0)))

def pad_front(inputs):
    return jnp.pad(inputs, ((0, 0), (2, 0), (0, 0), (0, 0), (0, 0)))

def reference(block_data, code_index, levels, w_space, w_time, enc_proj, dec_proj):
    frame_count, row_count, col_count = (block_data.shape[2], block_data.shape[3], block_data.shape[4])
    channel_count = block_data.shape[5]
    grad_scale = float(block_data.shape[1] * frame_count * row_count * col_count) ** (-0.5)
    latents = latent_values(code_index, levels)
    latent_count = latents.shape[-1]
    dec_in = high_dot(latents, dec_proj.astype(jnp.float32)).astype(jnp.bfloat16)
    dec_padded = pad_space(dec_in)
    dec_pre = space_apply(dec_padded, w_space[1], row_count, col_count)
    dec_hidden = jax.nn.silu(dec_pre).astype(jnp.bfloat16)
    out_grad = block_data[1]
    dec_inner = (time_transpose(out_grad, w_time[1]) * silu_slope(dec_pre)).astype(jnp.bfloat16)
    dec_input_grad = out_grad.astype(jnp.float32) + space_transpose(pad_space(dec_inner), w_space[1], row_count, col_count)
    latent_grad = high_dot(dec_input_grad, dec_proj.astype(jnp.float32).T)
    enc_in = block_data[0]
    enc_padded = pad_space(enc_in)
    enc_pre = space_apply(enc_padded, w_space[0], row_count, col_count)
    enc_hidden = jax.nn.silu(enc_pre).astype(jnp.bfloat16)
    enc_out = enc_in.astype(jnp.float32) + time_apply(enc_hidden, w_time[0])
    bounded = high_dot(enc_out, enc_proj.astype(jnp.float32).T)
    code_grad = latent_grad * (1.0 - jnp.tanh(bounded) ** 2)
    enc_out_grad = high_dot(code_grad, enc_proj.astype(jnp.float32)).astype(jnp.bfloat16)
    enc_inner = (time_transpose(enc_out_grad, w_time[0]) * silu_slope(enc_pre)).astype(jnp.bfloat16)
    enc_proj_grad = jnp.dot(code_grad.reshape(-1, latent_count).T, enc_out.reshape(-1, channel_count), precision=HIGH, preferred_element_type=jnp.float32)
    dec_proj_grad = jnp.dot(latents.reshape(-1, latent_count).T, dec_input_grad.reshape(-1, channel_count), precision=HIGH, preferred_element_type=jnp.float32)
    enc_space = jnp.stack(space_kernel_grad(enc_padded, enc_inner, row_count, col_count))
    dec_space = jnp.stack(space_kernel_grad(dec_padded, dec_inner, row_count, col_count))
    enc_time = jnp.stack(time_kernel_grad(pad_front(enc_hidden), enc_out_grad, frame_count))
    dec_time = jnp.stack(time_kernel_grad(pad_front(dec_hidden), out_grad, frame_count))
    space_grad = jnp.stack([enc_space, dec_space]) * grad_scale
    time_grad = jnp.stack([enc_time, dec_time]) * grad_scale
    proj_grad = jnp.stack([enc_proj_grad, dec_proj_grad]) * grad_scale
    return (space_grad, time_grad, proj_grad)
```

```python
import jax
import jax.numpy as jnp
from jax import lax
from jax.sharding import PartitionSpec as P

HIGH = lax.Precision.HIGHEST
F32 = jnp.float32
BF16 = jnp.bfloat16


def ring_order(count):
    return list(range(0, count, 2)) + list(range(count - 1, 0, -2))


def ring_gather(shard, axis):
    count = lax.axis_size(axis)
    order = ring_order(count)
    place = [order.index(i) for i in range(count)]
    forward = [(order[i], order[(i + 1) % count]) for i in range(count)]
    backward = [(target, source) for source, target in forward]
    here = jnp.array(place, jnp.int32)[lax.axis_index(axis)]
    order_table = jnp.array(order, jnp.int32)
    gathered = jnp.zeros((count,) + shard.shape, shard.dtype)

    def put(gathered, block, position):
        return lax.dynamic_update_index_in_dim(
            gathered, block, order_table[position % count], 0
        )

    gathered = put(gathered, shard, here)
    down = up = shard
    for step in range(1, count // 2 + 1):
        down = lax.ppermute(down, axis, forward)
        gathered = put(gathered, down, here - step + count)
        if step < count - step:
            up = lax.ppermute(up, axis, backward)
            gathered = put(gathered, up, here + step)
    return gathered


def swap_sum(values, axis):
    count = lax.axis_size(axis)
    bit = 1
    while bit < count:
        values = values + lax.ppermute(values, axis, [(i, i ^ bit) for i in range(count)])
        bit *= 2
    return values


def silu_slope(inputs):
    logistic = jax.nn.sigmoid(inputs)
    return logistic * (1.0 + inputs * (1.0 - logistic))


def dot32(left, right):
    return jnp.dot(left, right, precision=HIGH, preferred_element_type=F32)


def dot16(left, right):
    return jnp.dot(left, right, preferred_element_type=F32)


def move(values, dim, by):
    if by == 0:
        return values
    pads = [(0, 0, 0)] * values.ndim
    pads[dim] = (by, -by, 0)
    return lax.pad(values, jnp.zeros((), values.dtype), pads)


def local(block_data, code_index, levels, w_space, w_time, enc_proj, dec_proj):
    sp = lax.axis_size("sp")
    decoder = lax.axis_index("sec") == 1
    x = block_data[0, 0, :, 0]
    frames, cols, chans = x.shape
    lat = code_index.shape[1]
    own = w_space.shape[2]
    scale = float(lax.axis_size("dp") * frames * sp * cols) ** (-0.5)
    mine = lax.axis_index("sp")

    v = ring_gather(x.reshape(frames * cols, chans), "sp")
    pieces = w_space[0].reshape(9, own, sp, own).transpose(2, 1, 0, 3).reshape(sp, own, 9 * own)
    w_cat = lax.all_to_all(pieces, "sp", 0, 0, tiled=True).reshape(chans, 9 * own)
    codes = lax.all_gather(code_index[0, :, :, 0], "sp", axis=0)
    half = (levels.astype(F32) - 1.0) * 0.5
    latents = (codes.astype(F32) - half[:, None, None]) / half[:, None, None]
    latents = latents.transpose(0, 2, 3, 1).reshape(-1, lat)
    v = v.reshape(-1, chans)
    count = v.shape[0]
    grid = (sp, frames, cols)
    proj = jnp.where(decoder, dec_proj, enc_proj).astype(F32)
    wt = w_time[0]

    def conv_sum(taps):
        taps = taps.reshape(grid + (3, 3, own))
        total = 0.0
        for j in range(3):
            rows = sum(move(taps[:, :, :, i, j], 0, 1 - i) for i in range(3))
            total = total + move(rows, 2, 1 - j)
        return total.reshape(count, own)

    def spread(inner):
        inner = inner.reshape(grid + (own,))
        shifted = [move(move(inner, 0, i - 1), 2, j - 1) for i in range(3) for j in range(3)]
        return jnp.stack(shifted, axis=3).reshape(count, 9 * own)

    def later(values, k):
        return move(values.reshape(grid + (-1,)), 1, -k).reshape(count, -1)

    def earlier(values, k):
        return move(values.reshape(grid + (-1,)), 1, k).reshape(count, -1)

    def decoder_first():
        p_cat = dot32(proj, w_cat.astype(F32))
        pre = conv_sum(dot32(latents, p_cat))
        back = sum(later(dot16(v, wt[k].T), k) for k in range(3))
        inner = (back * silu_slope(pre)).astype(BF16)
        part = dot32(spread(inner).astype(F32), p_cat.T)
        return pre, inner, part.T

    def encoder_first():
        pre = conv_sum(dot16(v, w_cat))
        hidden = jax.nn.silu(pre).astype(BF16).astype(F32)
        back = dot32(wt.reshape(3 * own, chans).astype(F32), proj.T).reshape(3, own, lat)
        part = sum(dot32(earlier(hidden, k), back[k]) for k in range(3))
        return pre, jnp.zeros((count, own), BF16), part.T

    pre, inner_dec, part = lax.cond(decoder, decoder_first, encoder_first)
    total = swap_sum(part, "sp").T + dot32(v.astype(F32), proj.T)
    received = lax.ppermute(total, "sec", [(1, 0)])
    hidden = jax.nn.silu(pre).astype(BF16)
    hid_cat = jnp.stack([earlier(hidden, k) for k in range(3)], axis=1).reshape(count, 3 * own)
    own_rows = lax.dynamic_slice_in_dim(v, mine * frames * cols, frames * cols, 0).astype(F32)

    def rows_of(values):
        return lax.dynamic_slice_in_dim(values, mine * frames * cols, frames * cols, 0)

    def decoder_second():
        inner_cat = spread(inner_dec)
        short = dot32(latents.T, inner_cat.astype(F32))
        big = dot32(proj.T, short)
        time = dot16(hid_cat.T, v)
        part = dot32(short, w_cat.astype(F32).T) + dot32(rows_of(latents).T, own_rows)
        return big, time, part

    def encoder_second():
        code_grad = received * (1.0 - jnp.tanh(total) ** 2)
        flat = wt.reshape(3 * own, chans).astype(F32)
        back = dot32(proj, flat.T)
        spread_back = dot32(code_grad, back).reshape(count, 3, own)
        inner = sum(later(spread_back[:, k], k) for k in range(3)) * silu_slope(pre)
        big = dot16(v.T, spread(inner.astype(BF16)))
        short = dot32(code_grad.T, hid_cat.astype(F32))
        time = dot32(short.T, proj)
        part = dot32(short, flat) + dot32(rows_of(code_grad).T, own_rows)
        return big, time, part

    big, time, part = lax.cond(decoder, decoder_second, encoder_second)
    big = (big * scale).astype(BF16).reshape(sp, own, 9 * own)
    big = lax.all_to_all(big, "sp", 0, 0, tiled=True)
    swap = [(0, 1), (1, 0)]
    time = time * scale
    both = jnp.concatenate([big.reshape(-1, 9 * own)], 0)
    other = lax.ppermute(both, "dp", swap)
    summed = both.astype(F32) + other.astype(F32)
    space = summed.reshape(sp, own, 9, own).transpose(2, 1, 0, 3).reshape(9, own, chans)
    time = time + lax.ppermute(time, "dp", swap)
    proj_total = swap_sum(part * scale, "sp")
    proj_total = proj_total + lax.ppermute(proj_total, "dp", swap)
    return space[None], time.reshape(1, 3, own, chans), proj_total[None]


def solution(mesh):
    placed = (
        P("sec", "dp", None, "sp", None, None),
        P("dp", None, None, "sp", None),
        P(),
        P("sec", None, "sp", None),
        P("sec", None, "sp", None),
        P(),
        P(),
    )
    return jax.shard_map(
        local,
        mesh=mesh,
        in_specs=placed,
        out_specs=(P("sec", None, "sp", None), P("sec", None, "sp", None), P("sec", None, None)),
        check_vma=False,
    )
```

```python
import functools

import jax
import jax.numpy as jnp
from jax import lax
from jax.experimental import pallas as pl
from jax.experimental.pallas import tpu as pltpu
from jax.sharding import PartitionSpec as P

F32 = jnp.float32
BF16 = jnp.bfloat16
LANES = 128
NN = (((1,), (0,)), ((), ()))
NT = (((1,), (1,)), ((), ()))
TN = (((0,), (0,)), ((), ()))
VMEM_BYTES = 56 * 1024 * 1024


def up_to(value, multiple):
    return -(-value // multiple) * multiple


def ring_place(index, count):
    return jnp.where(index % 2 == 0, index // 2, count - (index + 1) // 2)


def ring_device(place, count):
    place = lax.rem(place + 2 * count, count)
    return jnp.where(place < count // 2, 2 * place, 2 * (count - place) - 1)


def ring_gather(shard, axis):
    count = lax.axis_size(axis)
    order = list(range(0, count, 2)) + list(range(count - 1, 0, -2))
    forward = [(order[i], order[(i + 1) % count]) for i in range(count)]
    backward = [(target, source) for source, target in forward]
    blocks, steps = [shard], [0]
    down = up = shard
    for step in range(1, count // 2 + 1):
        down = lax.ppermute(down, axis, forward)
        blocks.append(down)
        steps.append(-step)
        if step < count - step:
            up = lax.ppermute(up, axis, backward)
            blocks.append(up)
            steps.append(step)
    return blocks, steps


def swap_sum(values, axis):
    count = lax.axis_size(axis)
    bit = 1
    while bit < count:
        values = values + lax.ppermute(values, axis, [(i, i ^ bit) for i in range(count)])
        bit *= 2
    return values


def dot(left, right, dims):
    return lax.dot_general(left, right, dims, preferred_element_type=F32)


def thirds(values):
    high = values.astype(BF16).astype(F32)
    rest = values - high
    middle = rest.astype(BF16).astype(F32)
    return high, middle, rest - middle


def stack3(values):
    return jnp.concatenate(thirds(values), axis=0).astype(BF16)


def sum3(stacked):
    rows = stacked.shape[0] // 3
    return stacked[:rows] + stacked[rows : 2 * rows] + stacked[2 * rows :]


def lanes_down(values, by):
    by = by % LANES
    return values if by == 0 else pltpu.roll(values, LANES - by, 1)


def spots(parts, own):
    return [((p * own) // LANES, (p * own) % LANES) for p in range(parts)]


def col_move(values, by, cols):
    if by == 0:
        return values
    rows = values.shape[0]
    col = lax.broadcasted_iota(jnp.int32, values.shape, 0) % cols
    edge = 0 if by > 0 else cols - 1
    return jnp.where(col == edge, 0.0, pltpu.roll(values, by % rows, 0))


def frames_move(values, by, cols):
    if by == 0:
        return values
    zeros = jnp.zeros((abs(by) * cols, values.shape[1]), values.dtype)
    if by > 0:
        return jnp.concatenate([zeros, values[: -by * cols]], axis=0)
    return jnp.concatenate([values[-by * cols :], zeros], axis=0)


def merge(pieces, own):
    blocks = [None] * (spots(len(pieces), own)[-1][0] + 1)
    for piece, (block, offset) in zip(pieces, spots(len(pieces), own)):
        moved = lanes_down(piece, -offset)
        blocks[block] = moved if blocks[block] is None else blocks[block] + moved
    return blocks


class Sizes:
    def __init__(self, sp, frames, cols, chans, own, lat):
        self.sp, self.frames, self.cols = sp, frames, cols
        self.chans, self.own, self.lat = chans, own, lat
        self.row = frames * cols
        self.count = sp * self.row
        self.wide = up_to(9 * own, LANES)
        self.thin = up_to(3 * own, LANES)


def load_rows(z, steps, chunks, v, codes, sems):
    place = ring_place(lax.axis_index("sp"), z.sp)
    started = []
    for k, (chunk, step) in enumerate(zip(chunks, steps)):
        row = ring_device(place + step, z.sp)
        copy = pltpu.make_async_copy(
            chunk.at[pl.ds(0, z.row)],
            v.at[pl.ds(pl.multiple_of(row * z.row, z.row), z.row)],
            sems.at[0, k],
        )
        copy.start()
        started.append(copy)
        copy = pltpu.make_async_copy(chunk.at[pl.ds(z.row, 16)], codes.at[row], sems.at[1, k])
        copy.start()
        started.append(copy)
    return started


def rows_at(r, z):
    return pl.ds(pl.multiple_of(r * z.row, z.row), z.row)


def conv_row(z, taps, r):
    total = None
    for j in range(3):
        by_offset = {}
        for i in range(3):
            block, offset = spots(9, z.own)[3 * i + j]
            value = taps[r + i, :, block * LANES : (block + 1) * LANES]
            by_offset[offset] = by_offset.get(offset, 0.0) + value
        column = sum(lanes_down(value, offset) for offset, value in by_offset.items())
        column = col_move(column, 1 - j, z.cols)
        total = column if total is None else total + column
    return total


def later_row(z, taps, r):
    total = None
    for k, (block, offset) in enumerate(spots(3, z.own)):
        value = taps[rows_at(r, z), block * LANES : (block + 1) * LANES]
        value = frames_move(lanes_down(value, offset), -k, z.cols)
        total = value if total is None else total + value
    return total


def keep_own(z, values):
    lane = lax.broadcasted_iota(jnp.int32, values.shape, 1)
    return jnp.where(lane < z.own, values, 0.0)


def put_shifts(z, inner, shifts, r):
    for j in range(3):
        shifts[j, r + 1] = col_move(inner, j - 1, z.cols).astype(BF16)


def spread(z, shifts, inner_cat):
    def body(r, carry):
        pieces = [
            shifts[j, r + 2 - i].astype(F32) for i in range(3) for j in range(3)
        ]
        for b, block in enumerate(merge(pieces, z.own)):
            inner_cat[rows_at(r, z), b * LANES : (b + 1) * LANES] = block.astype(BF16)
        return carry

    lax.fori_loop(0, z.sp, body, 0)


def zero_ends(z, padded):
    padded[0] = jnp.zeros(padded.shape[1:], padded.dtype)
    padded[z.sp + 1] = jnp.zeros(padded.shape[1:], padded.dtype)


def in_blocks(z, action):
    step = 8 if z.sp % 8 == 0 else 1
    if z.sp == step:
        action(0, step)
    else:

        def body(b, carry):
            action(b * step, step)
            return carry

        lax.fori_loop(0, z.sp // step, body, 0)


def position_codes(z, codes, out):
    def body(r, carry):
        block = codes[r].astype(F32)[:, : up_to(z.row, LANES)]
        block = jnp.concatenate([block] * 3 + [jnp.zeros((LANES - 48, block.shape[1]), F32)], 0)
        out[rows_at(r, z)] = block.T[: z.row].astype(BF16)
        return carry

    lax.fori_loop(0, z.sp, body, 0)


def first_kernel(z, steps, *refs):
    n = len(steps)
    chunks, (w_cat, wt, proj, halves) = refs[:n], refs[n : n + 4]
    part, hid_cat, slope, inner_out = refs[n + 4 : n + 8]
    v, codes, taps, shifts, inner_cat, pos, thin, sems = refs[n + 8 :]
    started = load_rows(z, steps, chunks, v, codes, sems)
    decoder = lax.axis_index("sec") == 1
    first = lax.axis_index("sp") == 0
    zero_ends(z, taps)
    for copy in started:
        copy.wait()
    whole = dot(proj[...], v[...], NT)[:8]

    def store_hidden(pre, logistic, r):
        hidden = keep_own(z, (pre * logistic).astype(BF16).astype(F32))
        moved = [frames_move(hidden, k, z.cols) for k in range(3)]
        for b, block in enumerate(merge(moved, z.own)):
            hid_cat[rows_at(r, z), b * LANES : (b + 1) * LANES] = block.astype(BF16)

    def finish(weights, cat):
        stacked = jnp.concatenate([weights[:8]] * 1, axis=0)
        partial = sum3(dot(stack3(stacked), cat, NT))
        part[...] = partial + jnp.where(first, whole, 0.0)

    @pl.when(decoder)
    def _():
        for j in range(3):
            zero_ends(z, shifts.at[j])
        p_cat = dot(proj[...], w_cat[...], NN)
        half = halves[:, :1]
        row = lax.broadcasted_iota(jnp.int32, p_cat.shape, 0)
        scaled = jnp.where(
            row == z.lat, -jnp.sum(p_cat, axis=0, keepdims=True), p_cat / half
        )
        table = jnp.concatenate(
            list(thirds(scaled)) + [jnp.zeros((LANES - 48, z.wide), F32)], axis=0
        ).astype(BF16)
        position_codes(z, codes, pos)

        def block(r0, rows):
            place = pl.ds(pl.multiple_of(r0 * z.row, rows * z.row), rows * z.row)
            taps[pl.ds(r0 + 1, rows)] = dot(pos[place], table, NN).reshape(rows, z.row, z.wide)
            thin[place] = dot(v[place], wt[...], NT)

        in_blocks(z, block)

        def body(r, carry):
            pre = conv_row(z, taps, r)
            logistic = 1.0 / (1.0 + jnp.exp(-pre))
            store_hidden(pre, logistic, r)
            rate = logistic * (1.0 + pre * (1.0 - logistic))
            inner = keep_own(z, (later_row(z, thin, r) * rate).astype(BF16).astype(F32))
            put_shifts(z, inner, shifts, r)
            inner_out[r] = inner.astype(BF16)
            return carry

        lax.fori_loop(0, z.sp, body, 0)
        spread(z, shifts, inner_cat)
        finish(p_cat, inner_cat[...])

    @pl.when(jnp.logical_not(decoder))
    def _():
        def block(r0, rows):
            place = pl.ds(pl.multiple_of(r0 * z.row, rows * z.row), rows * z.row)
            taps[pl.ds(r0 + 1, rows)] = dot(v[place], w_cat[...], NN).reshape(
                rows, z.row, z.wide
            )

        in_blocks(z, block)

        def body(r, carry):
            pre = conv_row(z, taps, r)
            logistic = 1.0 / (1.0 + jnp.exp(-pre))
            store_hidden(pre, logistic, r)
            slope[r] = logistic * (1.0 + pre * (1.0 - logistic))
            return carry

        lax.fori_loop(0, z.sp, body, 0)
        finish(dot(proj[...], wt[...], NT), hid_cat[...])


def second_kernel(z, steps, scale, *refs):
    n = len(steps)
    chunks = refs[:n]
    w_cat, wt, proj, halves, hid_cat, slope, inner_in, total, received = refs[n : n + 9]
    big, time, part = refs[n + 9 : n + 12]
    v, codes, shifts, inner_cat, pos, thin, sems = refs[n + 12 :]
    started = load_rows(z, steps, chunks, v, codes, sems)
    decoder = lax.axis_index("sec") == 1
    first = lax.axis_index("sp") == 0
    for j in range(3):
        zero_ends(z, shifts.at[j])
    for copy in started:
        copy.wait()

    @pl.when(decoder)
    def _():
        position_codes(z, codes, pos)

        def body(r, carry):
            put_shifts(z, inner_in[r].astype(F32), shifts, r)
            return carry

        lax.fori_loop(0, z.sp, body, 0)
        spread(z, shifts, inner_cat)
        half = halves[:8, :1]

        def latent_rows(raw):
            row = lax.broadcasted_iota(jnp.int32, raw.shape, 0)
            return jnp.where(row < z.lat, raw / half - raw[z.lat : z.lat + 1], 0.0)

        short = latent_rows(dot(pos[...], inner_cat[...], TN)[:8])
        proj8 = proj[:8].astype(F32)
        proj24 = jnp.concatenate([proj8] * 3, axis=0).astype(BF16)
        big[...] = (dot(proj24, stack3(short), TN) * scale).astype(BF16)
        time[...] = dot(hid_cat[...], v[...], TN)[: 3 * z.own] * scale
        whole = latent_rows(dot(pos[...], v[...], TN)[:8])
        partial = sum3(dot(stack3(short), w_cat[...], NT))
        part[...] = (partial + jnp.where(first, whole, 0.0)) * scale

    @pl.when(jnp.logical_not(decoder))
    def _():
        bounded = jnp.tanh(total[...])
        grad = received[...] * (1.0 - bounded * bounded)
        back = dot(proj[...], wt[...], NT)[:8]
        gh, gm, gl = thirds(grad)
        bh, bm, bl = thirds(back)
        left = jnp.concatenate([gh, gh, gm, gh, gl, gm], axis=0).astype(BF16)
        right = jnp.concatenate([bh, bm, bh, bl, bh, bm], axis=0).astype(BF16)
        thin[...] = dot(left, right, TN)

        def body(r, carry):
            inner = keep_own(z, later_row(z, thin, r) * slope[r])
            put_shifts(z, inner, shifts, r)
            return carry

        lax.fori_loop(0, z.sp, body, 0)
        spread(z, shifts, inner_cat)
        big[...] = (dot(v[...], inner_cat[...], TN) * scale).astype(BF16)
        grad3 = jnp.concatenate([gh, gm, gl], axis=0).astype(BF16)
        short = sum3(dot(grad3, hid_cat[...], NN))
        short3 = stack3(short)
        proj8 = proj[:8].astype(F32)
        proj24 = jnp.concatenate([proj8] * 3, axis=0).astype(BF16)
        time[...] = dot(short3, proj24, TN)[: 3 * z.own] * scale
        whole = sum3(dot(grad3, v[...], NN))
        partial = sum3(dot(short3, wt[...], NN))
        part[...] = (partial + jnp.where(first, whole, 0.0)) * scale


def last_kernel(z, mine, other, time_mine, time_other, space, time):
    time[...] = time_mine[...] + time_other[...]
    per = LANES // z.own
    for tap, (block, offset) in enumerate(spots(9, z.own)):
        for m in range(z.chans // LANES):
            total = None
            for p in range(per):
                at = (m * per + p, slice(None), slice(block * LANES, (block + 1) * LANES))
                value = mine[at].astype(F32) + other[at].astype(F32)
                value = lanes_down(value, offset - p * z.own)
                if total is None:
                    total = value
                else:
                    lane = lax.broadcasted_iota(jnp.int32, value.shape, 1)
                    total = jnp.where(lane < p * z.own, total, value)
            space[tap, :, m * LANES : (m + 1) * LANES] = total


VM = pl.BlockSpec(memory_space=pltpu.VMEM)
ANY = pl.BlockSpec(memory_space=pl.ANY)


def shaped(shape, dtype):
    return jax.ShapeDtypeStruct(shape, dtype)


def local(block_data, code_index, levels, w_space, w_time, enc_proj, dec_proj):
    frames, cols, chans = block_data.shape[2], block_data.shape[4], block_data.shape[5]
    lat, own = code_index.shape[1], w_space.shape[2]
    z = Sizes(lax.axis_size("sp"), frames, cols, chans, own, lat)
    scale = float(lax.axis_size("dp") * z.count) ** (-0.5)
    decoder = lax.axis_index("sec") == 1
    params = pltpu.CompilerParams(vmem_limit_bytes=VMEM_BYTES)

    code_rows = code_index.reshape(lat, z.row).astype(BF16)
    ones = jnp.ones((1, z.row), BF16)
    code_rows = jnp.concatenate([code_rows, ones], axis=0)
    code_rows = jnp.pad(code_rows, ((0, 16 - lat - 1), (0, chans - z.row)))
    shard = jnp.concatenate([block_data.reshape(z.row, chans), code_rows], axis=0)
    chunks, steps = ring_gather(shard, "sp")
    pieces = w_space[0].reshape(9, own, z.sp, own).transpose(2, 1, 0, 3)
    pieces = pieces.reshape(z.sp, own, 9 * own)
    pieces = jnp.pad(pieces, ((0, 0), (0, 0), (0, z.wide - 9 * own)))
    w_cat = lax.all_to_all(pieces, "sp", 0, 0, tiled=True).reshape(chans, z.wide)
    wt = jnp.pad(w_time.reshape(3 * own, chans), ((0, z.thin - 3 * own), (0, 0)))
    proj = jnp.pad(jnp.where(decoder, dec_proj, enc_proj), ((0, 16 - lat), (0, 0)))
    half = jnp.pad((levels.astype(F32) - 1.0) * 0.5, (0, 16 - lat), constant_values=1.0)
    halves = jnp.broadcast_to(half[:, None], (16, LANES))

    part, hid_cat, slope, inner = pl.pallas_call(
        functools.partial(first_kernel, z, steps),
        out_shape=(
            shaped((8, z.count), F32),
            shaped((z.count, z.thin), BF16),
            shaped((z.sp, z.row, LANES), F32),
            shaped((z.sp, z.row, LANES), BF16),
        ),
        in_specs=[ANY] * z.sp + [VM] * 4,
        out_specs=(VM,) * 4,
        scratch_shapes=[
            pltpu.VMEM((z.count, chans), BF16),
            pltpu.VMEM((z.sp, 16, chans), BF16),
            pltpu.VMEM((z.sp + 2, z.row, z.wide), F32),
            pltpu.VMEM((3, z.sp + 2, z.row, LANES), BF16),
            pltpu.VMEM((z.count, z.wide), BF16),
            pltpu.VMEM((z.count, LANES), BF16),
            pltpu.VMEM((z.count, z.thin), F32),
            pltpu.SemaphoreType.DMA((2, z.sp)),
        ],
        compiler_params=params,
        name="first",
    )(*chunks, w_cat, wt, proj, halves)
    total = swap_sum(part, "sp")
    received = lax.ppermute(total, "sec", [(1, 0)])
    big, time, part = pl.pallas_call(
        functools.partial(second_kernel, z, steps, scale),
        out_shape=(
            shaped((chans, z.wide), BF16),
            shaped((3 * own, chans), F32),
            shaped((8, chans), F32),
        ),
        in_specs=[ANY] * z.sp + [VM] * 9,
        out_specs=(VM,) * 3,
        scratch_shapes=[
            pltpu.VMEM((z.count, chans), BF16),
            pltpu.VMEM((z.sp, 16, chans), BF16),
            pltpu.VMEM((3, z.sp + 2, z.row, LANES), BF16),
            pltpu.VMEM((z.count, z.wide), BF16),
            pltpu.VMEM((z.count, LANES), BF16),
            pltpu.VMEM((z.count, z.thin), F32),
            pltpu.SemaphoreType.DMA((2, z.sp)),
        ],
        compiler_params=params,
        name="second",
    )(*chunks, w_cat, wt, proj, halves, hid_cat, slope, inner, total, received)
    swap = [(0, 1), (1, 0)]
    big = lax.all_to_all(big.reshape(z.sp, own, z.wide), "sp", 0, 0, tiled=True)
    space, time = pl.pallas_call(
        functools.partial(last_kernel, z),
        out_shape=(shaped((9, own, chans), F32), shaped((3 * own, chans), F32)),
        in_specs=[VM] * 4,
        out_specs=(VM,) * 2,
        compiler_params=params,
        name="last",
    )(big, lax.ppermute(big, "dp", swap), time, lax.ppermute(time, "dp", swap))
    part = swap_sum(part, "sp")
    part = part + lax.ppermute(part, "dp", swap)
    return space[None], time.reshape(1, 3, own, chans), part[None, :lat]


def solution(mesh):
    placed = (
        P("sec", "dp", None, "sp", None, None),
        P("dp", None, None, "sp", None),
        P(),
        P("sec", None, "sp", None),
        P("sec", None, "sp", None),
        P(),
        P(),
    )
    return jax.shard_map(
        local,
        mesh=mesh,
        in_specs=placed,
        out_specs=(P("sec", None, "sp", None), P("sec", None, "sp", None), P("sec", None, None)),
        check_vma=False,
    )
```

```python
import functools

import jax
import jax.numpy as jnp
from jax import lax
from jax.experimental import pallas as pl
from jax.experimental.pallas import tpu as pltpu
from jax.sharding import PartitionSpec as P

F32 = jnp.float32
BF16 = jnp.bfloat16
LANES = 128
NN = (((1,), (0,)), ((), ()))
NT = (((1,), (1,)), ((), ()))
TN = (((0,), (0,)), ((), ()))
VMEM_BYTES = 56 * 1024 * 1024


def up_to(value, multiple):
    return -(-value // multiple) * multiple


def ring_place(index, count):
    return jnp.where(index % 2 == 0, index // 2, count - (index + 1) // 2)


def ring_device(place, count):
    place = lax.rem(place + 2 * count, count)
    return jnp.where(place < count // 2, 2 * place, 2 * (count - place) - 1)


def ring_maps(count):
    order = list(range(0, count, 2)) + list(range(count - 1, 0, -2))
    forward = [(order[i], order[(i + 1) % count]) for i in range(count)]
    return forward, [(target, source) for source, target in forward]


def ring_exchange(shard, ahead, behind, own_piece):
    count = lax.axis_size("sp")
    up, down = ring_maps(count)
    swap = [(0, 1), (1, 0)]
    first = shard
    shards, shard_steps = [shard], [0]
    mine, other, piece_steps = [own_piece], [lax.ppermute(own_piece, "dp", swap)], [0]
    second = shard
    for step in range(1, count // 2 + 1):
        first = lax.ppermute(first, "sp", up)
        shards.append(first)
        shard_steps.append(-step)
        if step < count - step:
            second = lax.ppermute(second, "sp", down)
            shards.append(second)
            shard_steps.append(step)
        fresh = []
        behind = lax.ppermute(behind, "sp", down)
        fresh.append(behind[0])
        piece_steps.append(step)
        behind = behind[1:]
        if step < count - step:
            ahead = lax.ppermute(ahead, "sp", up)
            fresh.append(ahead[0])
            piece_steps.append(-step)
            ahead = ahead[1:]
        both = lax.ppermute(jnp.stack(fresh), "dp", swap)
        mine += fresh
        other += [both[i] for i in range(len(fresh))]
    return shards, shard_steps, mine, other, piece_steps


def swap_sum(values, axis):
    count = lax.axis_size(axis)
    bit = 1
    while bit < count:
        values = values + lax.ppermute(values, axis, [(i, i ^ bit) for i in range(count)])
        bit *= 2
    return values


def dot(left, right, dims):
    return lax.dot_general(left, right, dims, preferred_element_type=F32)


def thirds(values):
    high = values.astype(BF16).astype(F32)
    rest = values - high
    middle = rest.astype(BF16).astype(F32)
    return high, middle, rest - middle


def stack3(values):
    return jnp.concatenate(thirds(values), axis=0).astype(BF16)


def sum3(stacked):
    rows = stacked.shape[0] // 3
    return stacked[:rows] + stacked[rows : 2 * rows] + stacked[2 * rows :]


def lanes_down(values, by):
    by = by % LANES
    return values if by == 0 else pltpu.roll(values, LANES - by, 1)


def spots(parts, own):
    return [((p * own) // LANES, (p * own) % LANES) for p in range(parts)]


def col_move(values, by, cols):
    if by == 0:
        return values
    rows = values.shape[0]
    col = lax.broadcasted_iota(jnp.int32, values.shape, 0) % cols
    edge = 0 if by > 0 else cols - 1
    return jnp.where(col == edge, 0.0, pltpu.roll(values, by % rows, 0))


def frames_move(values, by, cols):
    if by == 0:
        return values
    zeros = jnp.zeros((abs(by) * cols, values.shape[1]), values.dtype)
    if by > 0:
        return jnp.concatenate([zeros, values[: -by * cols]], axis=0)
    return jnp.concatenate([values[-by * cols :], zeros], axis=0)


def merge(pieces, own):
    blocks = [None] * (spots(len(pieces), own)[-1][0] + 1)
    for piece, (block, offset) in zip(pieces, spots(len(pieces), own)):
        moved = lanes_down(piece, -offset)
        blocks[block] = moved if blocks[block] is None else blocks[block] + moved
    return blocks


class Sizes:
    def __init__(self, sp, frames, cols, chans, own, lat):
        self.sp, self.frames, self.cols = sp, frames, cols
        self.chans, self.own, self.lat = chans, own, lat
        self.row = frames * cols
        self.count = sp * self.row
        self.wide = up_to(9 * own, LANES)
        self.thin = up_to(3 * own, LANES)
        self.half = own // 2
        code_rows = frames * lat
        self.code_rows = up_to(code_rows, 16)
        self.half_pad = up_to(self.half, 16)
        if self.wide - 9 * own >= cols and self.half >= code_rows:
            self.code_row, self.code_lane = 0, 9 * own
            self.piece_rows = self.half
        else:
            self.code_row, self.code_lane = up_to(self.half, 16), 0
            self.piece_rows = self.code_row + up_to(code_rows, 16)
        self.carries = self.wide - 9 * own >= LANES // 2 and own * (LANES // 2) >= 8 * chans


def load_shards(z, steps, shards, v, sems):
    place = ring_place(lax.axis_index("sp"), z.sp)
    started = []
    for k, (shard, step) in enumerate(zip(shards, steps)):
        row = ring_device(place + step, z.sp)
        copy = pltpu.make_async_copy(shard, v.at[rows_at(row, z)], sems.at[k])
        copy.start()
        started.append(copy)
    return started


def load_pieces(z, steps, mine, other, halves, codes, sems):
    place = ring_place(lax.axis_index("sp"), z.sp)
    core = lax.axis_index("dp")
    started = []
    for k, (one, two, step) in enumerate(zip(mine, other, steps)):
        row = ring_device(place + step, z.sp)
        for at, (source, target) in enumerate(
            (
                (one.at[pl.ds(0, z.half_pad)], halves.at[row, core]),
                (two.at[pl.ds(0, z.half_pad)], halves.at[row, 1 - core]),
                (one.at[pl.ds(z.code_row, z.code_rows)], codes.at[row]),
            )
        ):
            copy = pltpu.make_async_copy(source, target, sems.at[at, k])
            copy.start()
            started.append(copy)
    return started


def rows_at(r, z):
    return pl.ds(pl.multiple_of(r * z.row, z.row), z.row)


def conv_row(z, taps, r):
    total = None
    for j in range(3):
        by_offset = {}
        for i in range(3):
            block, offset = spots(9, z.own)[3 * i + j]
            value = taps[r + i, :, block * LANES : (block + 1) * LANES]
            by_offset[offset] = by_offset.get(offset, 0.0) + value
        column = sum(lanes_down(value, offset) for offset, value in by_offset.items())
        column = col_move(column, 1 - j, z.cols)
        total = column if total is None else total + column
    return total


def later_row(z, taps, r):
    total = None
    for k, (block, offset) in enumerate(spots(3, z.own)):
        value = taps[rows_at(r, z), block * LANES : (block + 1) * LANES]
        value = frames_move(lanes_down(value, offset), -k, z.cols)
        total = value if total is None else total + value
    return total


def keep_own(z, values):
    lane = lax.broadcasted_iota(jnp.int32, values.shape, 1)
    return jnp.where(lane < z.own, values, 0.0)


def put_shifts(z, inner, shifts, r):
    for j in range(3):
        shifts[j, r + 1] = col_move(inner, j - 1, z.cols).astype(BF16)


def spread(z, shifts, inner_cat):
    def body(r, carry):
        pieces = [
            shifts[j, r + 2 - i].astype(F32) for i in range(3) for j in range(3)
        ]
        for b, block in enumerate(merge(pieces, z.own)):
            inner_cat[rows_at(r, z), b * LANES : (b + 1) * LANES] = block.astype(BF16)
        return carry

    lax.fori_loop(0, z.sp, body, 0)


def zero_ends(z, padded):
    padded[0] = jnp.zeros(padded.shape[1:], padded.dtype)
    padded[z.sp + 1] = jnp.zeros(padded.shape[1:], padded.dtype)


def in_blocks(z, action):
    step = 8 if z.sp % 8 == 0 else 1
    if z.sp == step:
        action(0, step)
    else:

        def body(b, carry):
            action(b * step, step)
            return carry

        lax.fori_loop(0, z.sp // step, body, 0)


def position_codes(z, codes, out):
    block, offset = z.code_lane // LANES, z.code_lane % LANES

    def body(r, carry):
        raw = codes[r, :, block * LANES : (block + 1) * LANES].astype(F32)
        raw = jnp.concatenate([raw, jnp.zeros((LANES - z.code_rows, LANES), F32)], axis=0)
        turned = raw.T[offset : offset + z.cols]
        lane = lax.broadcasted_iota(jnp.int32, turned.shape, 1)
        frames = []
        for t in range(z.frames):
            values = lanes_down(turned, t * z.lat)
            values = jnp.where(lane < z.lat, values, jnp.where(lane == z.lat, 1.0, 0.0))
            frames.append(
                values + pltpu.roll(values, 16, 1) + pltpu.roll(values, 32, 1)
            )
        out[rows_at(r, z)] = jnp.concatenate(frames, axis=0).astype(BF16)
        return carry

    lax.fori_loop(0, z.sp, body, 0)


def piece_kernel(z, w, codes, ahead, behind, own_piece):
    place = ring_place(lax.axis_index("sp"), z.sp)
    core = lax.axis_index("dp")
    lane = lax.broadcasted_iota(jnp.int32, (z.half, LANES), 1)
    code_block = codes[...]
    for j in range(z.sp):
        block, offset = (j * z.own) // LANES, (j * z.own) % LANES
        taps = []
        for tap in range(9):
            at = slice(block * LANES, (block + 1) * LANES)
            if z.half == z.half_pad:
                value = w[tap, pl.ds(pl.multiple_of(core * z.half, z.half), z.half), at]
                value = value.astype(F32)
            else:
                value = w[tap, :, at].astype(F32)
                value = jnp.where(core == 0, value[: z.half], value[z.half :])
            value = lanes_down(value, offset)
            taps.append(jnp.where(lane < z.own, value, 0.0))
        blocks = merge(taps, z.own)
        if z.code_row == 0:
            blocks[-1] = blocks[-1] + code_block
        distance = lax.rem(ring_place(jnp.int32(j), z.sp) - place + z.sp, z.sp)

        def store(target, index):
            for b, value in enumerate(blocks):
                at = slice(b * LANES, (b + 1) * LANES)
                if index is None:
                    target[: z.half, at] = value.astype(BF16)
                else:
                    target[index, : z.half, at] = value.astype(BF16)
            if z.code_row:
                tail = slice(z.code_row, z.piece_rows)
                if index is None:
                    target[tail, :LANES] = code_block.astype(BF16)
                else:
                    target[index, tail, :LANES] = code_block.astype(BF16)

        @pl.when(distance == 0)
        def _():
            store(own_piece, None)

        @pl.when(jnp.logical_and(distance > 0, distance < z.sp // 2))
        def _():
            store(ahead, distance - 1)

        @pl.when(distance >= z.sp // 2)
        def _():
            store(behind, z.sp - distance - 1)


def first_kernel(z, steps, piece_steps, *refs):
    n = z.sp
    shards, mine, other = refs[:n], refs[n : 2 * n], refs[2 * n : 3 * n]
    wt, proj, halves = refs[3 * n : 3 * n + 3]
    part, hid_cat, slope, inner_out, w_cat, pos = refs[3 * n + 3 : 3 * n + 9]
    v, w_halves, codes, taps, shifts, inner_cat, thin, sems, piece_sems = refs[3 * n + 9 :]
    started = load_pieces(z, piece_steps, mine, other, w_halves, codes, piece_sems)
    started += load_shards(z, steps, shards, v, sems)
    decoder = lax.axis_index("sec") == 1
    first = lax.axis_index("sp") == 0
    zero_ends(z, taps)
    for copy in started:
        copy.wait()
    if z.half == z.half_pad:
        w_cat[...] = w_halves[...].reshape(z.chans, z.wide)
    else:
        for j in range(z.sp):
            for core in range(2):
                rows = slice(j * z.own + core * z.half, j * z.own + (core + 1) * z.half)
                w_cat[rows] = w_halves[j, core, : z.half]
    whole = dot(proj[...], v[...], NT)[:8]

    def store_hidden(pre, logistic, r):
        hidden = keep_own(z, (pre * logistic).astype(BF16).astype(F32))
        moved = [frames_move(hidden, k, z.cols) for k in range(3)]
        for b, block in enumerate(merge(moved, z.own)):
            hid_cat[rows_at(r, z), b * LANES : (b + 1) * LANES] = block.astype(BF16)

    def finish(weights, cat):
        partial = sum3(dot(stack3(weights[:8]), cat, NT))
        part[...] = partial + jnp.where(first, whole, 0.0)

    @pl.when(decoder)
    def _():
        for j in range(3):
            zero_ends(z, shifts.at[j])
        p_cat = dot(proj[...], w_cat[...], NN)
        half = halves[:, :1]
        row = lax.broadcasted_iota(jnp.int32, p_cat.shape, 0)
        scaled = jnp.where(
            row == z.lat, -jnp.sum(p_cat, axis=0, keepdims=True), p_cat / half
        )
        table = jnp.concatenate(
            list(thirds(scaled)) + [jnp.zeros((LANES - 48, z.wide), F32)], axis=0
        ).astype(BF16)
        position_codes(z, codes, pos)

        def block(r0, rows):
            place = pl.ds(pl.multiple_of(r0 * z.row, rows * z.row), rows * z.row)
            taps[pl.ds(r0 + 1, rows)] = dot(pos[place], table, NN).reshape(rows, z.row, z.wide)
            thin[place] = dot(v[place], wt[...], NT)

        in_blocks(z, block)

        def body(r, carry):
            pre = conv_row(z, taps, r)
            logistic = 1.0 / (1.0 + jnp.exp(-pre))
            store_hidden(pre, logistic, r)
            rate = logistic * (1.0 + pre * (1.0 - logistic))
            inner = keep_own(z, (later_row(z, thin, r) * rate).astype(BF16).astype(F32))
            put_shifts(z, inner, shifts, r)
            inner_out[r] = inner.astype(BF16)
            return carry

        lax.fori_loop(0, z.sp, body, 0)
        spread(z, shifts, inner_cat)
        finish(p_cat, inner_cat[...])

    @pl.when(jnp.logical_not(decoder))
    def _():
        def block(r0, rows):
            place = pl.ds(pl.multiple_of(r0 * z.row, rows * z.row), rows * z.row)
            taps[pl.ds(r0 + 1, rows)] = dot(v[place], w_cat[...], NN).reshape(
                rows, z.row, z.wide
            )

        in_blocks(z, block)

        def body(r, carry):
            pre = conv_row(z, taps, r)
            logistic = 1.0 / (1.0 + jnp.exp(-pre))
            store_hidden(pre, logistic, r)
            slope[r] = logistic * (1.0 + pre * (1.0 - logistic))
            return carry

        lax.fori_loop(0, z.sp, body, 0)
        finish(dot(proj[...], wt[...], NT), hid_cat[...])


def second_kernel(z, steps, scale, *refs):
    n = len(steps)
    shards = refs[:n]
    w_cat, pos, wt, proj, halves, hid_cat, slope, inner_in, total, received = refs[n : n + 10]
    big, time, part = refs[n + 10 : n + 13]
    v, shifts, inner_cat, thin, sems = refs[n + 13 :]
    started = load_shards(z, steps, shards, v, sems)
    decoder = lax.axis_index("sec") == 1
    first = lax.axis_index("sp") == 0
    for j in range(3):
        zero_ends(z, shifts.at[j])
    for copy in started:
        copy.wait()

    def put_out(kernel_grad, proj_part):
        part[...] = proj_part
        if not z.carries:
            big[...] = kernel_grad.astype(BF16)
            return
        side = z.wide - LANES
        big[:, :side] = kernel_grad[:, :side].astype(BF16)
        pieces = []
        for b in range(2 * z.chans // LANES):
            block = proj_part[:, (b // 2) * LANES : (b // 2 + 1) * LANES]
            pieces.append(block if b % 2 else pltpu.roll(block, LANES // 2, 1))
        carried = jnp.concatenate(pieces, axis=0)
        lane = lax.broadcasted_iota(jnp.int32, carried.shape, 1)
        for j in range(z.sp):
            rows = slice(j * z.own, (j + 1) * z.own)
            big[rows, side:] = jnp.where(
                lane < LANES // 2, kernel_grad[rows, side:], carried
            ).astype(BF16)

    @pl.when(decoder)
    def _():
        def body(r, carry):
            put_shifts(z, inner_in[r].astype(F32), shifts, r)
            return carry

        lax.fori_loop(0, z.sp, body, 0)
        spread(z, shifts, inner_cat)
        half = halves[:8, :1]

        def latent_rows(raw):
            row = lax.broadcasted_iota(jnp.int32, raw.shape, 0)
            return jnp.where(row < z.lat, raw / half - raw[z.lat : z.lat + 1], 0.0)

        short = latent_rows(dot(pos[...], inner_cat[...], TN)[:8])
        proj8 = proj[:8].astype(F32)
        proj24 = jnp.concatenate([proj8] * 3, axis=0).astype(BF16)
        kernel_grad = dot(proj24, stack3(short), TN) * scale
        time[...] = dot(hid_cat[...], v[...], TN)[: 3 * z.own] * scale
        whole = latent_rows(dot(pos[...], v[...], TN)[:8])
        partial = sum3(dot(stack3(short), w_cat[...], NT))
        put_out(kernel_grad, (partial + jnp.where(first, whole, 0.0)) * scale)

    @pl.when(jnp.logical_not(decoder))
    def _():
        bounded = jnp.tanh(total[...])
        grad = received[...] * (1.0 - bounded * bounded)
        back = dot(proj[...], wt[...], NT)[:8]
        gh, gm, gl = thirds(grad)
        bh, bm, bl = thirds(back)
        left = jnp.concatenate([gh, gh, gm, gh, gl, gm], axis=0).astype(BF16)
        right = jnp.concatenate([bh, bm, bh, bl, bh, bm], axis=0).astype(BF16)
        thin[...] = dot(left, right, TN)

        def body(r, carry):
            inner = keep_own(z, later_row(z, thin, r) * slope[r])
            put_shifts(z, inner, shifts, r)
            return carry

        lax.fori_loop(0, z.sp, body, 0)
        spread(z, shifts, inner_cat)
        kernel_grad = dot(v[...], inner_cat[...], TN) * scale
        grad3 = jnp.concatenate([gh, gm, gl], axis=0).astype(BF16)
        short = sum3(dot(grad3, hid_cat[...], NN))
        short3 = stack3(short)
        proj8 = proj[:8].astype(F32)
        proj24 = jnp.concatenate([proj8] * 3, axis=0).astype(BF16)
        time[...] = dot(short3, proj24, TN)[: 3 * z.own] * scale
        whole = sum3(dot(grad3, v[...], NN))
        partial = sum3(dot(short3, wt[...], NN))
        put_out(kernel_grad, (partial + jnp.where(first, whole, 0.0)) * scale)


def last_kernel(z, mine, other, time_mine, time_other, space, time, part):
    time[...] = time_mine[...] + time_other[...]
    if z.carries:
        side = slice(z.wide - LANES, z.wide)
        carried = 0.0
        for j in range(z.sp):
            carried = carried + (mine[j, :, side].astype(F32) + other[j, :, side].astype(F32))
        lane = lax.broadcasted_iota(jnp.int32, (8, LANES), 1)
        for m in range(z.chans // LANES):
            low = pltpu.roll(carried[16 * m : 16 * m + 8], LANES // 2, 1)
            high = carried[16 * m + 8 : 16 * m + 16]
            part[:, m * LANES : (m + 1) * LANES] = jnp.where(lane < LANES // 2, low, high)
    else:
        part[...] = jnp.zeros(part.shape, F32)
    per = LANES // z.own
    for tap, (block, offset) in enumerate(spots(9, z.own)):
        for m in range(z.chans // LANES):
            total = None
            for p in range(per):
                at = (m * per + p, slice(None), slice(block * LANES, (block + 1) * LANES))
                value = mine[at].astype(F32) + other[at].astype(F32)
                value = lanes_down(value, offset - p * z.own)
                if total is None:
                    total = value
                else:
                    lane = lax.broadcasted_iota(jnp.int32, value.shape, 1)
                    total = jnp.where(lane < p * z.own, total, value)
            space[tap, :, m * LANES : (m + 1) * LANES] = total


VM = pl.BlockSpec(memory_space=pltpu.VMEM)
ANY = pl.BlockSpec(memory_space=pl.ANY)


def shaped(shape, dtype):
    return jax.ShapeDtypeStruct(shape, dtype)


def local(block_data, code_index, levels, w_space, w_time, enc_proj, dec_proj):
    frames, cols, chans = block_data.shape[2], block_data.shape[4], block_data.shape[5]
    lat, own = code_index.shape[1], w_space.shape[2]
    z = Sizes(lax.axis_size("sp"), frames, cols, chans, own, lat)
    scale = float(lax.axis_size("dp") * z.count) ** (-0.5)
    decoder = lax.axis_index("sec") == 1
    params = pltpu.CompilerParams(vmem_limit_bytes=VMEM_BYTES)

    codes = jnp.transpose(code_index[0, :, :, 0], (1, 0, 2)).reshape(frames * lat, cols)
    left = z.code_lane % LANES
    codes = jnp.pad(
        codes.astype(F32),
        ((0, (z.half if z.code_row == 0 else z.code_rows) - frames * lat), (left, LANES - left - cols)),
    )
    ahead, behind, own_piece = pl.pallas_call(
        functools.partial(piece_kernel, z),
        out_shape=(
            shaped((z.sp // 2 - 1, z.piece_rows, z.wide), BF16),
            shaped((z.sp // 2, z.piece_rows, z.wide), BF16),
            shaped((z.piece_rows, z.wide), BF16),
        ),
        in_specs=[VM] * 2,
        out_specs=(VM,) * 3,
        compiler_params=params,
        name="pieces",
    )(w_space[0], codes)
    shards, steps, mine, other, piece_steps = ring_exchange(
        block_data.reshape(z.row, chans), ahead, behind, own_piece
    )
    wt = jnp.pad(w_time.reshape(3 * own, chans), ((0, z.thin - 3 * own), (0, 0)))
    proj = jnp.pad(jnp.where(decoder, dec_proj, enc_proj), ((0, 16 - lat), (0, 0)))
    half = jnp.pad((levels.astype(F32) - 1.0) * 0.5, (0, 16 - lat), constant_values=1.0)
    halves = jnp.broadcast_to(half[:, None], (16, LANES))

    part, hid_cat, slope, inner, w_cat, pos = pl.pallas_call(
        functools.partial(first_kernel, z, steps, piece_steps),
        out_shape=(
            shaped((8, z.count), F32),
            shaped((z.count, z.thin), BF16),
            shaped((z.sp, z.row, LANES), F32),
            shaped((z.sp, z.row, LANES), BF16),
            shaped((chans, z.wide), BF16),
            shaped((z.count, LANES), BF16),
        ),
        in_specs=[ANY] * (3 * z.sp) + [VM] * 3,
        out_specs=(VM,) * 6,
        scratch_shapes=[
            pltpu.VMEM((z.count, chans), BF16),
            pltpu.VMEM((z.sp, 2, z.half_pad, z.wide), BF16),
            pltpu.VMEM((z.sp, z.code_rows, z.wide), BF16),
            pltpu.VMEM((z.sp + 2, z.row, z.wide), F32),
            pltpu.VMEM((3, z.sp + 2, z.row, LANES), BF16),
            pltpu.VMEM((z.count, z.wide), BF16),
            pltpu.VMEM((z.count, z.thin), F32),
            pltpu.SemaphoreType.DMA((z.sp,)),
            pltpu.SemaphoreType.DMA((3, z.sp)),
        ],
        compiler_params=params,
        name="first",
    )(*shards, *mine, *other, wt, proj, halves)
    swap = [(0, 1), (1, 0)]
    total = swap_sum(part, "sp")
    received = lax.ppermute(total, "sec", swap)
    big, time, part = pl.pallas_call(
        functools.partial(second_kernel, z, steps, scale),
        out_shape=(
            shaped((chans, z.wide), BF16),
            shaped((3 * own, chans), F32),
            shaped((8, chans), F32),
        ),
        in_specs=[ANY] * z.sp + [VM] * 10,
        out_specs=(VM,) * 3,
        scratch_shapes=[
            pltpu.VMEM((z.count, chans), BF16),
            pltpu.VMEM((3, z.sp + 2, z.row, LANES), BF16),
            pltpu.VMEM((z.count, z.wide), BF16),
            pltpu.VMEM((z.count, z.thin), F32),
            pltpu.SemaphoreType.DMA((z.sp,)),
        ],
        compiler_params=params,
        name="second",
    )(*shards, w_cat, pos, wt, proj, halves, hid_cat, slope, inner, total, received)
    big = lax.all_to_all(big.reshape(z.sp, own, z.wide), "sp", 0, 0, tiled=True)
    space, time, carried = pl.pallas_call(
        functools.partial(last_kernel, z),
        out_shape=(
            shaped((9, own, chans), F32),
            shaped((3 * own, chans), F32),
            shaped((8, chans), F32),
        ),
        in_specs=[VM] * 4,
        out_specs=(VM,) * 3,
        compiler_params=params,
        name="last",
    )(big, lax.ppermute(big, "dp", swap), time, lax.ppermute(time, "dp", swap))
    if z.carries:
        part = carried
    else:
        part = swap_sum(part, "sp")
        part = part + lax.ppermute(part, "dp", swap)
    return space[None], time.reshape(1, 3, own, chans), part[None, :lat]


def solution(mesh):
    placed = (
        P("sec", "dp", None, "sp", None, None),
        P("dp", None, None, "sp", None),
        P(),
        P("sec", None, "sp", None),
        P("sec", None, "sp", None),
        P(),
        P(),
    )
    return jax.shard_map(
        local,
        mesh=mesh,
        in_specs=placed,
        out_specs=(P("sec", None, "sp", None), P("sec", None, "sp", None), P("sec", None, None)),
        check_vma=False,
    )
```

```python
import functools

import jax
import jax.numpy as jnp
from jax import lax
from jax.experimental import pallas as pl
from jax.experimental.pallas import tpu as pltpu
from jax.sharding import PartitionSpec as P

F32 = jnp.float32
BF16 = jnp.bfloat16
LANES = 128
NN = (((1,), (0,)), ((), ()))
NT = (((1,), (1,)), ((), ()))
TN = (((0,), (0,)), ((), ()))


def up_to(value, multiple):
    return -(-value // multiple) * multiple


def ring_place(index, count):
    return jnp.where(index % 2 == 0, index // 2, count - (index + 1) // 2)


def ring_device(place, count):
    place = lax.rem(place + 2 * count, count)
    return jnp.where(place < count // 2, 2 * place, 2 * (count - place) - 1)


def ring_maps(count):
    order = list(range(0, count, 2)) + list(range(count - 1, 0, -2))
    forward = [(order[i], order[(i + 1) % count]) for i in range(count)]
    return forward, [(target, source) for source, target in forward]


def ring_exchange(shard, ahead, behind, own_piece):
    count = lax.axis_size("sp")
    up, down = ring_maps(count)
    swap = [(0, 1), (1, 0)]
    shards, shard_steps = [shard], [0]
    mine, piece_steps, other = [own_piece], [0], []
    first = second = shard

    def meet():
        fresh = mine[len(other) :]
        both = lax.ppermute(jnp.stack(fresh), "dp", swap)
        other.extend(both[i] for i in range(len(fresh)))

    for step in range(1, count // 2 + 1):
        first = lax.ppermute(first, "sp", up)
        shards.append(first)
        shard_steps.append(-step)
        last = step == count - step
        if not last:
            second = lax.ppermute(second, "sp", down)
            shards.append(second)
            shard_steps.append(step)
            ahead = lax.ppermute(ahead, "sp", up)
            mine.append(ahead[0])
            piece_steps.append(-step)
            ahead = ahead[1:]
        behind = lax.ppermute(behind, "sp", down)
        mine.append(behind[0])
        piece_steps.append(step)
        behind = behind[1:]
        if last or step % 2 == 0:
            meet()
    return shards, shard_steps, mine, other, piece_steps


def swap_sum(values, axis):
    count = lax.axis_size(axis)
    bit = 1
    while bit < count:
        values = values + lax.ppermute(values, axis, [(i, i ^ bit) for i in range(count)])
        bit *= 2
    return values


def dot(left, right, dims):
    return lax.dot_general(left, right, dims, preferred_element_type=F32)


def thirds(values):
    high = values.astype(BF16).astype(F32)
    rest = values - high
    middle = rest.astype(BF16).astype(F32)
    return high, middle, rest - middle


def stack3(values):
    return jnp.concatenate(thirds(values), axis=0).astype(BF16)


def sum3(stacked):
    rows = stacked.shape[0] // 3
    return stacked[:rows] + stacked[rows : 2 * rows] + stacked[2 * rows :]


def lanes_down(values, by):
    by = by % LANES
    return values if by == 0 else pltpu.roll(values, LANES - by, 1)


def spots(parts, own):
    return [((p * own) // LANES, (p * own) % LANES) for p in range(parts)]


def col_move(values, by, cols):
    if by == 0:
        return values
    rows = values.shape[0]
    col = lax.broadcasted_iota(jnp.int32, values.shape, 0) % cols
    edge = 0 if by > 0 else cols - 1
    return jnp.where(col == edge, 0.0, pltpu.roll(values, by % rows, 0))


def frames_move(values, by, cols):
    if by == 0:
        return values
    zeros = jnp.zeros((abs(by) * cols, values.shape[1]), values.dtype)
    if by > 0:
        return jnp.concatenate([zeros, values[: -by * cols]], axis=0)
    return jnp.concatenate([values[-by * cols :], zeros], axis=0)


def merge(pieces, own):
    blocks = [None] * (spots(len(pieces), own)[-1][0] + 1)
    for piece, (block, offset) in zip(pieces, spots(len(pieces), own)):
        moved = lanes_down(piece, -offset)
        blocks[block] = moved if blocks[block] is None else blocks[block] + moved
    return blocks


class Sizes:
    def __init__(self, sp, frames, cols, chans, own, lat):
        self.sp, self.frames, self.cols = sp, frames, cols
        self.chans, self.own, self.lat = chans, own, lat
        self.row = frames * cols
        self.count = sp * self.row
        self.wide = up_to(9 * own, LANES)
        self.thin = up_to(3 * own + 8, LANES)
        self.copies = min(3, LANES // own)
        self.half = own // 2
        code_rows = frames * lat
        self.code_rows = up_to(code_rows, 16)
        self.half_pad = up_to(self.half, 16)
        if self.wide - 9 * own >= cols and self.half >= code_rows:
            self.code_row, self.code_lane = 0, 9 * own
            self.piece_rows = self.half
        else:
            self.code_row, self.code_lane = up_to(self.half, 16), 0
            self.piece_rows = self.code_row + up_to(code_rows, 16)
        self.carries = self.wide - 9 * own >= LANES // 2 and own * (LANES // 2) >= 8 * chans


def place_shards(z, steps, shards, v):
    place = ring_place(lax.axis_index("sp"), z.sp)
    for shard, step in zip(shards, steps):
        v[rows_at(ring_device(place + step, z.sp), z)] = shard[...]


def place_pieces(z, steps, mine, other, w_cat, codes):
    place = ring_place(lax.axis_index("sp"), z.sp)
    core = lax.axis_index("dp")
    for one, two, step in zip(mine, other, steps):
        device = ring_device(place + step, z.sp)
        start = pl.multiple_of(device * z.own, z.own)
        codes[device] = one[z.code_row : z.code_row + z.code_rows]
        low = jnp.where(core == 0, one[: z.half], two[: z.half])
        high = jnp.where(core == 0, two[: z.half], one[: z.half])
        if z.half == z.half_pad:
            w_cat[pl.ds(start, z.half)] = low
            w_cat[pl.ds(start + z.half, z.half)] = high
        else:
            both = jnp.concatenate([low.astype(F32), high.astype(F32)], axis=0)
            w_cat[pl.ds(start, z.own)] = both.astype(BF16)


def each_row(z, body):
    if z.sp <= 8:
        for r in range(z.sp):
            body(r)
    else:

        def step(r, carry):
            body(r)
            return carry

        lax.fori_loop(0, z.sp, step, 0)


def rows_at(r, z):
    if isinstance(r, int):
        return pl.ds(r * z.row, z.row)
    return pl.ds(pl.multiple_of(r * z.row, z.row), z.row)


def rows_from(r0, rows, z):
    if isinstance(r0, int):
        return pl.ds(r0 * z.row, rows * z.row)
    return pl.ds(pl.multiple_of(r0 * z.row, rows * z.row), rows * z.row)


def conv_row(z, taps, r):
    total = None
    for j in range(3):
        by_offset = {}
        for i in range(3):
            block, offset = spots(9, z.own)[3 * i + j]
            value = taps[r + i, :, block * LANES : (block + 1) * LANES]
            by_offset[offset] = by_offset.get(offset, 0.0) + value
        column = sum(lanes_down(value, offset) for offset, value in by_offset.items())
        column = col_move(column, 1 - j, z.cols)
        total = column if total is None else total + column
    return total


def later_row(z, taps, r):
    total = None
    for k, (block, offset) in enumerate(spots(3, z.own)):
        value = taps[rows_at(r, z), block * LANES : (block + 1) * LANES]
        value = frames_move(lanes_down(value, offset), -k, z.cols)
        total = value if total is None else total + value
    return total


def keep_own(z, values):
    lane = lax.broadcasted_iota(jnp.int32, values.shape, 1)
    return jnp.where(lane < z.own, values, 0.0)


def put_shifts(z, inner, shifts, r):
    for j in range(3):
        shifts[j, r + 1] = col_move(inner, j - 1, z.cols).astype(BF16)


def spread(z, shifts, inner_cat):
    def body(r):
        pieces = [
            shifts[j, r + 2 - i].astype(F32) for i in range(3) for j in range(3)
        ]
        for b, block in enumerate(merge(pieces, z.own)):
            inner_cat[rows_at(r, z), b * LANES : (b + 1) * LANES] = block.astype(BF16)

    each_row(z, body)


def zero_ends(z, padded):
    padded[0] = jnp.zeros(padded.shape[1:], padded.dtype)
    padded[z.sp + 1] = jnp.zeros(padded.shape[1:], padded.dtype)


def in_blocks(z, action):
    step = 8 if z.sp % 8 == 0 else 1
    if z.sp == step:
        action(0, step)
    else:

        def body(b, carry):
            action(b * step, step)
            return carry

        lax.fori_loop(0, z.sp // step, body, 0)


def position_codes(z, codes, out):
    block, offset = z.code_lane // LANES, z.code_lane % LANES

    def body(r):
        raw = codes[r, :, block * LANES : (block + 1) * LANES].astype(F32)
        raw = jnp.concatenate([raw, jnp.zeros((LANES - z.code_rows, LANES), F32)], axis=0)
        turned = raw.T[offset : offset + z.cols]
        lane = lax.broadcasted_iota(jnp.int32, turned.shape, 1)
        frames = []
        for t in range(z.frames):
            values = lanes_down(turned, t * z.lat)
            values = jnp.where(lane < z.lat, values, jnp.where(lane == z.lat, 1.0, 0.0))
            frames.append(
                values + pltpu.roll(values, 16, 1) + pltpu.roll(values, 32, 1)
            )
        out[rows_at(r, z)] = jnp.concatenate(frames, axis=0).astype(BF16)

    each_row(z, body)


def piece_kernel(z, w, codes, ahead, behind, own_piece):
    place = ring_place(lax.axis_index("sp"), z.sp)
    core = lax.axis_index("dp")
    lane = lax.broadcasted_iota(jnp.int32, (z.half, LANES), 1)
    code_block = codes[...]
    for j in range(z.sp):
        block, offset = (j * z.own) // LANES, (j * z.own) % LANES
        taps = []
        for tap in range(9):
            at = slice(block * LANES, (block + 1) * LANES)
            if z.half == z.half_pad:
                value = w[tap, pl.ds(pl.multiple_of(core * z.half, z.half), z.half), at]
                value = value.astype(F32)
            else:
                value = w[tap, :, at].astype(F32)
                value = jnp.where(core == 0, value[: z.half], value[z.half :])
            value = lanes_down(value, offset)
            taps.append(jnp.where(lane < z.own, value, 0.0))
        blocks = merge(taps, z.own)
        if z.code_row == 0:
            blocks[-1] = blocks[-1] + code_block
        distance = lax.rem(ring_place(jnp.int32(j), z.sp) - place + z.sp, z.sp)

        def store(target, index):
            for b, value in enumerate(blocks):
                at = slice(b * LANES, (b + 1) * LANES)
                if index is None:
                    target[: z.half, at] = value.astype(BF16)
                else:
                    target[index, : z.half, at] = value.astype(BF16)
            if z.code_row:
                tail = slice(z.code_row, z.piece_rows)
                if index is None:
                    target[tail, :LANES] = code_block.astype(BF16)
                else:
                    target[index, tail, :LANES] = code_block.astype(BF16)

        @pl.when(distance == 0)
        def _():
            store(own_piece, None)

        @pl.when(jnp.logical_and(distance > 0, distance < z.sp // 2))
        def _():
            store(ahead, distance - 1)

        @pl.when(distance >= z.sp // 2)
        def _():
            store(behind, z.sp - distance - 1)


def first_kernel(z, steps, piece_steps, *refs):
    n = z.sp
    shards, mine, other = refs[:n], refs[n : 2 * n], refs[2 * n : 3 * n]
    wt, proj, halves = refs[3 * n : 3 * n + 3]
    part, hid_cat, slope, inner_out, w_cat, pos, v = refs[3 * n + 3 : 3 * n + 10]
    codes, taps, back, spots_of, thin = refs[3 * n + 10 :]
    decoder = lax.axis_index("sec") == 1
    first = lax.axis_index("sp") == 0
    zero_ends(z, taps)
    place_shards(z, steps, shards, v)
    place_pieces(z, piece_steps, mine, other, w_cat, codes)

    def store_hidden(pre, logistic, r):
        hidden = keep_own(z, (pre * logistic).astype(BF16).astype(F32))
        moved = [frames_move(hidden, k, z.cols) for k in range(3)]
        for b, block in enumerate(merge(moved, z.own)):
            hid_cat[rows_at(r, z), b * LANES : (b + 1) * LANES] = block.astype(BF16)

    @pl.when(decoder)
    def _():
        zero_ends(z, back)
        p_cat = dot(proj[...], w_cat[...], NN)
        half = halves[:, :1]
        row = lax.broadcasted_iota(jnp.int32, p_cat.shape, 0)
        scaled = jnp.where(
            row == z.lat, -jnp.sum(p_cat, axis=0, keepdims=True), p_cat / half
        )
        table = jnp.concatenate(
            list(thirds(scaled)) + [jnp.zeros((LANES - 48, z.wide), F32)], axis=0
        ).astype(BF16)
        position_codes(z, codes, pos)
        by_tap = [
            keep_own(z, lanes_down(p_cat[:8, block * LANES : (block + 1) * LANES], offset))
            for block, offset in spots(9, z.own)
        ]
        by_tap = jnp.concatenate(by_tap + [jnp.zeros((LANES - 72, LANES), F32)], axis=0)
        by_tap = sum(
            lanes_down(term, -c * z.own) for c, term in enumerate(thirds(by_tap)[: z.copies])
        ).astype(BF16)

        def block(r0, rows):
            place = rows_from(r0, rows, z)
            taps[pl.ds(r0 + 1, rows)] = dot(pos[place], table, NN).reshape(rows, z.row, z.wide)
            thin[place] = dot(v[place], wt[...], NT)

        in_blocks(z, block)

        def body(r):
            pre = conv_row(z, taps, r)
            logistic = 1.0 / (1.0 + jnp.exp(-pre))
            store_hidden(pre, logistic, r)
            rate = logistic * (1.0 + pre * (1.0 - logistic))
            inner = keep_own(z, (later_row(z, thin, r) * rate).astype(BF16).astype(F32))
            inner_out[r] = inner.astype(BF16)
            many = sum(lanes_down(inner, -c * z.own) for c in range(z.copies))
            back[r + 1] = dot(many.astype(BF16), by_tap, NT)

        each_row(z, body)
        block_of, offset = (3 * z.own) // LANES, (3 * z.own) % LANES

        def collect(r):
            lane = lax.broadcasted_iota(jnp.int32, (z.row, LANES), 1)
            value = jnp.where(lane < 24, back[r + 2], jnp.where(lane < 48, back[r + 1], back[r]))
            j = (lane // 8) % 3
            moved = jnp.where(
                j == 0,
                col_move(value, -1, z.cols),
                jnp.where(j == 1, value, col_move(value, 1, z.cols)),
            )
            whole = thin[rows_at(r, z), block_of * LANES : (block_of + 1) * LANES]
            whole = jnp.where(first, lanes_down(whole, offset - 72), 0.0)
            spots_of[rows_at(r, z)] = jnp.where(lane < 72, moved, whole)

        each_row(z, collect)
        turned = spots_of[...].T
        part[...] = sum(turned[8 * g : 8 * g + 8] for g in range(10))

    @pl.when(jnp.logical_not(decoder))
    def _():
        def block(r0, rows):
            place = rows_from(r0, rows, z)
            taps[pl.ds(r0 + 1, rows)] = dot(v[place], w_cat[...], NN).reshape(
                rows, z.row, z.wide
            )

        in_blocks(z, block)

        def body(r):
            pre = conv_row(z, taps, r)
            logistic = 1.0 / (1.0 + jnp.exp(-pre))
            store_hidden(pre, logistic, r)
            slope[r] = logistic * (1.0 + pre * (1.0 - logistic))

        each_row(z, body)
        weights = dot(proj[...], wt[...], NT)[:8]
        whole = dot(proj[...], v[...], NT)[:8]
        part[...] = sum3(dot(stack3(weights), hid_cat[...], NT)) + jnp.where(first, whole, 0.0)


def second_kernel(z, scale, *refs):
    v, w_cat, pos, wt, proj, halves, hid_cat, slope, inner_in, total, received = refs[:11]
    big, time, part = refs[11:14]
    shifts, inner_cat, thin = refs[14:]
    decoder = lax.axis_index("sec") == 1
    first = lax.axis_index("sp") == 0
    for j in range(3):
        zero_ends(z, shifts.at[j])

    def put_out(kernel_grad, proj_part):
        part[...] = proj_part
        if not z.carries:
            big[...] = kernel_grad.astype(BF16)
            return
        side = z.wide - LANES
        big[:, :side] = kernel_grad[:, :side].astype(BF16)
        pieces = []
        for b in range(2 * z.chans // LANES):
            block = proj_part[:, (b // 2) * LANES : (b // 2 + 1) * LANES]
            pieces.append(block if b % 2 else pltpu.roll(block, LANES // 2, 1))
        carried = jnp.concatenate(pieces, axis=0)
        lane = lax.broadcasted_iota(jnp.int32, carried.shape, 1)
        for j in range(z.sp):
            rows = slice(j * z.own, (j + 1) * z.own)
            big[rows, side:] = jnp.where(
                lane < LANES // 2, kernel_grad[rows, side:], carried
            ).astype(BF16)

    @pl.when(decoder)
    def _():
        def body(r):
            put_shifts(z, inner_in[r].astype(F32), shifts, r)

        each_row(z, body)
        spread(z, shifts, inner_cat)
        half = halves[:8, :1]

        def latent_rows(raw):
            row = lax.broadcasted_iota(jnp.int32, raw.shape, 0)
            return jnp.where(row < z.lat, raw / half - raw[z.lat : z.lat + 1], 0.0)

        short = latent_rows(dot(pos[...], inner_cat[...], TN)[:8])
        proj8 = proj[:8].astype(F32)
        proj24 = jnp.concatenate([proj8] * 3, axis=0).astype(BF16)
        kernel_grad = dot(proj24, stack3(short), TN) * scale
        time[...] = dot(hid_cat[...], v[...], TN)[: 3 * z.own] * scale
        whole = latent_rows(dot(pos[...], v[...], TN)[:8])
        partial = sum3(dot(stack3(short), w_cat[...], NT))
        put_out(kernel_grad, (partial + jnp.where(first, whole, 0.0)) * scale)

    @pl.when(jnp.logical_not(decoder))
    def _():
        bounded = jnp.tanh(total[...])
        grad = received[...] * (1.0 - bounded * bounded)
        back = dot(proj[...], wt[...], NT)[:8]
        gh, gm, gl = thirds(grad)
        bh, bm, bl = thirds(back)
        left = jnp.concatenate([gh, gh, gm, gh, gl, gm], axis=0).astype(BF16)
        right = jnp.concatenate([bh, bm, bh, bl, bh, bm], axis=0).astype(BF16)
        thin[...] = dot(left, right, TN)

        def body(r):
            inner = keep_own(z, later_row(z, thin, r) * slope[r])
            put_shifts(z, inner, shifts, r)

        each_row(z, body)
        spread(z, shifts, inner_cat)
        kernel_grad = dot(v[...], inner_cat[...], TN) * scale
        grad3 = jnp.concatenate([gh, gm, gl], axis=0).astype(BF16)
        short = sum3(dot(grad3, hid_cat[...], NN))
        short3 = stack3(short)
        proj8 = proj[:8].astype(F32)
        proj24 = jnp.concatenate([proj8] * 3, axis=0).astype(BF16)
        time[...] = dot(short3, proj24, TN)[: 3 * z.own] * scale
        whole = sum3(dot(grad3, v[...], NN))
        partial = sum3(dot(short3, wt[...], NN))
        put_out(kernel_grad, (partial + jnp.where(first, whole, 0.0)) * scale)


def last_kernel(z, mine, other, time_mine, time_other, space, time, part):
    time[...] = time_mine[...] + time_other[...]
    if z.carries:
        side = slice(z.wide - LANES, z.wide)
        carried = 0.0
        for j in range(z.sp):
            carried = carried + (mine[j, :, side].astype(F32) + other[j, :, side].astype(F32))
        lane = lax.broadcasted_iota(jnp.int32, (8, LANES), 1)
        for m in range(z.chans // LANES):
            low = pltpu.roll(carried[16 * m : 16 * m + 8], LANES // 2, 1)
            high = carried[16 * m + 8 : 16 * m + 16]
            both = jnp.where(lane < LANES // 2, low, high)
            part[:, m * LANES : (m + 1) * LANES] = both[: z.lat]
    else:
        part[...] = jnp.zeros(part.shape, F32)
    per = LANES // z.own
    for tap, (block, offset) in enumerate(spots(9, z.own)):
        for m in range(z.chans // LANES):
            total = None
            for p in range(per):
                at = (m * per + p, slice(None), slice(block * LANES, (block + 1) * LANES))
                value = mine[at].astype(F32) + other[at].astype(F32)
                value = lanes_down(value, offset - p * z.own)
                if total is None:
                    total = value
                else:
                    lane = lax.broadcasted_iota(jnp.int32, value.shape, 1)
                    total = jnp.where(lane < p * z.own, total, value)
            space[tap, :, m * LANES : (m + 1) * LANES] = total


VM = pl.BlockSpec(memory_space=pltpu.VMEM)


def shaped(shape, dtype):
    return jax.ShapeDtypeStruct(shape, dtype)


def local(block_data, code_index, levels, w_space, w_time, enc_proj, dec_proj):
    frames, cols, chans = block_data.shape[2], block_data.shape[4], block_data.shape[5]
    lat, own = code_index.shape[1], w_space.shape[2]
    z = Sizes(lax.axis_size("sp"), frames, cols, chans, own, lat)
    scale = float(lax.axis_size("dp") * z.count) ** (-0.5)
    decoder = lax.axis_index("sec") == 1
    room = 20 * 1024 * 1024 + 5 * z.count * chans * 4 // 2 * (1 if z.sp > 8 else 0)
    params = pltpu.CompilerParams(vmem_limit_bytes=min(room, 60 * 1024 * 1024))

    codes = jnp.transpose(code_index[0, :, :, 0], (1, 0, 2)).reshape(frames * lat, cols)
    left = z.code_lane % LANES
    codes = jnp.pad(
        codes.astype(F32),
        ((0, (z.half if z.code_row == 0 else z.code_rows) - frames * lat), (left, LANES - left - cols)),
    )
    ahead, behind, own_piece = pl.pallas_call(
        functools.partial(piece_kernel, z),
        out_shape=(
            shaped((z.sp // 2 - 1, z.piece_rows, z.wide), BF16),
            shaped((z.sp // 2, z.piece_rows, z.wide), BF16),
            shaped((z.piece_rows, z.wide), BF16),
        ),
        in_specs=[VM] * 2,
        out_specs=(VM,) * 3,
        compiler_params=params,
        name="pieces",
    )(w_space[0], codes)
    shards, steps, mine, other, piece_steps = ring_exchange(
        block_data.reshape(z.row, chans), ahead, behind, own_piece
    )
    proj = jnp.pad(jnp.where(decoder, dec_proj, enc_proj), ((0, 16 - lat), (0, 0)))
    wt = jnp.concatenate([w_time.reshape(3 * own, chans), proj[:8]], axis=0)
    wt = jnp.pad(wt, ((0, z.thin - 3 * own - 8), (0, 0)))
    half = jnp.pad((levels.astype(F32) - 1.0) * 0.5, (0, 16 - lat), constant_values=1.0)
    halves = jnp.broadcast_to(half[:, None], (16, LANES))

    part, hid_cat, slope, inner, w_cat, pos, v = pl.pallas_call(
        functools.partial(first_kernel, z, steps, piece_steps),
        out_shape=(
            shaped((8, z.count), F32),
            shaped((z.count, z.thin), BF16),
            shaped((z.sp, z.row, LANES), F32),
            shaped((z.sp, z.row, LANES), BF16),
            shaped((chans, z.wide), BF16),
            shaped((z.count, LANES), BF16),
            shaped((z.count, chans), BF16),
        ),
        in_specs=[VM] * (3 * z.sp + 3),
        out_specs=(VM,) * 7,
        scratch_shapes=[
            pltpu.VMEM((z.sp, z.code_rows, z.wide), BF16),
            pltpu.VMEM((z.sp + 2, z.row, z.wide), F32),
            pltpu.VMEM((z.sp + 2, z.row, LANES), F32),
            pltpu.VMEM((z.count, LANES), F32),
            pltpu.VMEM((z.count, z.thin), F32),
        ],
        compiler_params=params,
        name="first",
    )(*shards, *mine, *other, wt, proj, halves)
    swap = [(0, 1), (1, 0)]
    total = swap_sum(part, "sp")
    received = lax.ppermute(total, "sec", swap)
    big, time, part = pl.pallas_call(
        functools.partial(second_kernel, z, scale),
        out_shape=(
            shaped((chans, z.wide), BF16),
            shaped((3 * own, chans), F32),
            shaped((8, chans), F32),
        ),
        in_specs=[VM] * 11,
        out_specs=(VM,) * 3,
        scratch_shapes=[
            pltpu.VMEM((3, z.sp + 2, z.row, LANES), BF16),
            pltpu.VMEM((z.count, z.wide), BF16),
            pltpu.VMEM((z.count, z.thin), F32),
        ],
        compiler_params=params,
        name="second",
    )(v, w_cat, pos, wt, proj, halves, hid_cat, slope, inner, total, received)
    big = lax.all_to_all(big.reshape(z.sp, own, z.wide), "sp", 0, 0, tiled=True)
    space, time, carried = pl.pallas_call(
        functools.partial(last_kernel, z),
        out_shape=(
            shaped((9, own, chans), F32),
            shaped((3 * own, chans), F32),
            shaped((lat, chans), F32),
        ),
        in_specs=[VM] * 4,
        out_specs=(VM,) * 3,
        compiler_params=params,
        name="last",
    )(big, lax.ppermute(big, "dp", swap), time, lax.ppermute(time, "dp", swap))
    if z.carries:
        part = carried
    else:
        part = swap_sum(part, "sp")
        part = (part + lax.ppermute(part, "dp", swap))[:lat]
    return space[None], time.reshape(1, 3, own, chans), part[None]


def solution(mesh):
    placed = (
        P("sec", "dp", None, "sp", None, None),
        P("dp", None, None, "sp", None),
        P(),
        P("sec", None, "sp", None),
        P("sec", None, "sp", None),
        P(),
        P(),
    )
    return jax.shard_map(
        local,
        mesh=mesh,
        in_specs=placed,
        out_specs=(P("sec", None, "sp", None), P("sec", None, "sp", None), P("sec", None, None)),
        check_vma=False,
    )
```

```python
import functools

import jax
import jax.numpy as jnp
from jax import lax
from jax.experimental import pallas as pl
from jax.experimental.pallas import tpu as pltpu
from jax.sharding import PartitionSpec as P

F32 = jnp.float32
BF16 = jnp.bfloat16
LANES = 128
NN = (((1,), (0,)), ((), ()))
NT = (((1,), (1,)), ((), ()))
TN = (((0,), (0,)), ((), ()))


def up_to(value, multiple):
    return -(-value // multiple) * multiple


def ring_place(index, count):
    return jnp.where(index % 2 == 0, index // 2, count - (index + 1) // 2)


def ring_device(place, count):
    place = lax.rem(place + 2 * count, count)
    return jnp.where(place < count // 2, 2 * place, 2 * (count - place) - 1)


def ring_maps(count):
    order = list(range(0, count, 2)) + list(range(count - 1, 0, -2))
    forward = [(order[i], order[(i + 1) % count]) for i in range(count)]
    return forward, [(target, source) for source, target in forward]


def ring_exchange(shard, ahead, behind, own_piece):
    count = lax.axis_size("sp")
    up, down = ring_maps(count)
    swap = [(0, 1), (1, 0)]
    shards, shard_steps = [shard], [0]
    mine, piece_steps, other = [own_piece], [0], []
    first = second = shard

    def meet():
        fresh = mine[len(other) :]
        both = lax.ppermute(jnp.stack(fresh), "dp", swap)
        other.extend(both[i] for i in range(len(fresh)))

    for step in range(1, count // 2 + 1):
        first = lax.ppermute(first, "sp", up)
        shards.append(first)
        shard_steps.append(-step)
        last = step == count - step
        if not last:
            second = lax.ppermute(second, "sp", down)
            shards.append(second)
            shard_steps.append(step)
            ahead = lax.ppermute(ahead, "sp", up)
            mine.append(ahead[0])
            piece_steps.append(-step)
            ahead = ahead[1:]
        behind = lax.ppermute(behind, "sp", down)
        mine.append(behind[0])
        piece_steps.append(step)
        behind = behind[1:]
        if last or step % 2 == 0:
            meet()
    return shards, shard_steps, mine, other, piece_steps


def swap_sum(values, axis):
    count = lax.axis_size(axis)
    bit = 1
    while bit < count:
        values = values + lax.ppermute(values, axis, [(i, i ^ bit) for i in range(count)])
        bit *= 2
    return values


def dot(left, right, dims):
    return lax.dot_general(left, right, dims, preferred_element_type=F32)


def thirds(values):
    high = values.astype(BF16).astype(F32)
    rest = values - high
    middle = rest.astype(BF16).astype(F32)
    return high, middle, rest - middle


def stack3(values):
    return jnp.concatenate(thirds(values), axis=0).astype(BF16)


def sum3(stacked):
    rows = stacked.shape[0] // 3
    return stacked[:rows] + stacked[rows : 2 * rows] + stacked[2 * rows :]


def lanes_down(values, by):
    by = by % LANES
    return values if by == 0 else pltpu.roll(values, LANES - by, 1)


def spots(parts, own):
    return [((p * own) // LANES, (p * own) % LANES) for p in range(parts)]


def col_move(values, by, cols):
    if by == 0:
        return values
    rows = values.shape[0]
    col = lax.broadcasted_iota(jnp.int32, values.shape, 0) % cols
    edge = 0 if by > 0 else cols - 1
    return jnp.where(col == edge, 0.0, pltpu.roll(values, by % rows, 0))


def frames_move(values, by, cols):
    if by == 0:
        return values
    zeros = jnp.zeros((abs(by) * cols, values.shape[1]), values.dtype)
    if by > 0:
        return jnp.concatenate([zeros, values[: -by * cols]], axis=0)
    return jnp.concatenate([values[-by * cols :], zeros], axis=0)


def merge(pieces, own):
    blocks = [None] * (spots(len(pieces), own)[-1][0] + 1)
    for piece, (block, offset) in zip(pieces, spots(len(pieces), own)):
        moved = lanes_down(piece, -offset)
        blocks[block] = moved if blocks[block] is None else blocks[block] + moved
    return blocks


class Sizes:
    def __init__(self, sp, frames, cols, chans, own, lat):
        self.sp, self.frames, self.cols = sp, frames, cols
        self.chans, self.own, self.lat = chans, own, lat
        self.row = frames * cols
        self.count = sp * self.row
        self.wide = up_to(9 * own, LANES)
        self.thin = up_to(3 * own + 8, LANES)
        self.copies = min(3, LANES // own)
        self.half = own // 2
        self.half_pad = up_to(self.half, 16)
        self.code_rows = up_to(cols, 16)
        if self.wide - 9 * own >= 8 * frames and self.half >= cols:
            self.code_row, self.code_lane = 0, 9 * own
            self.piece_rows = self.half
        else:
            self.code_row, self.code_lane = self.half_pad, 0
            self.piece_rows = self.code_row + self.code_rows
        self.split = self.half == self.half_pad
        self.carries = self.wide - 9 * own >= LANES // 2 and own * (LANES // 2) >= 8 * chans


def place_shards(z, steps, shards, v):
    place = ring_place(lax.axis_index("sp"), z.sp)
    for shard, step in zip(shards, steps):
        v[rows_at(ring_device(place + step, z.sp), z)] = shard[...]


def place_pieces(z, steps, mine, other, w_cat, codes):
    place = ring_place(lax.axis_index("sp"), z.sp)
    core = lax.axis_index("dp")
    for one, two, step in zip(mine, other, steps):
        device = ring_device(place + step, z.sp)
        start = pl.multiple_of(device * z.own, z.own)
        codes[device] = one[z.code_row : z.code_row + z.code_rows]
        low = jnp.where(core == 0, one[: z.half], two[: z.half])
        high = jnp.where(core == 0, two[: z.half], one[: z.half])
        if z.half == z.half_pad:
            w_cat[pl.ds(start, z.half)] = low
            w_cat[pl.ds(start + z.half, z.half)] = high
        else:
            both = jnp.concatenate([low.astype(F32), high.astype(F32)], axis=0)
            w_cat[pl.ds(start, z.own)] = both.astype(BF16)


def each_row(z, body):
    if z.sp <= 8:
        for r in range(z.sp):
            body(r)
    else:

        def step(r, carry):
            body(r)
            return carry

        lax.fori_loop(0, z.sp, step, 0)


def rows_at(r, z):
    if isinstance(r, int):
        return pl.ds(r * z.row, z.row)
    return pl.ds(pl.multiple_of(r * z.row, z.row), z.row)


def rows_from(r0, rows, z):
    if isinstance(r0, int):
        return pl.ds(r0 * z.row, rows * z.row)
    return pl.ds(pl.multiple_of(r0 * z.row, rows * z.row), rows * z.row)


def conv_row(z, taps, r):
    total = None
    for j in range(3):
        by_offset = {}
        for i in range(3):
            block, offset = spots(9, z.own)[3 * i + j]
            value = taps[r + i, :, block * LANES : (block + 1) * LANES]
            by_offset[offset] = by_offset.get(offset, 0.0) + value
        column = sum(lanes_down(value, offset) for offset, value in by_offset.items())
        column = col_move(column, 1 - j, z.cols)
        total = column if total is None else total + column
    return total


def later_row(z, taps, r):
    total = None
    for k, (block, offset) in enumerate(spots(3, z.own)):
        value = taps[rows_at(r, z), block * LANES : (block + 1) * LANES]
        value = frames_move(lanes_down(value, offset), -k, z.cols)
        total = value if total is None else total + value
    return total


def keep_own(z, values):
    lane = lax.broadcasted_iota(jnp.int32, values.shape, 1)
    return jnp.where(lane < z.own, values, 0.0)


def put_shifts(z, inner, shifts, r):
    for j in range(3):
        shifts[j, r + 1] = col_move(inner, j - 1, z.cols).astype(BF16)


def spread(z, shifts, inner_cat):
    def body(r):
        pieces = [
            shifts[j, r + 2 - i].astype(F32) for i in range(3) for j in range(3)
        ]
        for b, block in enumerate(merge(pieces, z.own)):
            inner_cat[rows_at(r, z), b * LANES : (b + 1) * LANES] = block.astype(BF16)

    each_row(z, body)


def zero_ends(z, padded):
    padded[0] = jnp.zeros(padded.shape[1:], padded.dtype)
    padded[z.sp + 1] = jnp.zeros(padded.shape[1:], padded.dtype)


def in_blocks(z, action):
    step = 8 if z.sp % 8 == 0 else 1
    if z.sp == step:
        action(0, step)
    else:

        def body(b, carry):
            action(b * step, step)
            return carry

        lax.fori_loop(0, z.sp // step, body, 0)


def position_codes(z, codes, out):
    block, offset = z.code_lane // LANES, z.code_lane % LANES
    run = 8 * z.frames

    def body(r):
        raw = codes[r, : z.cols, block * LANES : (block + 1) * LANES].astype(F32)
        lane = lax.broadcasted_iota(jnp.int32, raw.shape, 1)
        raw = jnp.where(lane < run, lanes_down(raw, offset), 0.0)
        raw = raw + pltpu.roll(raw, run, 1) + pltpu.roll(raw, 2 * run, 1)
        frame = (lane % run) // 8
        blocks = [jnp.where(frame == t, raw, 0.0) for t in range(z.frames)]
        out[rows_at(r, z)] = jnp.concatenate(blocks, axis=0).astype(BF16)

    each_row(z, body)


def frame_sum(z, raw):
    return sum(raw[8 * t : 8 * t + 8] for t in range(z.frames))


def piece_kernel(z, w, codes, ahead, behind, own_piece):
    place = ring_place(lax.axis_index("sp"), z.sp)
    core = lax.axis_index("dp")
    lane = lax.broadcasted_iota(jnp.int32, (z.half, LANES), 1)
    code_block = codes[...]
    for j in range(z.sp):
        block, offset = (j * z.own) // LANES, (j * z.own) % LANES
        taps = []
        for tap in range(9):
            at = slice(block * LANES, (block + 1) * LANES)
            if z.half == z.half_pad:
                value = w[tap, pl.ds(pl.multiple_of(core * z.half, z.half), z.half), at]
                value = value.astype(F32)
            else:
                value = w[tap, :, at].astype(F32)
                value = jnp.where(core == 0, value[: z.half], value[z.half :])
            value = lanes_down(value, offset)
            taps.append(jnp.where(lane < z.own, value, 0.0))
        blocks = merge(taps, z.own)
        if z.code_row == 0:
            blocks[-1] = blocks[-1] + code_block
        distance = lax.rem(ring_place(jnp.int32(j), z.sp) - place + z.sp, z.sp)

        def store(target, index):
            for b, value in enumerate(blocks):
                at = slice(b * LANES, (b + 1) * LANES)
                if index is None:
                    target[: z.half, at] = value.astype(BF16)
                else:
                    target[index, : z.half, at] = value.astype(BF16)
            if z.code_row:
                tail = slice(z.code_row, z.piece_rows)
                if index is None:
                    target[tail, :LANES] = code_block.astype(BF16)
                else:
                    target[index, tail, :LANES] = code_block.astype(BF16)

        @pl.when(distance == 0)
        def _():
            store(own_piece, None)

        @pl.when(jnp.logical_and(distance > 0, distance < z.sp // 2))
        def _():
            store(ahead, distance - 1)

        @pl.when(distance >= z.sp // 2)
        def _():
            store(behind, z.sp - distance - 1)


def store_hidden(z, pre, logistic, hid_cat, r):
    hidden = keep_own(z, (pre * logistic).astype(BF16).astype(F32))
    moved = [frames_move(hidden, k, z.cols) for k in range(3)]
    for b, block in enumerate(merge(moved, z.own)):
        hid_cat[rows_at(r, z), b * LANES : (b + 1) * LANES] = block.astype(BF16)


def activate(z, taps, hid_cat, slope):
    def body(r):
        pre = conv_row(z, taps, r)
        logistic = 1.0 / (1.0 + jnp.exp(-pre))
        store_hidden(z, pre, logistic, hid_cat, r)
        slope[r] = logistic * (1.0 + pre * (1.0 - logistic))

    each_row(z, body)


def early_kernel(z, piece_steps, *refs):
    n = z.sp
    mine, other = refs[:n], refs[n : 2 * n]
    wt, proj, halves = refs[2 * n : 2 * n + 3]
    w_cat, pos, hid_cat, slope, table_out = refs[2 * n + 3 : 2 * n + 8]
    codes, taps = refs[2 * n + 8 :]
    decoder = lax.axis_index("sec") == 1
    place_pieces(z, piece_steps, mine, other, w_cat, codes)

    @pl.when(decoder)
    def _():
        zero_ends(z, taps)
        p_cat = dot(proj[...], w_cat[...], NN)[:8]
        half = halves[:8, :1]
        row = lax.broadcasted_iota(jnp.int32, p_cat.shape, 0)
        scaled = jnp.where(row == z.lat, -jnp.sum(p_cat, axis=0, keepdims=True), p_cat / half)
        table = [term for term in thirds(scaled) for _ in range(z.frames)]
        spare = jnp.zeros((LANES - 24 * z.frames, z.wide), F32)
        table = jnp.concatenate(table + [spare], axis=0).astype(BF16)
        position_codes(z, codes, pos)

        def block(r0, rows):
            place = rows_from(r0, rows, z)
            taps[pl.ds(r0 + 1, rows)] = dot(pos[place], table, NN).reshape(rows, z.row, z.wide)

        in_blocks(z, block)
        activate(z, taps, hid_cat, slope)
        by_tap = [
            keep_own(z, lanes_down(p_cat[:, block * LANES : (block + 1) * LANES], offset))
            for block, offset in spots(9, z.own)
        ]
        by_tap = jnp.concatenate(by_tap + [jnp.zeros((LANES - 72, LANES), F32)], axis=0)
        table_out[...] = sum(
            lanes_down(term, -c * z.own) for c, term in enumerate(thirds(by_tap)[: z.copies])
        )

    @pl.when(jnp.logical_not(decoder))
    def _():
        weights = dot(proj[...], wt[...], NT)[:8]
        table_out[:8] = weights[:, :LANES]
        table_out[8:16] = weights[:, LANES:] if z.thin > LANES else weights


def back_weights(z, table):
    if z.thin > LANES:
        return jnp.concatenate([table[:8], table[8:16]], axis=1)
    return table[:8]


def first_kernel(z, steps, *refs):
    n = z.sp
    shards, (w_cat, wt, proj, table, rate) = refs[:n], refs[n : n + 5]
    part, hid_cat, slope, inner_out, v = refs[n + 5 : n + 10]
    taps, back, spots_of, thin = refs[n + 10 :]
    decoder = lax.axis_index("sec") == 1
    first = lax.axis_index("sp") == 0
    place_shards(z, steps, shards, v)

    @pl.when(decoder)
    def _():
        zero_ends(z, back)
        by_tap = table[...].astype(BF16)

        def block(r0, rows):
            place = rows_from(r0, rows, z)
            thin[place] = dot(v[place], wt[...], NT)

        in_blocks(z, block)

        def body(r):
            inner = keep_own(z, (later_row(z, thin, r) * rate[r]).astype(BF16).astype(F32))
            inner_out[r] = inner.astype(BF16)
            many = sum(lanes_down(inner, -c * z.own) for c in range(z.copies))
            back[r + 1] = dot(many.astype(BF16), by_tap, NT)

        each_row(z, body)
        block_of, offset = (3 * z.own) // LANES, (3 * z.own) % LANES

        def collect(r):
            lane = lax.broadcasted_iota(jnp.int32, (z.row, LANES), 1)
            value = jnp.where(lane < 24, back[r + 2], jnp.where(lane < 48, back[r + 1], back[r]))
            j = (lane // 8) % 3
            moved = jnp.where(
                j == 0,
                col_move(value, -1, z.cols),
                jnp.where(j == 1, value, col_move(value, 1, z.cols)),
            )
            whole = thin[rows_at(r, z), block_of * LANES : (block_of + 1) * LANES]
            whole = jnp.where(first, lanes_down(whole, offset - 72), 0.0)
            spots_of[rows_at(r, z)] = jnp.where(lane < 72, moved, whole)

        each_row(z, collect)
        turned = spots_of[...].T
        part[...] = sum(turned[8 * g : 8 * g + 8] for g in range(10))

    @pl.when(jnp.logical_not(decoder))
    def _():
        zero_ends(z, taps)

        def block(r0, rows):
            place = rows_from(r0, rows, z)
            taps[pl.ds(r0 + 1, rows)] = dot(v[place], w_cat[...], NN).reshape(
                rows, z.row, z.wide
            )

        in_blocks(z, block)
        activate(z, taps, hid_cat, slope)
        weights = back_weights(z, table)
        whole = dot(proj[...], v[...], NT)[:8]
        part[...] = sum3(dot(stack3(weights), hid_cat[...], NT)) + jnp.where(first, whole, 0.0)


def second_kernel(z, scale, *refs):
    v, w_cat, pos, wt, proj, halves, table, hid_dec, hid_cat, slope, inner_in, total, received = refs[:13]
    big, send, time, part = refs[13:17]
    shifts, inner_cat, thin = refs[17:]
    core = lax.axis_index("dp")
    decoder = lax.axis_index("sec") == 1
    first = lax.axis_index("sp") == 0
    for j in range(3):
        zero_ends(z, shifts.at[j])

    def put_out(kernel_grad, proj_part):
        part[...] = proj_part
        side = z.wide - LANES
        if z.carries:
            pieces = []
            for b in range(2 * z.chans // LANES):
                block = proj_part[:, (b // 2) * LANES : (b // 2 + 1) * LANES]
                pieces.append(block if b % 2 else pltpu.roll(block, LANES // 2, 1))
            carried = jnp.concatenate(pieces, axis=0)
            lane = lax.broadcasted_iota(jnp.int32, carried.shape, 1)
        for j in range(z.sp):
            rows = kernel_grad[j * z.own : (j + 1) * z.own]
            if z.carries:
                tail = jnp.where(lane < LANES // 2, rows[:, side:], carried)
                rows = jnp.concatenate([rows[:, :side], tail], axis=1) if side else tail
            if z.split:
                big[j] = jnp.where(core == 0, rows[: z.half], rows[z.half :])
                send[j] = jnp.where(core == 0, rows[z.half :], rows[: z.half]).astype(BF16)
            else:
                big[j] = rows

    @pl.when(decoder)
    def _():
        def body(r):
            put_shifts(z, inner_in[r].astype(F32), shifts, r)

        each_row(z, body)
        spread(z, shifts, inner_cat)
        half = halves[:8, :1]

        def latent_rows(raw):
            row = lax.broadcasted_iota(jnp.int32, raw.shape, 0)
            return jnp.where(row < z.lat, raw / half - raw[z.lat : z.lat + 1], 0.0)

        short = latent_rows(frame_sum(z, dot(pos[...], inner_cat[...], TN)))
        proj8 = proj[:8].astype(F32)
        proj24 = jnp.concatenate([proj8] * 3, axis=0).astype(BF16)
        kernel_grad = dot(proj24, stack3(short), TN) * scale
        time[...] = dot(hid_dec[...], v[...], TN)[: 3 * z.own] * scale
        whole = latent_rows(frame_sum(z, dot(pos[...], v[...], TN)))
        partial = sum3(dot(stack3(short), w_cat[...], NT))
        put_out(kernel_grad, (partial + jnp.where(first, whole, 0.0)) * scale)

    @pl.when(jnp.logical_not(decoder))
    def _():
        bounded = jnp.tanh(total[...])
        grad = received[...] * (1.0 - bounded * bounded)
        back = back_weights(z, table)
        gh, gm, gl = thirds(grad)
        bh, bm, bl = thirds(back)
        left = jnp.concatenate([gh, gh, gm, gh, gl, gm], axis=0).astype(BF16)
        right = jnp.concatenate([bh, bm, bh, bl, bh, bm], axis=0).astype(BF16)
        thin[...] = dot(left, right, TN)

        def body(r):
            inner = keep_own(z, later_row(z, thin, r) * slope[r])
            put_shifts(z, inner, shifts, r)

        each_row(z, body)
        spread(z, shifts, inner_cat)
        kernel_grad = dot(v[...], inner_cat[...], TN) * scale
        grad3 = jnp.concatenate([gh, gm, gl], axis=0).astype(BF16)
        short = sum3(dot(grad3, hid_cat[...], NN))
        short3 = stack3(short)
        proj8 = proj[:8].astype(F32)
        proj24 = jnp.concatenate([proj8] * 3, axis=0).astype(BF16)
        time[...] = dot(short3, proj24, TN)[: 3 * z.own] * scale
        whole = sum3(dot(grad3, v[...], NN))
        partial = sum3(dot(short3, wt[...], NN))
        put_out(kernel_grad, (partial + jnp.where(first, whole, 0.0)) * scale)


def meet_kernel(mine, other, both):
    both[...] = (mine[...] + other[...].astype(F32)).astype(BF16)


def last_kernel(z, mine, other, time_mine, time_other, space, time, part):
    time[...] = time_mine[...] + time_other[...]
    core = lax.axis_index("dp")
    per = LANES // z.own
    if z.split:
        low = pl.ds(pl.multiple_of(core * z.half, z.half), z.half)
        high = pl.ds(pl.multiple_of((1 - core) * z.half, z.half), z.half)
        sources = ((low, lambda at: mine[at].astype(F32)), (high, lambda at: other[at].astype(F32)))
    else:
        sources = ((slice(0, z.own), lambda at: mine[at].astype(F32) + other[at].astype(F32)),)
    for rows, source in sources:
        for tap, (block, offset) in enumerate(spots(9, z.own)):
            for m in range(z.chans // LANES):
                total = None
                for p in range(per):
                    at = (m * per + p, slice(None), slice(block * LANES, (block + 1) * LANES))
                    value = lanes_down(source(at), offset - p * z.own)
                    if total is None:
                        total = value
                    else:
                        lane = lax.broadcasted_iota(jnp.int32, value.shape, 1)
                        total = jnp.where(lane < p * z.own, total, value)
                space[tap, rows, m * LANES : (m + 1) * LANES] = total
    if z.carries:
        side = slice(z.wide - LANES, z.wide)
        one, two = (
            sum(source[j, :, side].astype(F32) for j in range(z.sp)) for source in (mine, other)
        )
        if z.split:
            carried = jnp.concatenate(
                [jnp.where(core == 0, one, two), jnp.where(core == 0, two, one)], axis=0
            )
        else:
            carried = one + two
        lane = lax.broadcasted_iota(jnp.int32, (8, LANES), 1)
        for m in range(z.chans // LANES):
            low = pltpu.roll(carried[16 * m : 16 * m + 8], LANES // 2, 1)
            high = carried[16 * m + 8 : 16 * m + 16]
            both = jnp.where(lane < LANES // 2, low, high)
            for l in range(z.lat):
                part[l, :, m * LANES : (m + 1) * LANES] = both[l : l + 1]
    else:
        part[...] = jnp.zeros(part.shape, F32)


VM = pl.BlockSpec(memory_space=pltpu.VMEM)


def shaped(shape, dtype):
    return jax.ShapeDtypeStruct(shape, dtype)


def local(block_data, code_index, levels, w_space, w_time, enc_proj, dec_proj):
    frames, cols, chans = block_data.shape[2], block_data.shape[4], block_data.shape[5]
    lat, own = code_index.shape[1], w_space.shape[2]
    z = Sizes(lax.axis_size("sp"), frames, cols, chans, own, lat)
    scale = float(lax.axis_size("dp") * z.count) ** (-0.5)
    decoder = lax.axis_index("sec") == 1
    room = 20 * 1024 * 1024 + 5 * z.count * chans * 4 // 2 * (1 if z.sp > 8 else 0)
    params = pltpu.CompilerParams(vmem_limit_bytes=min(room, 60 * 1024 * 1024))

    codes = jnp.transpose(code_index[0, :, :, 0].astype(F32), (2, 1, 0))
    codes = jnp.concatenate([codes, jnp.ones((cols, frames, 1), F32)], axis=2)
    codes = jnp.pad(codes, ((0, 0), (0, 0), (0, 7 - lat))).reshape(cols, 8 * frames)
    left = z.code_lane % LANES
    code_rows = z.half if z.code_row == 0 else z.code_rows
    codes = jnp.pad(codes, ((0, code_rows - cols), (left, LANES - left - 8 * frames)))
    ahead, behind, own_piece = pl.pallas_call(
        functools.partial(piece_kernel, z),
        out_shape=(
            shaped((z.sp // 2 - 1, z.piece_rows, z.wide), BF16),
            shaped((z.sp // 2, z.piece_rows, z.wide), BF16),
            shaped((z.piece_rows, z.wide), BF16),
        ),
        in_specs=[VM] * 2,
        out_specs=(VM,) * 3,
        compiler_params=params,
        name="pieces",
    )(w_space[0], codes)
    shards, steps, mine, other, piece_steps = ring_exchange(
        block_data.reshape(z.row, chans), ahead, behind, own_piece
    )
    proj = jnp.pad(jnp.where(decoder, dec_proj, enc_proj), ((0, 16 - lat), (0, 0)))
    wt = jnp.concatenate([w_time.reshape(3 * own, chans), proj[:8]], axis=0)
    wt = jnp.pad(wt, ((0, z.thin - 3 * own - 8), (0, 0)))
    half = jnp.pad((levels.astype(F32) - 1.0) * 0.5, (0, 16 - lat), constant_values=1.0)
    halves = jnp.broadcast_to(half[:, None], (16, LANES))

    w_cat, pos, hid_dec, rate, table = pl.pallas_call(
        functools.partial(early_kernel, z, piece_steps),
        out_shape=(
            shaped((chans, z.wide), BF16),
            shaped((z.count, LANES), BF16),
            shaped((z.count, z.thin), BF16),
            shaped((z.sp, z.row, LANES), F32),
            shaped((LANES, LANES), F32),
        ),
        in_specs=[VM] * (2 * z.sp + 3),
        out_specs=(VM,) * 5,
        scratch_shapes=[
            pltpu.VMEM((z.sp, z.code_rows, z.wide), BF16),
            pltpu.VMEM((z.sp + 2, z.row, z.wide), F32),
        ],
        compiler_params=params,
        name="early",
    )(*mine, *other, wt, proj, halves)
    part, hid_cat, slope, inner, v = pl.pallas_call(
        functools.partial(first_kernel, z, steps),
        out_shape=(
            shaped((8, z.count), F32),
            shaped((z.count, z.thin), BF16),
            shaped((z.sp, z.row, LANES), F32),
            shaped((z.sp, z.row, LANES), BF16),
            shaped((z.count, chans), BF16),
        ),
        in_specs=[VM] * (z.sp + 5),
        out_specs=(VM,) * 5,
        scratch_shapes=[
            pltpu.VMEM((z.sp + 2, z.row, z.wide), F32),
            pltpu.VMEM((z.sp + 2, z.row, LANES), F32),
            pltpu.VMEM((z.count, LANES), F32),
            pltpu.VMEM((z.count, z.thin), F32),
        ],
        compiler_params=params,
        name="first",
    )(*shards, w_cat, wt, proj, table, rate)
    swap = [(0, 1), (1, 0)]
    total = swap_sum(part, "sp")
    received = lax.ppermute(total, "sec", swap)
    part_rows = (z.sp, z.half if z.split else own, z.wide)
    big, send, time, part = pl.pallas_call(
        functools.partial(second_kernel, z, scale),
        out_shape=(
            shaped(part_rows, F32),
            shaped(part_rows, BF16),
            shaped((3 * own, chans), F32),
            shaped((8, chans), F32),
        ),
        in_specs=[VM] * 13,
        out_specs=(VM,) * 4,
        scratch_shapes=[
            pltpu.VMEM((3, z.sp + 2, z.row, LANES), BF16),
            pltpu.VMEM((z.count, z.wide), BF16),
            pltpu.VMEM((z.count, z.thin), F32),
        ],
        compiler_params=params,
        name="second",
    )(v, w_cat, pos, wt, proj, halves, table, hid_dec, hid_cat, slope, inner, total, received)
    if z.split:
        big = pl.pallas_call(
            meet_kernel,
            out_shape=shaped(part_rows, BF16),
            in_specs=[VM] * 2,
            out_specs=VM,
            compiler_params=params,
            name="meet",
        )(big, lax.ppermute(send, "dp", swap))
    big = lax.all_to_all(big.astype(BF16), "sp", 0, 0, tiled=True)
    space, time, carried = pl.pallas_call(
        functools.partial(last_kernel, z),
        out_shape=(
            shaped((9, own, chans), F32),
            shaped((3 * own, chans), F32),
            shaped((lat, 1, chans), F32),
        ),
        in_specs=[VM] * 4,
        out_specs=(VM,) * 3,
        compiler_params=params,
        name="last",
    )(big, lax.ppermute(big, "dp", swap), time, lax.ppermute(time, "dp", swap))
    if z.carries:
        part = carried.reshape(lat, chans)
    else:
        part = swap_sum(part, "sp")
        part = (part + lax.ppermute(part, "dp", swap))[:lat]
    return space[None], time.reshape(1, 3, own, chans), part[None]


def solution(mesh):
    placed = (
        P("sec", "dp", None, "sp", None, None),
        P("dp", None, None, "sp", None),
        P(),
        P("sec", None, "sp", None),
        P("sec", None, "sp", None),
        P(),
        P(),
    )
    return jax.shard_map(
        local,
        mesh=mesh,
        in_specs=placed,
        out_specs=(P("sec", None, "sp", None), P("sec", None, "sp", None), P("sec", None, None)),
        check_vma=False,
    )
```

```python
import functools

import jax
import jax.numpy as jnp
from jax import lax
from jax.experimental import pallas as pl
from jax.experimental.pallas import tpu as pltpu
from jax.sharding import PartitionSpec as P

F32 = jnp.float32
BF16 = jnp.bfloat16
LANES = 128
NN = (((1,), (0,)), ((), ()))
NT = (((1,), (1,)), ((), ()))
TN = (((0,), (0,)), ((), ()))


def up_to(value, multiple):
    return -(-value // multiple) * multiple


def ring_place(index, count):
    return jnp.where(index % 2 == 0, index // 2, count - (index + 1) // 2)


def ring_device(place, count):
    place = lax.rem(place + 2 * count, count)
    return jnp.where(place < count // 2, 2 * place, 2 * (count - place) - 1)


def ring_maps(count):
    order = list(range(0, count, 2)) + list(range(count - 1, 0, -2))
    forward = [(order[i], order[(i + 1) % count]) for i in range(count)]
    return forward, [(target, source) for source, target in forward]


def ring_gather(shard):
    count = lax.axis_size("sp")
    up, down = ring_maps(count)
    shards, steps = [shard], [0]
    first = second = shard
    for step in range(1, count // 2 + 1):
        first = lax.ppermute(first, "sp", up)
        shards.append(first)
        steps.append(-step)
        if step < count - step:
            second = lax.ppermute(second, "sp", down)
            shards.append(second)
            steps.append(step)
    return shards, steps


def exchange_pieces(pairs, shards):
    arrived = [pairs[0]] + [swap(pair, 2 * k) for k, pair in enumerate(pairs) if k]
    arrived = lax.optimization_barrier((arrived, shards[3]))[0]
    even = jnp.stack([pair[0] for pair in arrived])
    odd = swap(jnp.stack([pair[1] for pair in arrived]), 1)
    return even, odd, swap_core(even), swap_core(odd)


def swap(values, distance):
    count = lax.axis_size("sp")
    return lax.ppermute(values, "sp", [(i, i ^ distance) for i in range(count)])


def swap_core(values):
    return lax.ppermute(values, "dp", [(0, 1), (1, 0)])


def sum_pairs(values, bits):
    bits = list(bits)
    while bits:
        if len(bits) == 1:
            values = values + swap(values, bits.pop())
        else:
            one, two = bits.pop(0), bits.pop(0)
            values = values + (swap(values, one) + swap(values, two) + swap(values, one | two))
    return values


def sum_and_cross(values):
    count, sections = lax.axis_size("sp"), lax.axis_size("sec")
    bits = [1 << b for b in range(count.bit_length() - 1)]
    values = sum_pairs(values, bits[1:])
    beside = swap(values, 1)
    across = lax.ppermute(values, "sec", [(0, 1), (1, 0)])
    corner = lax.ppermute(
        values,
        ("sec", "sp"),
        [(s * count + i, (1 - s) * count + (i ^ 1)) for s in range(sections) for i in range(count)],
    )
    return values + beside, across + corner


def dot(left, right, dims):
    return lax.dot_general(left, right, dims, preferred_element_type=F32)


def thirds(values):
    high = values.astype(BF16).astype(F32)
    rest = values - high
    middle = rest.astype(BF16).astype(F32)
    return high, middle, rest - middle


def stack3(values):
    return jnp.concatenate(thirds(values), axis=0).astype(BF16)


def sum3(stacked):
    rows = stacked.shape[0] // 3
    return stacked[:rows] + stacked[rows : 2 * rows] + stacked[2 * rows :]


def lanes_down(values, by):
    by = by % LANES
    return values if by == 0 else pltpu.roll(values, LANES - by, 1)


def spots(parts, own):
    return [((p * own) // LANES, (p * own) % LANES) for p in range(parts)]


def col_move(values, by, cols):
    if by == 0:
        return values
    rows = values.shape[0]
    col = lax.broadcasted_iota(jnp.int32, values.shape, 0) % cols
    edge = 0 if by > 0 else cols - 1
    return jnp.where(col == edge, 0.0, pltpu.roll(values, by % rows, 0))


def frames_move(values, by, cols):
    if by == 0:
        return values
    zeros = jnp.zeros((abs(by) * cols, values.shape[1]), values.dtype)
    if by > 0:
        return jnp.concatenate([zeros, values[: -by * cols]], axis=0)
    return jnp.concatenate([values[-by * cols :], zeros], axis=0)


def merge(pieces, own):
    blocks = [None] * (spots(len(pieces), own)[-1][0] + 1)
    for piece, (block, offset) in zip(pieces, spots(len(pieces), own)):
        moved = lanes_down(piece, -offset)
        blocks[block] = moved if blocks[block] is None else blocks[block] + moved
    return blocks


class Sizes:
    def __init__(self, sp, frames, cols, chans, own, lat):
        self.sp, self.frames, self.cols = sp, frames, cols
        self.chans, self.own, self.lat = chans, own, lat
        self.row = frames * cols
        self.count = sp * self.row
        self.wide = up_to(9 * own, LANES)
        self.thin = up_to(3 * own + 8, LANES)
        self.copies = min(3, LANES // own)
        self.half = own // 2
        self.half_pad = up_to(self.half, 16)
        self.code_rows = up_to(cols, 16)
        if self.wide - 9 * own >= 8 * frames and self.half >= cols:
            self.code_row, self.code_lane = 0, 9 * own
            self.piece_rows = self.half
        else:
            self.code_row, self.code_lane = self.half_pad, 0
            self.piece_rows = self.code_row + self.code_rows
        self.split = self.half == self.half_pad
        self.carries = self.wide - 9 * own >= LANES // 2 and own * (LANES // 2) >= 8 * chans


def place_shards(z, steps, shards, v):
    place = ring_place(lax.axis_index("sp"), z.sp)
    for shard, step in zip(shards, steps):
        v[rows_at(ring_device(place + step, z.sp), z)] = shard[...]


def place_pieces(z, even, odd, even_other, odd_other, w_cat, codes):
    me, core = lax.axis_index("sp"), lax.axis_index("dp")
    for distance in range(z.sp):
        mine, other = ((even, even_other), (odd, odd_other))[distance % 2]
        device = lax.bitwise_xor(me, distance)
        start = pl.multiple_of(device * z.own, z.own)
        at = distance // 2
        codes[device] = mine[at, z.code_row : z.code_row + z.code_rows]
        one, two = mine[at, : z.half], other[at, : z.half]
        low, high = jnp.where(core == 0, one, two), jnp.where(core == 0, two, one)
        if z.split:
            w_cat[pl.ds(start, z.half)] = low
            w_cat[pl.ds(start + z.half, z.half)] = high
        else:
            both = jnp.concatenate([low.astype(F32), high.astype(F32)], axis=0)
            w_cat[pl.ds(start, z.own)] = both.astype(BF16)


def each_row(z, body):
    if z.sp <= 8:
        for r in range(z.sp):
            body(r)
    else:

        def step(r, carry):
            body(r)
            return carry

        lax.fori_loop(0, z.sp, step, 0)


def rows_at(r, z):
    if isinstance(r, int):
        return pl.ds(r * z.row, z.row)
    return pl.ds(pl.multiple_of(r * z.row, z.row), z.row)


def rows_from(r0, rows, z):
    if isinstance(r0, int):
        return pl.ds(r0 * z.row, rows * z.row)
    return pl.ds(pl.multiple_of(r0 * z.row, rows * z.row), rows * z.row)


def conv_row(z, taps, r):
    total = None
    for j in range(3):
        by_offset = {}
        for i in range(3):
            block, offset = spots(9, z.own)[3 * i + j]
            value = taps[r + i, :, block * LANES : (block + 1) * LANES]
            by_offset[offset] = by_offset.get(offset, 0.0) + value
        column = sum(lanes_down(value, offset) for offset, value in by_offset.items())
        column = col_move(column, 1 - j, z.cols)
        total = column if total is None else total + column
    return total


def later_row(z, taps, r):
    total = None
    for k, (block, offset) in enumerate(spots(3, z.own)):
        value = taps[rows_at(r, z), block * LANES : (block + 1) * LANES]
        value = frames_move(lanes_down(value, offset), -k, z.cols)
        total = value if total is None else total + value
    return total


def keep_own(z, values):
    lane = lax.broadcasted_iota(jnp.int32, values.shape, 1)
    return jnp.where(lane < z.own, values, 0.0)


def put_shifts(z, inner, shifts, r):
    for j in range(3):
        shifts[j, r + 1] = col_move(inner, j - 1, z.cols).astype(BF16)


def spread(z, shifts, inner_cat):
    def body(r):
        pieces = [
            shifts[j, r + 2 - i].astype(F32) for i in range(3) for j in range(3)
        ]
        for b, block in enumerate(merge(pieces, z.own)):
            inner_cat[rows_at(r, z), b * LANES : (b + 1) * LANES] = block.astype(BF16)

    each_row(z, body)


def zero_ends(z, padded):
    padded[0] = jnp.zeros(padded.shape[1:], padded.dtype)
    padded[z.sp + 1] = jnp.zeros(padded.shape[1:], padded.dtype)


def in_blocks(z, action):
    step = 8 if z.sp % 8 == 0 else 1
    if z.sp == step:
        action(0, step)
    else:

        def body(b, carry):
            action(b * step, step)
            return carry

        lax.fori_loop(0, z.sp // step, body, 0)


def position_codes(z, codes, out):
    block, offset = z.code_lane // LANES, z.code_lane % LANES
    run = 8 * z.frames

    def body(r):
        raw = codes[r, : z.cols, block * LANES : (block + 1) * LANES].astype(F32)
        lane = lax.broadcasted_iota(jnp.int32, raw.shape, 1)
        raw = jnp.where(lane < run, lanes_down(raw, offset), 0.0)
        raw = raw + pltpu.roll(raw, run, 1) + pltpu.roll(raw, 2 * run, 1)
        frame = (lane % run) // 8
        blocks = [jnp.where(frame == t, raw, 0.0) for t in range(z.frames)]
        out[rows_at(r, z)] = jnp.concatenate(blocks, axis=0).astype(BF16)

    each_row(z, body)


def frame_sum(z, raw):
    return sum(raw[8 * t : 8 * t + 8] for t in range(z.frames))


def piece_kernel(z, w, codes, *pairs):
    me = lax.axis_index("sp")
    core = lax.axis_index("dp")
    lane = lax.broadcasted_iota(jnp.int32, (z.half, LANES), 1)
    code_block = codes[...]
    for distance in range(z.sp):
        begin = lax.bitwise_xor(me, distance) * z.own
        block, offset = begin // LANES, begin % LANES
        at = pl.ds(pl.multiple_of(block * LANES, LANES), LANES)
        taps = []
        for tap in range(9):
            if z.split:
                value = w[tap, pl.ds(pl.multiple_of(core * z.half, z.half), z.half), at]
                value = value.astype(F32)
            else:
                value = w[tap, :, at].astype(F32)
                value = jnp.where(core == 0, value[: z.half], value[z.half :])
            value = pltpu.roll(value, (LANES - offset) % LANES, 1)
            taps.append(jnp.where(lane < z.own, value, 0.0))
        blocks = merge(taps, z.own)
        if z.code_row == 0:
            blocks[-1] = blocks[-1] + code_block
        target = pairs[distance // 2]
        for b, value in enumerate(blocks):
            lanes = slice(b * LANES, (b + 1) * LANES)
            target[distance % 2, : z.half, lanes] = value.astype(BF16)
        if z.code_row:
            target[distance % 2, z.code_row : z.piece_rows, :LANES] = code_block.astype(BF16)


def store_hidden(z, pre, logistic, hid_cat, r):
    hidden = keep_own(z, (pre * logistic).astype(BF16).astype(F32))
    moved = [frames_move(hidden, k, z.cols) for k in range(3)]
    for b, block in enumerate(merge(moved, z.own)):
        hid_cat[rows_at(r, z), b * LANES : (b + 1) * LANES] = block.astype(BF16)


def activate(z, taps, hid_cat, slope):
    def body(r):
        pre = conv_row(z, taps, r)
        logistic = 1.0 / (1.0 + jnp.exp(-pre))
        store_hidden(z, pre, logistic, hid_cat, r)
        slope[r] = logistic * (1.0 + pre * (1.0 - logistic))

    each_row(z, body)


def early_kernel(z, *refs):
    wt, proj, halves = refs[4:7]
    w_cat, pos, hid_cat, slope, table_out = refs[7:12]
    codes, taps = refs[12:]
    decoder = lax.axis_index("sec") == 1
    place_pieces(z, *refs[:4], w_cat, codes)

    @pl.when(decoder)
    def _():
        zero_ends(z, taps)
        p_cat = dot(proj[...], w_cat[...], NN)[:8]
        half = halves[:8, :1]
        row = lax.broadcasted_iota(jnp.int32, p_cat.shape, 0)
        scaled = jnp.where(row == z.lat, -jnp.sum(p_cat, axis=0, keepdims=True), p_cat / half)
        table = [term for term in thirds(scaled) for _ in range(z.frames)]
        spare = jnp.zeros((LANES - 24 * z.frames, z.wide), F32)
        table = jnp.concatenate(table + [spare], axis=0).astype(BF16)
        position_codes(z, codes, pos)

        def block(r0, rows):
            place = rows_from(r0, rows, z)
            taps[pl.ds(r0 + 1, rows)] = dot(pos[place], table, NN).reshape(rows, z.row, z.wide)

        in_blocks(z, block)
        activate(z, taps, hid_cat, slope)
        by_tap = [
            keep_own(z, lanes_down(p_cat[:, block * LANES : (block + 1) * LANES], offset))
            for block, offset in spots(9, z.own)
        ]
        by_tap = jnp.concatenate(by_tap + [jnp.zeros((LANES - 72, LANES), F32)], axis=0)
        table_out[...] = sum(
            lanes_down(term, -c * z.own) for c, term in enumerate(thirds(by_tap)[: z.copies])
        )

    @pl.when(jnp.logical_not(decoder))
    def _():
        weights = dot(proj[...], wt[...], NT)[:8]
        table_out[:8] = weights[:, :LANES]
        table_out[8:16] = weights[:, LANES:] if z.thin > LANES else weights


def back_weights(z, table):
    if z.thin > LANES:
        return jnp.concatenate([table[:8], table[8:16]], axis=1)
    return table[:8]


def first_kernel(z, steps, *refs):
    n = z.sp
    shards, (w_cat, wt, proj, table, rate) = refs[:n], refs[n : n + 5]
    part, hid_cat, slope, inner_out, v = refs[n + 5 : n + 10]
    taps, back, spots_of, thin = refs[n + 10 :]
    decoder = lax.axis_index("sec") == 1
    first = lax.axis_index("sp") == 0
    place_shards(z, steps, shards, v)

    @pl.when(decoder)
    def _():
        zero_ends(z, back)
        by_tap = table[...].astype(BF16)

        def block(r0, rows):
            place = rows_from(r0, rows, z)
            thin[place] = dot(v[place], wt[...], NT)

        in_blocks(z, block)

        def body(r):
            inner = keep_own(z, (later_row(z, thin, r) * rate[r]).astype(BF16).astype(F32))
            inner_out[r] = inner.astype(BF16)
            many = sum(lanes_down(inner, -c * z.own) for c in range(z.copies))
            back[r + 1] = dot(many.astype(BF16), by_tap, NT)

        each_row(z, body)
        block_of, offset = (3 * z.own) // LANES, (3 * z.own) % LANES

        def collect(r):
            lane = lax.broadcasted_iota(jnp.int32, (z.row, LANES), 1)
            value = jnp.where(lane < 24, back[r + 2], jnp.where(lane < 48, back[r + 1], back[r]))
            j = (lane // 8) % 3
            moved = jnp.where(
                j == 0,
                col_move(value, -1, z.cols),
                jnp.where(j == 1, value, col_move(value, 1, z.cols)),
            )
            whole = thin[rows_at(r, z), block_of * LANES : (block_of + 1) * LANES]
            whole = jnp.where(first, lanes_down(whole, offset - 72), 0.0)
            spots_of[rows_at(r, z)] = jnp.where(lane < 72, moved, whole)

        each_row(z, collect)
        turned = spots_of[...].T
        part[...] = sum(turned[8 * g : 8 * g + 8] for g in range(10))

    @pl.when(jnp.logical_not(decoder))
    def _():
        zero_ends(z, taps)

        def block(r0, rows):
            place = rows_from(r0, rows, z)
            taps[pl.ds(r0 + 1, rows)] = dot(v[place], w_cat[...], NN).reshape(
                rows, z.row, z.wide
            )

        in_blocks(z, block)
        activate(z, taps, hid_cat, slope)
        weights = back_weights(z, table)
        whole = dot(proj[...], v[...], NT)[:8]
        part[...] = sum3(dot(stack3(weights), hid_cat[...], NT)) + jnp.where(first, whole, 0.0)


def second_kernel(z, scale, *refs):
    v, w_cat, pos, wt, proj, halves, table, hid_dec, hid_cat, slope, inner_in, total, received = refs[:13]
    big, send, time, part = refs[13:17]
    shifts, inner_cat, thin = refs[17:]
    core = lax.axis_index("dp")
    decoder = lax.axis_index("sec") == 1
    first = lax.axis_index("sp") == 0
    for j in range(3):
        zero_ends(z, shifts.at[j])

    def put_out(kernel_grad, proj_part):
        part[...] = proj_part
        side = z.wide - LANES
        if z.carries:
            pieces = []
            for b in range(2 * z.chans // LANES):
                block = proj_part[:, (b // 2) * LANES : (b // 2 + 1) * LANES]
                pieces.append(block if b % 2 else pltpu.roll(block, LANES // 2, 1))
            carried = jnp.concatenate(pieces, axis=0)
            lane = lax.broadcasted_iota(jnp.int32, carried.shape, 1)
        for j in range(z.sp):
            rows = kernel_grad[j * z.own : (j + 1) * z.own]
            if z.carries:
                tail = jnp.where(lane < LANES // 2, rows[:, side:], carried)
                rows = jnp.concatenate([rows[:, :side], tail], axis=1) if side else tail
            if z.split:
                big[j] = jnp.where(core == 0, rows[: z.half], rows[z.half :])
                send[j] = jnp.where(core == 0, rows[z.half :], rows[: z.half]).astype(BF16)
            else:
                big[j] = rows

    @pl.when(decoder)
    def _():
        def body(r):
            put_shifts(z, inner_in[r].astype(F32), shifts, r)

        each_row(z, body)
        spread(z, shifts, inner_cat)
        half = halves[:8, :1]

        def latent_rows(raw):
            row = lax.broadcasted_iota(jnp.int32, raw.shape, 0)
            return jnp.where(row < z.lat, raw / half - raw[z.lat : z.lat + 1], 0.0)

        short = latent_rows(frame_sum(z, dot(pos[...], inner_cat[...], TN)))
        proj8 = proj[:8].astype(F32)
        proj24 = jnp.concatenate([proj8] * 3, axis=0).astype(BF16)
        kernel_grad = dot(proj24, stack3(short), TN) * scale
        time[...] = dot(hid_dec[...], v[...], TN)[: 3 * z.own] * scale
        whole = latent_rows(frame_sum(z, dot(pos[...], v[...], TN)))
        partial = sum3(dot(stack3(short), w_cat[...], NT))
        put_out(kernel_grad, (partial + jnp.where(first, whole, 0.0)) * scale)

    @pl.when(jnp.logical_not(decoder))
    def _():
        bounded = jnp.tanh(total[...])
        grad = received[...] * (1.0 - bounded * bounded)
        back = back_weights(z, table)
        gh, gm, gl = thirds(grad)
        bh, bm, bl = thirds(back)
        left = jnp.concatenate([gh, gh, gm, gh, gl, gm], axis=0).astype(BF16)
        right = jnp.concatenate([bh, bm, bh, bl, bh, bm], axis=0).astype(BF16)
        thin[...] = dot(left, right, TN)

        def body(r):
            inner = keep_own(z, later_row(z, thin, r) * slope[r])
            put_shifts(z, inner, shifts, r)

        each_row(z, body)
        spread(z, shifts, inner_cat)
        kernel_grad = dot(v[...], inner_cat[...], TN) * scale
        grad3 = jnp.concatenate([gh, gm, gl], axis=0).astype(BF16)
        short = sum3(dot(grad3, hid_cat[...], NN))
        short3 = stack3(short)
        proj8 = proj[:8].astype(F32)
        proj24 = jnp.concatenate([proj8] * 3, axis=0).astype(BF16)
        time[...] = dot(short3, proj24, TN)[: 3 * z.own] * scale
        whole = sum3(dot(grad3, v[...], NN))
        partial = sum3(dot(short3, wt[...], NN))
        put_out(kernel_grad, (partial + jnp.where(first, whole, 0.0)) * scale)


def meet_kernel(mine, other, both):
    both[...] = (mine[...] + other[...].astype(F32)).astype(BF16)


def last_kernel(z, mine, other, time_mine, time_other, space, time, part):
    time[...] = time_mine[...] + time_other[...]
    core = lax.axis_index("dp")
    per = LANES // z.own
    if z.split:
        low = pl.ds(pl.multiple_of(core * z.half, z.half), z.half)
        high = pl.ds(pl.multiple_of((1 - core) * z.half, z.half), z.half)
        sources = ((low, lambda at: mine[at].astype(F32)), (high, lambda at: other[at].astype(F32)))
    else:
        sources = ((slice(0, z.own), lambda at: mine[at].astype(F32) + other[at].astype(F32)),)
    for rows, source in sources:
        for tap, (block, offset) in enumerate(spots(9, z.own)):
            for m in range(z.chans // LANES):
                total = None
                for p in range(per):
                    at = (m * per + p, slice(None), slice(block * LANES, (block + 1) * LANES))
                    value = lanes_down(source(at), offset - p * z.own)
                    if total is None:
                        total = value
                    else:
                        lane = lax.broadcasted_iota(jnp.int32, value.shape, 1)
                        total = jnp.where(lane < p * z.own, total, value)
                space[tap, rows, m * LANES : (m + 1) * LANES] = total
    if z.carries:
        side = slice(z.wide - LANES, z.wide)
        one, two = (
            sum(source[j, :, side].astype(F32) for j in range(z.sp)) for source in (mine, other)
        )
        if z.split:
            carried = jnp.concatenate(
                [jnp.where(core == 0, one, two), jnp.where(core == 0, two, one)], axis=0
            )
        else:
            carried = one + two
        lane = lax.broadcasted_iota(jnp.int32, (8, LANES), 1)
        for m in range(z.chans // LANES):
            low = pltpu.roll(carried[16 * m : 16 * m + 8], LANES // 2, 1)
            high = carried[16 * m + 8 : 16 * m + 16]
            both = jnp.where(lane < LANES // 2, low, high)
            for l in range(z.lat):
                part[l, :, m * LANES : (m + 1) * LANES] = both[l : l + 1]
    else:
        part[...] = jnp.zeros(part.shape, F32)


VM = pl.BlockSpec(memory_space=pltpu.VMEM)


def shaped(shape, dtype):
    return jax.ShapeDtypeStruct(shape, dtype)


def local(block_data, code_index, levels, w_space, w_time, enc_proj, dec_proj):
    frames, cols, chans = block_data.shape[2], block_data.shape[4], block_data.shape[5]
    lat, own = code_index.shape[1], w_space.shape[2]
    z = Sizes(lax.axis_size("sp"), frames, cols, chans, own, lat)
    scale = float(lax.axis_size("dp") * z.count) ** (-0.5)
    decoder = lax.axis_index("sec") == 1
    room = 20 * 1024 * 1024 + 5 * z.count * chans * 4 // 2 * (1 if z.sp > 8 else 0)
    params = pltpu.CompilerParams(vmem_limit_bytes=min(room, 60 * 1024 * 1024))

    codes = jnp.transpose(code_index[0, :, :, 0].astype(F32), (2, 1, 0))
    codes = jnp.concatenate([codes, jnp.ones((cols, frames, 1), F32)], axis=2)
    codes = jnp.pad(codes, ((0, 0), (0, 0), (0, 7 - lat))).reshape(cols, 8 * frames)
    left = z.code_lane % LANES
    code_rows = z.half if z.code_row == 0 else z.code_rows
    codes = jnp.pad(codes, ((0, code_rows - cols), (left, LANES - left - 8 * frames)))
    pairs = pl.pallas_call(
        functools.partial(piece_kernel, z),
        out_shape=[shaped((2, z.piece_rows, z.wide), BF16)] * (z.sp // 2),
        in_specs=[VM] * 2,
        out_specs=[VM] * (z.sp // 2),
        compiler_params=params,
        name="pieces",
    )(w_space[0], codes)
    shards, steps = ring_gather(block_data.reshape(z.row, chans))
    pieces = exchange_pieces(pairs, shards)
    proj = jnp.pad(jnp.where(decoder, dec_proj, enc_proj), ((0, 16 - lat), (0, 0)))
    wt = jnp.concatenate([w_time.reshape(3 * own, chans), proj[:8]], axis=0)
    wt = jnp.pad(wt, ((0, z.thin - 3 * own - 8), (0, 0)))
    half = jnp.pad((levels.astype(F32) - 1.0) * 0.5, (0, 16 - lat), constant_values=1.0)
    halves = jnp.broadcast_to(half[:, None], (16, LANES))

    w_cat, pos, hid_dec, rate, table = pl.pallas_call(
        functools.partial(early_kernel, z),
        out_shape=(
            shaped((chans, z.wide), BF16),
            shaped((z.count, LANES), BF16),
            shaped((z.count, z.thin), BF16),
            shaped((z.sp, z.row, LANES), F32),
            shaped((LANES, LANES), F32),
        ),
        in_specs=[VM] * 7,
        out_specs=(VM,) * 5,
        scratch_shapes=[
            pltpu.VMEM((z.sp, z.code_rows, z.wide), BF16),
            pltpu.VMEM((z.sp + 2, z.row, z.wide), F32),
        ],
        compiler_params=params,
        name="early",
    )(*pieces, wt, proj, halves)
    part, hid_cat, slope, inner, v = pl.pallas_call(
        functools.partial(first_kernel, z, steps),
        out_shape=(
            shaped((8, z.count), F32),
            shaped((z.count, z.thin), BF16),
            shaped((z.sp, z.row, LANES), F32),
            shaped((z.sp, z.row, LANES), BF16),
            shaped((z.count, chans), BF16),
        ),
        in_specs=[VM] * (z.sp + 5),
        out_specs=(VM,) * 5,
        scratch_shapes=[
            pltpu.VMEM((z.sp + 2, z.row, z.wide), F32),
            pltpu.VMEM((z.sp + 2, z.row, LANES), F32),
            pltpu.VMEM((z.count, LANES), F32),
            pltpu.VMEM((z.count, z.thin), F32),
        ],
        compiler_params=params,
        name="first",
    )(*shards, w_cat, wt, proj, table, rate)
    total, received = sum_and_cross(part)
    part_rows = (z.sp, z.half if z.split else own, z.wide)
    big, send, time, part = pl.pallas_call(
        functools.partial(second_kernel, z, scale),
        out_shape=(
            shaped(part_rows, F32),
            shaped(part_rows, BF16),
            shaped((3 * own, chans), F32),
            shaped((8, chans), F32),
        ),
        in_specs=[VM] * 13,
        out_specs=(VM,) * 4,
        scratch_shapes=[
            pltpu.VMEM((3, z.sp + 2, z.row, LANES), BF16),
            pltpu.VMEM((z.count, z.wide), BF16),
            pltpu.VMEM((z.count, z.thin), F32),
        ],
        compiler_params=params,
        name="second",
    )(v, w_cat, pos, wt, proj, halves, table, hid_dec, hid_cat, slope, inner, total, received)
    if z.split:
        big = pl.pallas_call(
            meet_kernel,
            out_shape=shaped(part_rows, BF16),
            in_specs=[VM] * 2,
            out_specs=VM,
            compiler_params=params,
            name="meet",
        )(big, swap_core(send))
    big = lax.all_to_all(big.astype(BF16), "sp", 0, 0, tiled=True)
    space, time, carried = pl.pallas_call(
        functools.partial(last_kernel, z),
        out_shape=(
            shaped((9, own, chans), F32),
            shaped((3 * own, chans), F32),
            shaped((lat, 1, chans), F32),
        ),
        in_specs=[VM] * 4,
        out_specs=(VM,) * 3,
        compiler_params=params,
        name="last",
    )(big, swap_core(big), time, swap_core(time))
    if z.carries:
        part = carried.reshape(lat, chans)
    else:
        part = sum_pairs(part, [1 << b for b in range(z.sp.bit_length() - 1)])
        part = (part + swap_core(part))[:lat]
    return space[None], time.reshape(1, 3, own, chans), part[None]


def solution(mesh):
    placed = (
        P("sec", "dp", None, "sp", None, None),
        P("dp", None, None, "sp", None),
        P(),
        P("sec", None, "sp", None),
        P("sec", None, "sp", None),
        P(),
        P(),
    )
    return jax.shard_map(
        local,
        mesh=mesh,
        in_specs=placed,
        out_specs=(P("sec", None, "sp", None), P("sec", None, "sp", None), P("sec", None, None)),
        check_vma=False,
    )
```

```python
import functools

import jax
import jax.numpy as jnp
from jax import lax
from jax.experimental import pallas as pl
from jax.experimental.pallas import tpu as pltpu
from jax.sharding import PartitionSpec as P

F32 = jnp.float32
BF16 = jnp.bfloat16
LANES = 128
NN = (((1,), (0,)), ((), ()))
NT = (((1,), (1,)), ((), ()))
TN = (((0,), (0,)), ((), ()))


def up_to(value, multiple):
    return -(-value // multiple) * multiple


def ring_place(index, count):
    return jnp.where(index % 2 == 0, index // 2, count - (index + 1) // 2)


def ring_device(place, count):
    place = lax.rem(place + 2 * count, count)
    return jnp.where(place < count // 2, 2 * place, 2 * (count - place) - 1)


def ring_maps(count):
    order = list(range(0, count, 2)) + list(range(count - 1, 0, -2))
    forward = [(order[i], order[(i + 1) % count]) for i in range(count)]
    return forward, [(target, source) for source, target in forward]


def ring_gather(shard):
    count = lax.axis_size("sp")
    up, down = ring_maps(count)
    shards, steps = [shard], [0]
    first = second = shard
    for step in range(1, count // 2 + 1):
        first = lax.ppermute(first, "sp", up)
        shards.append(first)
        steps.append(-step)
        if step < count - step:
            second = lax.ppermute(second, "sp", down)
            shards.append(second)
            steps.append(step)
    return shards, steps


def exchange_pieces(pairs, shards):
    arrived = [pairs[0]] + [swap(pair, 2 * k) for k, pair in enumerate(pairs) if k]
    arrived = lax.optimization_barrier((arrived, shards[3]))[0]
    even = jnp.stack([pair[0] for pair in arrived])
    odd = swap(jnp.stack([pair[1] for pair in arrived]), 1)
    return even, odd, swap_core(even), swap_core(odd)


def swap(values, distance):
    count = lax.axis_size("sp")
    return lax.ppermute(values, "sp", [(i, i ^ distance) for i in range(count)])


def swap_core(values):
    return lax.ppermute(values, "dp", [(0, 1), (1, 0)])


def sum_pairs(values, bits):
    bits = list(bits)
    while bits:
        if len(bits) == 1:
            values = values + swap(values, bits.pop())
        else:
            one, two = bits.pop(0), bits.pop(0)
            values = values + (swap(values, one) + swap(values, two) + swap(values, one | two))
    return values


def sum_and_cross(values):
    count, sections = lax.axis_size("sp"), lax.axis_size("sec")
    bits = [1 << b for b in range(count.bit_length() - 1)]
    values = sum_pairs(values, bits[1:])
    beside = swap(values, 1)
    across = lax.ppermute(values, "sec", [(0, 1), (1, 0)])
    corner = lax.ppermute(
        values,
        ("sec", "sp"),
        [(s * count + i, (1 - s) * count + (i ^ 1)) for s in range(sections) for i in range(count)],
    )
    return values + beside, across + corner


def dot(left, right, dims):
    return lax.dot_general(left, right, dims, preferred_element_type=F32)


def thirds(values):
    high = values.astype(BF16).astype(F32)
    rest = values - high
    middle = rest.astype(BF16).astype(F32)
    return high, middle, rest - middle


def stack3(values):
    return jnp.concatenate(thirds(values), axis=0).astype(BF16)


def sum3(stacked):
    rows = stacked.shape[0] // 3
    return stacked[:rows] + stacked[rows : 2 * rows] + stacked[2 * rows :]


def lanes_down(values, by):
    by = by % LANES
    return values if by == 0 else pltpu.roll(values, LANES - by, 1)


def spots(parts, own):
    return [((p * own) // LANES, (p * own) % LANES) for p in range(parts)]


def col_move(values, by, cols):
    if by == 0:
        return values
    rows = values.shape[0]
    col = lax.broadcasted_iota(jnp.int32, values.shape, 0) % cols
    edge = 0 if by > 0 else cols - 1
    return jnp.where(col == edge, 0.0, pltpu.roll(values, by % rows, 0))


def frames_move(values, by, cols):
    if by == 0:
        return values
    zeros = jnp.zeros((abs(by) * cols, values.shape[1]), values.dtype)
    if by > 0:
        return jnp.concatenate([zeros, values[: -by * cols]], axis=0)
    return jnp.concatenate([values[-by * cols :], zeros], axis=0)


def merge(pieces, own):
    blocks = [None] * (spots(len(pieces), own)[-1][0] + 1)
    for piece, (block, offset) in zip(pieces, spots(len(pieces), own)):
        moved = lanes_down(piece, -offset)
        blocks[block] = moved if blocks[block] is None else blocks[block] + moved
    return blocks


class Sizes:
    def __init__(self, sp, frames, cols, chans, own, lat):
        self.sp, self.frames, self.cols = sp, frames, cols
        self.chans, self.own, self.lat = chans, own, lat
        self.row = frames * cols
        self.count = sp * self.row
        self.wide = up_to(9 * own, LANES)
        self.thin = up_to(3 * own + 8, LANES)
        self.copies = min(3, LANES // own)
        self.half = own // 2
        self.half_pad = up_to(self.half, 16)
        self.code_rows = up_to(cols, 16)
        if self.wide - 9 * own >= 8 * frames and self.half >= cols:
            self.code_row, self.code_lane = 0, 9 * own
            self.piece_rows = self.half
        else:
            self.code_row, self.code_lane = self.half_pad, 0
            self.piece_rows = self.code_row + self.code_rows
        self.split = self.half == self.half_pad
        self.carries = self.wide - 9 * own >= LANES // 2 and own * (LANES // 2) >= 8 * chans


def place_shards(z, steps, shards, v):
    place = ring_place(lax.axis_index("sp"), z.sp)
    for shard, step in zip(shards, steps):
        v[rows_at(ring_device(place + step, z.sp), z)] = shard[...]


def place_pieces(z, even, odd, even_other, odd_other, w_cat, codes):
    me, core = lax.axis_index("sp"), lax.axis_index("dp")
    for distance in range(z.sp):
        mine, other = ((even, even_other), (odd, odd_other))[distance % 2]
        device = lax.bitwise_xor(me, distance)
        start = pl.multiple_of(device * z.own, z.own)
        at = distance // 2
        codes[device] = mine[at, z.code_row : z.code_row + z.code_rows]
        one, two = mine[at, : z.half], other[at, : z.half]
        low, high = jnp.where(core == 0, one, two), jnp.where(core == 0, two, one)
        if z.split:
            w_cat[pl.ds(start, z.half)] = low
            w_cat[pl.ds(start + z.half, z.half)] = high
        else:
            both = jnp.concatenate([low.astype(F32), high.astype(F32)], axis=0)
            w_cat[pl.ds(start, z.own)] = both.astype(BF16)


def each_row(z, body):
    if z.sp <= 8:
        for r in range(z.sp):
            body(r)
    else:

        def step(r, carry):
            body(r)
            return carry

        lax.fori_loop(0, z.sp, step, 0)


def rows_at(r, z):
    if isinstance(r, int):
        return pl.ds(r * z.row, z.row)
    return pl.ds(pl.multiple_of(r * z.row, z.row), z.row)


def rows_from(r0, rows, z):
    if isinstance(r0, int):
        return pl.ds(r0 * z.row, rows * z.row)
    return pl.ds(pl.multiple_of(r0 * z.row, rows * z.row), rows * z.row)


def conv_row(z, taps, r):
    total = None
    for j in range(3):
        by_offset = {}
        for i in range(3):
            block, offset = spots(9, z.own)[3 * i + j]
            value = taps[r + i, :, block * LANES : (block + 1) * LANES]
            by_offset[offset] = by_offset.get(offset, 0.0) + value
        column = sum(lanes_down(value, offset) for offset, value in by_offset.items())
        column = col_move(column, 1 - j, z.cols)
        total = column if total is None else total + column
    return total


def later_row(z, taps, r):
    total = None
    for k, (block, offset) in enumerate(spots(3, z.own)):
        value = taps[rows_at(r, z), block * LANES : (block + 1) * LANES]
        value = frames_move(lanes_down(value, offset), -k, z.cols)
        total = value if total is None else total + value
    return total


def keep_own(z, values):
    lane = lax.broadcasted_iota(jnp.int32, values.shape, 1)
    return jnp.where(lane < z.own, values, 0.0)


def put_shifts(z, inner, shifts, r):
    for j in range(3):
        shifts[j, r + 1] = col_move(inner, j - 1, z.cols).astype(BF16)


def spread(z, shifts, inner_cat):
    def body(r):
        pieces = [
            shifts[j, r + 2 - i].astype(F32) for i in range(3) for j in range(3)
        ]
        for b, block in enumerate(merge(pieces, z.own)):
            inner_cat[rows_at(r, z), b * LANES : (b + 1) * LANES] = block.astype(BF16)

    each_row(z, body)


def zero_ends(z, padded):
    padded[0] = jnp.zeros(padded.shape[1:], padded.dtype)
    padded[z.sp + 1] = jnp.zeros(padded.shape[1:], padded.dtype)


def in_blocks(z, action):
    step = 8 if z.sp % 8 == 0 else 1
    if z.sp == step:
        action(0, step)
    else:

        def body(b, carry):
            action(b * step, step)
            return carry

        lax.fori_loop(0, z.sp // step, body, 0)


def position_codes(z, codes, out):
    block, offset = z.code_lane // LANES, z.code_lane % LANES
    run = 8 * z.frames

    def body(r):
        raw = codes[r, : z.cols, block * LANES : (block + 1) * LANES].astype(F32)
        lane = lax.broadcasted_iota(jnp.int32, raw.shape, 1)
        raw = jnp.where(lane < run, lanes_down(raw, offset), 0.0)
        raw = raw + pltpu.roll(raw, run, 1) + pltpu.roll(raw, 2 * run, 1)
        frame = (lane % run) // 8
        blocks = [jnp.where(frame == t, raw, 0.0) for t in range(z.frames)]
        out[rows_at(r, z)] = jnp.concatenate(blocks, axis=0).astype(BF16)

    each_row(z, body)


def frame_sum(z, raw):
    return sum(raw[8 * t : 8 * t + 8] for t in range(z.frames))


def piece_kernel(z, w, codes, *pairs):
    me = lax.axis_index("sp")
    core = lax.axis_index("dp")
    lane = lax.broadcasted_iota(jnp.int32, (z.half, LANES), 1)
    code_block = codes[...]
    for distance in range(z.sp):
        begin = lax.bitwise_xor(me, distance) * z.own
        block, offset = begin // LANES, begin % LANES
        at = pl.ds(pl.multiple_of(block * LANES, LANES), LANES)
        taps = []
        for tap in range(9):
            if z.split:
                value = w[tap, pl.ds(pl.multiple_of(core * z.half, z.half), z.half), at]
                value = value.astype(F32)
            else:
                value = w[tap, :, at].astype(F32)
                value = jnp.where(core == 0, value[: z.half], value[z.half :])
            value = pltpu.roll(value, (LANES - offset) % LANES, 1)
            taps.append(jnp.where(lane < z.own, value, 0.0))
        blocks = merge(taps, z.own)
        if z.code_row == 0:
            blocks[-1] = blocks[-1] + code_block
        target = pairs[distance // 2]
        for b, value in enumerate(blocks):
            lanes = slice(b * LANES, (b + 1) * LANES)
            target[distance % 2, : z.half, lanes] = value.astype(BF16)
        if z.code_row:
            target[distance % 2, z.code_row : z.piece_rows, :LANES] = code_block.astype(BF16)


def store_hidden(z, pre, logistic, hid_cat, r):
    hidden = keep_own(z, (pre * logistic).astype(BF16).astype(F32))
    moved = [frames_move(hidden, k, z.cols) for k in range(3)]
    for b, block in enumerate(merge(moved, z.own)):
        hid_cat[rows_at(r, z), b * LANES : (b + 1) * LANES] = block.astype(BF16)


def activate(z, taps, hid_cat, slope):
    def body(r):
        pre = conv_row(z, taps, r)
        logistic = 1.0 / (1.0 + jnp.exp(-pre))
        store_hidden(z, pre, logistic, hid_cat, r)
        slope[r] = logistic * (1.0 + pre * (1.0 - logistic))

    each_row(z, body)


def early_kernel(z, *refs):
    wt, proj, halves = refs[4:7]
    w_cat, pos, hid_cat, slope, table_out = refs[7:12]
    codes, taps = refs[12:]
    decoder = lax.axis_index("sec") == 1
    place_pieces(z, *refs[:4], w_cat, codes)

    @pl.when(decoder)
    def _():
        zero_ends(z, taps)
        p_cat = dot(proj[...], w_cat[...], NN)[:8]
        half = halves[:8, :1]
        row = lax.broadcasted_iota(jnp.int32, p_cat.shape, 0)
        scaled = jnp.where(row == z.lat, -jnp.sum(p_cat, axis=0, keepdims=True), p_cat / half)
        table = [term for term in thirds(scaled) for _ in range(z.frames)]
        spare = jnp.zeros((LANES - 24 * z.frames, z.wide), F32)
        table = jnp.concatenate(table + [spare], axis=0).astype(BF16)
        position_codes(z, codes, pos)

        def block(r0, rows):
            place = rows_from(r0, rows, z)
            taps[pl.ds(r0 + 1, rows)] = dot(pos[place], table, NN).reshape(rows, z.row, z.wide)

        in_blocks(z, block)
        activate(z, taps, hid_cat, slope)
        by_tap = [
            keep_own(z, lanes_down(p_cat[:, block * LANES : (block + 1) * LANES], offset))
            for block, offset in spots(9, z.own)
        ]
        by_tap = jnp.concatenate(by_tap + [jnp.zeros((LANES - 72, LANES), F32)], axis=0)
        table_out[...] = sum(
            lanes_down(term, -c * z.own) for c, term in enumerate(thirds(by_tap)[: z.copies])
        )

    @pl.when(jnp.logical_not(decoder))
    def _():
        weights = dot(proj[...], wt[...], NT)[:8]
        table_out[:8] = weights[:, :LANES]
        table_out[8:16] = weights[:, LANES:] if z.thin > LANES else weights


def back_weights(z, table):
    if z.thin > LANES:
        return jnp.concatenate([table[:8], table[8:16]], axis=1)
    return table[:8]


def first_kernel(z, steps, *refs):
    n = z.sp
    shards, (w_cat, wt, proj, table, rate) = refs[:n], refs[n : n + 5]
    part, hid_cat, slope, inner_out, v = refs[n + 5 : n + 10]
    taps, back, spots_of, thin = refs[n + 10 :]
    decoder = lax.axis_index("sec") == 1
    first = lax.axis_index("sp") == 0
    place_shards(z, steps, shards, v)

    @pl.when(decoder)
    def _():
        zero_ends(z, back)
        by_tap = table[...].astype(BF16)

        def block(r0, rows):
            place = rows_from(r0, rows, z)
            thin[place] = dot(v[place], wt[...], NT)

        in_blocks(z, block)

        def body(r):
            inner = keep_own(z, (later_row(z, thin, r) * rate[r]).astype(BF16).astype(F32))
            inner_out[r] = inner.astype(BF16)
            many = sum(lanes_down(inner, -c * z.own) for c in range(z.copies))
            back[r + 1] = dot(many.astype(BF16), by_tap, NT)

        each_row(z, body)
        block_of, offset = (3 * z.own) // LANES, (3 * z.own) % LANES

        def collect(r):
            lane = lax.broadcasted_iota(jnp.int32, (z.row, LANES), 1)
            value = jnp.where(lane < 24, back[r + 2], jnp.where(lane < 48, back[r + 1], back[r]))
            j = (lane // 8) % 3
            moved = jnp.where(
                j == 0,
                col_move(value, -1, z.cols),
                jnp.where(j == 1, value, col_move(value, 1, z.cols)),
            )
            whole = thin[rows_at(r, z), block_of * LANES : (block_of + 1) * LANES]
            whole = jnp.where(first, lanes_down(whole, offset - 72), 0.0)
            spots_of[rows_at(r, z)] = jnp.where(lane < 72, moved, whole)

        each_row(z, collect)
        turned = spots_of[...].T
        part[...] = sum(turned[8 * g : 8 * g + 8] for g in range(10))

    @pl.when(jnp.logical_not(decoder))
    def _():
        zero_ends(z, taps)

        def block(r0, rows):
            place = rows_from(r0, rows, z)
            taps[pl.ds(r0 + 1, rows)] = dot(v[place], w_cat[...], NN).reshape(
                rows, z.row, z.wide
            )

        in_blocks(z, block)
        activate(z, taps, hid_cat, slope)
        weights = back_weights(z, table)
        whole = dot(proj[...], v[...], NT)[:8]
        part[...] = sum3(dot(stack3(weights), hid_cat[...], NT)) + jnp.where(first, whole, 0.0)


def second_kernel(z, scale, *refs):
    v, w_cat, pos, wt, proj, halves, table, hid_dec, hid_cat, slope, inner_in, total, received = refs[:13]
    big, send, time, part = refs[13:17]
    shifts, inner_cat, thin = refs[17:]
    core = lax.axis_index("dp")
    decoder = lax.axis_index("sec") == 1
    first = lax.axis_index("sp") == 0
    for j in range(3):
        zero_ends(z, shifts.at[j])

    def put_out(kernel_grad, proj_part):
        part[...] = proj_part
        side = z.wide - LANES
        if z.carries:
            pieces = []
            for b in range(2 * z.chans // LANES):
                block = proj_part[:, (b // 2) * LANES : (b // 2 + 1) * LANES]
                pieces.append(block if b % 2 else pltpu.roll(block, LANES // 2, 1))
            carried = jnp.concatenate(pieces, axis=0)
            lane = lax.broadcasted_iota(jnp.int32, carried.shape, 1)
        for j in range(z.sp):
            rows = kernel_grad[j * z.own : (j + 1) * z.own]
            if z.carries:
                tail = jnp.where(lane < LANES // 2, rows[:, side:], carried)
                rows = jnp.concatenate([rows[:, :side], tail], axis=1) if side else tail
            if z.split:
                big[j] = jnp.where(core == 0, rows[: z.half], rows[z.half :])
                send[j] = jnp.where(core == 0, rows[z.half :], rows[: z.half]).astype(BF16)
            else:
                big[j] = rows

    @pl.when(decoder)
    def _():
        def body(r):
            put_shifts(z, inner_in[r].astype(F32), shifts, r)

        each_row(z, body)
        spread(z, shifts, inner_cat)
        half = halves[:8, :1]

        def latent_rows(raw):
            row = lax.broadcasted_iota(jnp.int32, raw.shape, 0)
            return jnp.where(row < z.lat, raw / half - raw[z.lat : z.lat + 1], 0.0)

        short = latent_rows(frame_sum(z, dot(pos[...], inner_cat[...], TN)))
        proj8 = proj[...].astype(F32)[:8]
        proj24 = jnp.concatenate([proj8] * 3, axis=0).astype(BF16)
        kernel_grad = dot(proj24, stack3(short), TN) * scale
        time[...] = dot(hid_dec[...], v[...], TN)[: 3 * z.own] * scale
        whole = latent_rows(frame_sum(z, dot(pos[...], v[...], TN)))
        partial = sum3(dot(stack3(short), w_cat[...], NT))
        put_out(kernel_grad, (partial + jnp.where(first, whole, 0.0)) * scale)

    @pl.when(jnp.logical_not(decoder))
    def _():
        bounded = jnp.tanh(total[...])
        grad = received[...] * (1.0 - bounded * bounded)
        back = back_weights(z, table)
        gh, gm, gl = thirds(grad)
        bh, bm, bl = thirds(back)
        left = jnp.concatenate([gh, gh, gm, gh, gl, gm], axis=0).astype(BF16)
        right = jnp.concatenate([bh, bm, bh, bl, bh, bm], axis=0).astype(BF16)
        thin[...] = dot(left, right, TN)

        def body(r):
            inner = keep_own(z, later_row(z, thin, r) * slope[r])
            put_shifts(z, inner, shifts, r)

        each_row(z, body)
        spread(z, shifts, inner_cat)
        kernel_grad = dot(v[...], inner_cat[...], TN) * scale
        grad3 = jnp.concatenate([gh, gm, gl], axis=0).astype(BF16)
        short = sum3(dot(grad3, hid_cat[...], NN))
        short3 = stack3(short)
        proj8 = proj[...].astype(F32)[:8]
        proj24 = jnp.concatenate([proj8] * 3, axis=0).astype(BF16)
        time[...] = dot(short3, proj24, TN)[: 3 * z.own] * scale
        whole = sum3(dot(grad3, v[...], NN))
        partial = sum3(dot(short3, wt[...], NN))
        put_out(kernel_grad, (partial + jnp.where(first, whole, 0.0)) * scale)


def meet_kernel(mine, other, both):
    both[...] = (mine[...] + other[...].astype(F32)).astype(BF16)


def last_kernel(z, mine, other, time_mine, time_other, space, time, part):
    time[...] = time_mine[...] + time_other[...]
    core = lax.axis_index("dp")
    per = LANES // z.own
    if z.split:
        low = pl.ds(pl.multiple_of(core * z.half, z.half), z.half)
        high = pl.ds(pl.multiple_of((1 - core) * z.half, z.half), z.half)
        sources = ((low, lambda at: mine[at].astype(F32)), (high, lambda at: other[at].astype(F32)))
    else:
        sources = ((slice(0, z.own), lambda at: mine[at].astype(F32) + other[at].astype(F32)),)
    for rows, source in sources:
        for tap, (block, offset) in enumerate(spots(9, z.own)):
            for m in range(z.chans // LANES):
                total = None
                for p in range(per):
                    at = (m * per + p, slice(None), slice(block * LANES, (block + 1) * LANES))
                    value = lanes_down(source(at), offset - p * z.own)
                    if total is None:
                        total = value
                    else:
                        lane = lax.broadcasted_iota(jnp.int32, value.shape, 1)
                        total = jnp.where(lane < p * z.own, total, value)
                space[tap, rows, m * LANES : (m + 1) * LANES] = total
    if z.carries:
        side = slice(z.wide - LANES, z.wide)
        one, two = (
            sum(source[j, :, side].astype(F32) for j in range(z.sp)) for source in (mine, other)
        )
        if z.split:
            carried = jnp.concatenate(
                [jnp.where(core == 0, one, two), jnp.where(core == 0, two, one)], axis=0
            )
        else:
            carried = one + two
        lane = lax.broadcasted_iota(jnp.int32, (8, LANES), 1)
        for m in range(z.chans // LANES):
            low = pltpu.roll(carried[16 * m : 16 * m + 8], LANES // 2, 1)
            high = carried[16 * m + 8 : 16 * m + 16]
            both = jnp.where(lane < LANES // 2, low, high)
            for l in range(z.lat):
                part[l, :, m * LANES : (m + 1) * LANES] = both[l : l + 1]
    else:
        part[...] = jnp.zeros(part.shape, F32)


VM = pl.BlockSpec(memory_space=pltpu.VMEM)


def shaped(shape, dtype):
    return jax.ShapeDtypeStruct(shape, dtype)


def local(block_data, code_index, levels, w_space, w_time, enc_proj, dec_proj):
    frames, cols, chans = block_data.shape[2], block_data.shape[4], block_data.shape[5]
    lat, own = code_index.shape[1], w_space.shape[2]
    z = Sizes(lax.axis_size("sp"), frames, cols, chans, own, lat)
    scale = float(lax.axis_size("dp") * z.count) ** (-0.5)
    decoder = lax.axis_index("sec") == 1
    room = 20 * 1024 * 1024 + 5 * z.count * chans * 4 // 2 * (1 if z.sp > 8 else 0)
    params = pltpu.CompilerParams(vmem_limit_bytes=min(room, 60 * 1024 * 1024))

    codes = jnp.transpose(code_index[0, :, :, 0].astype(F32), (2, 1, 0))
    codes = jnp.concatenate([codes, jnp.ones((cols, frames, 1), F32)], axis=2)
    codes = jnp.pad(codes, ((0, 0), (0, 0), (0, 7 - lat))).reshape(cols, 8 * frames)
    left = z.code_lane % LANES
    code_rows = z.half if z.code_row == 0 else z.code_rows
    codes = jnp.pad(codes, ((0, code_rows - cols), (left, LANES - left - 8 * frames)))
    pairs = pl.pallas_call(
        functools.partial(piece_kernel, z),
        out_shape=[shaped((2, z.piece_rows, z.wide), BF16)] * (z.sp // 2),
        in_specs=[VM] * 2,
        out_specs=[VM] * (z.sp // 2),
        compiler_params=params,
        name="pieces",
    )(w_space[0], codes)
    shards, steps = ring_gather(block_data.reshape(z.row, chans))
    pieces = exchange_pieces(pairs, shards)
    proj = jnp.pad(jnp.where(decoder, dec_proj, enc_proj), ((0, 16 - lat), (0, 0)))
    wt = jnp.concatenate([w_time.reshape(3 * own, chans), proj[:8]], axis=0)
    wt = jnp.pad(wt, ((0, z.thin - 3 * own - 8), (0, 0)))
    half = jnp.pad((levels.astype(F32) - 1.0) * 0.5, (0, 16 - lat), constant_values=1.0)
    halves = jnp.broadcast_to(half[:, None], (16, LANES))

    w_cat, pos, hid_dec, rate, table = pl.pallas_call(
        functools.partial(early_kernel, z),
        out_shape=(
            shaped((chans, z.wide), BF16),
            shaped((z.count, LANES), BF16),
            shaped((z.count, z.thin), BF16),
            shaped((z.sp, z.row, LANES), F32),
            shaped((LANES, LANES), F32),
        ),
        in_specs=[VM] * 7,
        out_specs=(VM,) * 5,
        scratch_shapes=[
            pltpu.VMEM((z.sp, z.code_rows, z.wide), BF16),
            pltpu.VMEM((z.sp + 2, z.row, z.wide), F32),
        ],
        compiler_params=params,
        name="early",
    )(*pieces, wt, proj, halves)
    part, hid_cat, slope, inner, v = pl.pallas_call(
        functools.partial(first_kernel, z, steps),
        out_shape=(
            shaped((8, z.count), F32),
            shaped((z.count, z.thin), BF16),
            shaped((z.sp, z.row, LANES), F32),
            shaped((z.sp, z.row, LANES), BF16),
            shaped((z.count, chans), BF16),
        ),
        in_specs=[VM] * (z.sp + 5),
        out_specs=(VM,) * 5,
        scratch_shapes=[
            pltpu.VMEM((z.sp + 2, z.row, z.wide), F32),
            pltpu.VMEM((z.sp + 2, z.row, LANES), F32),
            pltpu.VMEM((z.count, LANES), F32),
            pltpu.VMEM((z.count, z.thin), F32),
        ],
        compiler_params=params,
        name="first",
    )(*shards, w_cat, wt, proj, table, rate)
    total, received = sum_and_cross(part)
    part_rows = (z.sp, z.half if z.split else own, z.wide)
    big, send, time, part = pl.pallas_call(
        functools.partial(second_kernel, z, scale),
        out_shape=(
            shaped(part_rows, F32),
            shaped(part_rows, BF16),
            shaped((3 * own, chans), F32),
            shaped((8, chans), F32),
        ),
        in_specs=[VM] * 13,
        out_specs=(VM,) * 4,
        scratch_shapes=[
            pltpu.VMEM((3, z.sp + 2, z.row, LANES), BF16),
            pltpu.VMEM((z.count, z.wide), BF16),
            pltpu.VMEM((z.count, z.thin), F32),
        ],
        compiler_params=params,
        name="second",
    )(v, w_cat, pos, wt, proj, halves, table, hid_dec, hid_cat, slope, inner, total, received)
    if z.split:
        big = pl.pallas_call(
            meet_kernel,
            out_shape=shaped(part_rows, BF16),
            in_specs=[VM] * 2,
            out_specs=VM,
            compiler_params=params,
            name="meet",
        )(big, swap_core(send))
    big = lax.all_to_all(big.astype(BF16), "sp", 0, 0, tiled=True)
    space, time, carried = pl.pallas_call(
        functools.partial(last_kernel, z),
        out_shape=(
            shaped((9, own, chans), F32),
            shaped((3 * own, chans), F32),
            shaped((lat, 1, chans), F32),
        ),
        in_specs=[VM] * 4,
        out_specs=(VM,) * 3,
        compiler_params=params,
        name="last",
    )(big, swap_core(big), time, swap_core(time))
    if z.carries:
        part = carried.reshape(lat, chans)
    else:
        part = sum_pairs(part, [1 << b for b in range(z.sp.bit_length() - 1)])
        part = (part + swap_core(part))[:lat]
    return space[None], time.reshape(1, 3, own, chans), part[None]


def solution(mesh):
    placed = (
        P("sec", "dp", None, "sp", None, None),
        P("dp", None, None, "sp", None),
        P(),
        P("sec", None, "sp", None),
        P("sec", None, "sp", None),
        P(),
        P(),
    )
    return jax.shard_map(
        local,
        mesh=mesh,
        in_specs=placed,
        out_specs=(P("sec", None, "sp", None), P("sec", None, "sp", None), P("sec", None, None)),
        check_vma=False,
    )
```

```python
import functools

import jax
import jax.numpy as jnp
from jax import lax
from jax.experimental import pallas as pl
from jax.experimental.pallas import tpu as pltpu
from jax.sharding import PartitionSpec as P

F32 = jnp.float32
BF16 = jnp.bfloat16
LANES = 128
NN = (((1,), (0,)), ((), ()))
NT = (((1,), (1,)), ((), ()))
TN = (((0,), (0,)), ((), ()))


def up_to(value, multiple):
    return -(-value // multiple) * multiple


def ring_place(index, count):
    return jnp.where(index % 2 == 0, index // 2, count - (index + 1) // 2)


def ring_device(place, count):
    place = lax.rem(place + 2 * count, count)
    return jnp.where(place < count // 2, 2 * place, 2 * (count - place) - 1)


def ring_maps(count):
    order = list(range(0, count, 2)) + list(range(count - 1, 0, -2))
    forward = [(order[i], order[(i + 1) % count]) for i in range(count)]
    return forward, [(target, source) for source, target in forward]


def ring_gather(shard):
    count = lax.axis_size("sp")
    up, down = ring_maps(count)
    shards, steps = [shard], [0]
    first = second = shard
    for step in range(1, count // 2 + 1):
        if step < count - step:
            second = lax.ppermute(second, "sp", down)
        first = lax.ppermute(first, "sp", up)
        shards.append(first)
        steps.append(-step)
        if step < count - step:
            shards.append(second)
            steps.append(step)
    return shards, steps


def exchange_pieces(pairs, shards):
    arrived = [pairs[0]] + [swap(pair, 2 * k) for k, pair in enumerate(pairs) if k]
    arrived = lax.optimization_barrier((arrived, shards[3]))[0]
    even = jnp.stack([pair[0] for pair in arrived])
    odd = swap(jnp.stack([pair[1] for pair in arrived]), 1)
    return even, odd, swap_core(even), swap_core(odd)


def swap(values, distance):
    count = lax.axis_size("sp")
    return lax.ppermute(values, "sp", [(i, i ^ distance) for i in range(count)])


def swap_core(values):
    return lax.ppermute(values, "dp", [(0, 1), (1, 0)])


def sum_pairs(values, bits):
    bits = list(bits)
    while bits:
        if len(bits) == 1:
            values = values + swap(values, bits.pop())
        else:
            one, two = bits.pop(0), bits.pop(0)
            values = values + (swap(values, one) + swap(values, two) + swap(values, one | two))
    return values


def sum_and_cross(values):
    count, sections = lax.axis_size("sp"), lax.axis_size("sec")
    bits = [1 << b for b in range(count.bit_length() - 1)]
    values = sum_pairs(values, bits[1:])
    beside = swap(values, 1)
    across = lax.ppermute(values, "sec", [(0, 1), (1, 0)])
    corner = lax.ppermute(
        values,
        ("sec", "sp"),
        [(s * count + i, (1 - s) * count + (i ^ 1)) for s in range(sections) for i in range(count)],
    )
    return values + beside, across + corner


def dot(left, right, dims):
    return lax.dot_general(left, right, dims, preferred_element_type=F32)


def thirds(values):
    high = values.astype(BF16).astype(F32)
    rest = values - high
    middle = rest.astype(BF16).astype(F32)
    return high, middle, rest - middle


def stack3(values):
    return jnp.concatenate(thirds(values), axis=0).astype(BF16)


def sum3(stacked):
    rows = stacked.shape[0] // 3
    return stacked[:rows] + stacked[rows : 2 * rows] + stacked[2 * rows :]


def lanes_down(values, by):
    by = by % LANES
    return values if by == 0 else pltpu.roll(values, LANES - by, 1)


def spots(parts, own):
    return [((p * own) // LANES, (p * own) % LANES) for p in range(parts)]


def col_move(values, by, cols):
    if by == 0:
        return values
    rows = values.shape[0]
    col = lax.broadcasted_iota(jnp.int32, values.shape, 0) % cols
    edge = 0 if by > 0 else cols - 1
    return jnp.where(col == edge, 0.0, pltpu.roll(values, by % rows, 0))


def frames_move(values, by, cols):
    if by == 0:
        return values
    zeros = jnp.zeros((abs(by) * cols, values.shape[1]), values.dtype)
    if by > 0:
        return jnp.concatenate([zeros, values[: -by * cols]], axis=0)
    return jnp.concatenate([values[-by * cols :], zeros], axis=0)


def merge(pieces, own):
    blocks = [None] * (spots(len(pieces), own)[-1][0] + 1)
    for piece, (block, offset) in zip(pieces, spots(len(pieces), own)):
        moved = lanes_down(piece, -offset)
        blocks[block] = moved if blocks[block] is None else blocks[block] + moved
    return blocks


class Sizes:
    def __init__(self, sp, frames, cols, chans, own, lat):
        self.sp, self.frames, self.cols = sp, frames, cols
        self.chans, self.own, self.lat = chans, own, lat
        self.row = frames * cols
        self.count = sp * self.row
        self.wide = up_to(9 * own, LANES)
        self.thin = up_to(3 * own + 8, LANES)
        self.copies = min(3, LANES // own)
        self.half = own // 2
        self.half_pad = up_to(self.half, 16)
        self.code_rows = up_to(cols, 16)
        if self.wide - 9 * own >= 8 * frames and self.half >= cols:
            self.code_row, self.code_lane = 0, 9 * own
            self.piece_rows = self.half
        else:
            self.code_row, self.code_lane = self.half_pad, 0
            self.piece_rows = self.code_row + self.code_rows
        self.split = self.half == self.half_pad
        self.carries = self.wide - 9 * own >= LANES // 2 and own * (LANES // 2) >= 8 * chans


def place_shards(z, steps, shards, v):
    place = ring_place(lax.axis_index("sp"), z.sp)
    for shard, step in zip(shards, steps):
        v[rows_at(ring_device(place + step, z.sp), z)] = shard[...]


def place_pieces(z, even, odd, even_other, odd_other, w_cat, codes):
    me, core = lax.axis_index("sp"), lax.axis_index("dp")
    for distance in range(z.sp):
        mine, other = ((even, even_other), (odd, odd_other))[distance % 2]
        device = lax.bitwise_xor(me, distance)
        start = pl.multiple_of(device * z.own, z.own)
        at = distance // 2
        codes[device] = mine[at, z.code_row : z.code_row + z.code_rows]
        one, two = mine[at, : z.half], other[at, : z.half]
        low, high = jnp.where(core == 0, one, two), jnp.where(core == 0, two, one)
        if z.split:
            w_cat[pl.ds(start, z.half)] = low
            w_cat[pl.ds(start + z.half, z.half)] = high
        else:
            both = jnp.concatenate([low.astype(F32), high.astype(F32)], axis=0)
            w_cat[pl.ds(start, z.own)] = both.astype(BF16)


def each_row(z, body):
    if z.sp <= 8:
        for r in range(z.sp):
            body(r)
    else:

        def step(r, carry):
            body(r)
            return carry

        lax.fori_loop(0, z.sp, step, 0)


def rows_at(r, z):
    if isinstance(r, int):
        return pl.ds(r * z.row, z.row)
    return pl.ds(pl.multiple_of(r * z.row, z.row), z.row)


def rows_from(r0, rows, z):
    if isinstance(r0, int):
        return pl.ds(r0 * z.row, rows * z.row)
    return pl.ds(pl.multiple_of(r0 * z.row, rows * z.row), rows * z.row)


def conv_row(z, taps, r):
    total = None
    for j in range(3):
        by_offset = {}
        for i in range(3):
            block, offset = spots(9, z.own)[3 * i + j]
            value = taps[r + i, :, block * LANES : (block + 1) * LANES]
            by_offset[offset] = by_offset.get(offset, 0.0) + value
        column = sum(lanes_down(value, offset) for offset, value in by_offset.items())
        column = col_move(column, 1 - j, z.cols)
        total = column if total is None else total + column
    return total


def later_row(z, taps, r):
    total = None
    for k, (block, offset) in enumerate(spots(3, z.own)):
        value = taps[rows_at(r, z), block * LANES : (block + 1) * LANES]
        value = frames_move(lanes_down(value, offset), -k, z.cols)
        total = value if total is None else total + value
    return total


def keep_own(z, values):
    lane = lax.broadcasted_iota(jnp.int32, values.shape, 1)
    return jnp.where(lane < z.own, values, 0.0)


def put_shifts(z, inner, shifts, r):
    for j in range(3):
        shifts[j, r + 1] = col_move(inner, j - 1, z.cols).astype(BF16)


def spread(z, shifts, inner_cat):
    def body(r):
        pieces = [
            shifts[j, r + 2 - i].astype(F32) for i in range(3) for j in range(3)
        ]
        for b, block in enumerate(merge(pieces, z.own)):
            inner_cat[rows_at(r, z), b * LANES : (b + 1) * LANES] = block.astype(BF16)

    each_row(z, body)


def zero_ends(z, padded):
    padded[0] = jnp.zeros(padded.shape[1:], padded.dtype)
    padded[z.sp + 1] = jnp.zeros(padded.shape[1:], padded.dtype)


def in_blocks(z, action):
    step = 8 if z.sp % 8 == 0 else 1
    if z.sp == step:
        action(0, step)
    else:

        def body(b, carry):
            action(b * step, step)
            return carry

        lax.fori_loop(0, z.sp // step, body, 0)


def position_codes(z, codes, out):
    block, offset = z.code_lane // LANES, z.code_lane % LANES
    run = 8 * z.frames

    def body(r):
        raw = codes[r, : z.cols, block * LANES : (block + 1) * LANES].astype(F32)
        lane = lax.broadcasted_iota(jnp.int32, raw.shape, 1)
        raw = jnp.where(lane < run, lanes_down(raw, offset), 0.0)
        raw = raw + pltpu.roll(raw, run, 1) + pltpu.roll(raw, 2 * run, 1)
        frame = (lane % run) // 8
        blocks = [jnp.where(frame == t, raw, 0.0) for t in range(z.frames)]
        out[rows_at(r, z)] = jnp.concatenate(blocks, axis=0).astype(BF16)

    each_row(z, body)


def frame_sum(z, raw):
    return sum(raw[8 * t : 8 * t + 8] for t in range(z.frames))


def piece_kernel(z, w, codes, *pairs):
    me = lax.axis_index("sp")
    core = lax.axis_index("dp")
    lane = lax.broadcasted_iota(jnp.int32, (z.half, LANES), 1)
    code_rows = []
    for t in range(z.frames):
        code_rows += [codes[l * z.frames + t] for l in range(z.lat)]
        code_rows += [jnp.ones((1, z.cols), jnp.int32), jnp.zeros((7 - z.lat, z.cols), jnp.int32)]
    code_rows.append(jnp.zeros((LANES - 8 * z.frames, z.cols), jnp.int32))
    code_block = jnp.concatenate(code_rows, axis=0).astype(F32)
    code_block = jnp.concatenate([code_block, jnp.zeros((LANES, LANES - z.cols), F32)], axis=1)
    code_block = code_block.T[: z.half if z.code_row == 0 else z.code_rows]
    code_block = lanes_down(code_block, -z.code_lane)
    for distance in range(z.sp):
        begin = lax.bitwise_xor(me, distance) * z.own
        block, offset = begin // LANES, begin % LANES
        at = pl.ds(pl.multiple_of(block * LANES, LANES), LANES)
        taps = []
        for tap in range(9):
            if z.split:
                value = w[tap, pl.ds(pl.multiple_of(core * z.half, z.half), z.half), at]
                value = value.astype(F32)
            else:
                value = w[tap, :, at].astype(F32)
                value = jnp.where(core == 0, value[: z.half], value[z.half :])
            value = pltpu.roll(value, (LANES - offset) % LANES, 1)
            taps.append(jnp.where(lane < z.own, value, 0.0))
        blocks = merge(taps, z.own)
        if z.code_row == 0:
            blocks[-1] = blocks[-1] + code_block
        target = pairs[distance // 2]
        for b, value in enumerate(blocks):
            lanes = slice(b * LANES, (b + 1) * LANES)
            target[distance % 2, : z.half, lanes] = value.astype(BF16)
        if z.code_row:
            target[distance % 2, z.code_row : z.piece_rows, :LANES] = code_block.astype(BF16)


def store_hidden(z, pre, logistic, hid_cat, r):
    hidden = keep_own(z, (pre * logistic).astype(BF16).astype(F32))
    moved = [frames_move(hidden, k, z.cols) for k in range(3)]
    for b, block in enumerate(merge(moved, z.own)):
        hid_cat[rows_at(r, z), b * LANES : (b + 1) * LANES] = block.astype(BF16)


def activate(z, taps, hid_cat, slope):
    def body(r):
        pre = conv_row(z, taps, r)
        logistic = 1.0 / (1.0 + jnp.exp(-pre))
        store_hidden(z, pre, logistic, hid_cat, r)
        slope[r] = logistic * (1.0 + pre * (1.0 - logistic))

    each_row(z, body)


def early_kernel(z, *refs):
    wt, proj, halves = refs[4:7]
    w_cat, pos, hid_cat, slope, table_out = refs[7:12]
    codes, taps = refs[12:]
    decoder = lax.axis_index("sec") == 1
    place_pieces(z, *refs[:4], w_cat, codes)

    @pl.when(decoder)
    def _():
        zero_ends(z, taps)
        p_cat = dot(proj[...], w_cat[...], NN)[:8]
        half = halves[:8, :1]
        row = lax.broadcasted_iota(jnp.int32, p_cat.shape, 0)
        scaled = jnp.where(row == z.lat, -jnp.sum(p_cat, axis=0, keepdims=True), p_cat / half)
        table = [term for term in thirds(scaled) for _ in range(z.frames)]
        spare = jnp.zeros((LANES - 24 * z.frames, z.wide), F32)
        table = jnp.concatenate(table + [spare], axis=0).astype(BF16)
        position_codes(z, codes, pos)

        def block(r0, rows):
            place = rows_from(r0, rows, z)
            taps[pl.ds(r0 + 1, rows)] = dot(pos[place], table, NN).reshape(rows, z.row, z.wide)

        in_blocks(z, block)
        activate(z, taps, hid_cat, slope)
        by_tap = [
            keep_own(z, lanes_down(p_cat[:, block * LANES : (block + 1) * LANES], offset))
            for block, offset in spots(9, z.own)
        ]
        by_tap = jnp.concatenate(by_tap + [jnp.zeros((LANES - 72, LANES), F32)], axis=0)
        table_out[...] = sum(
            lanes_down(term, -c * z.own) for c, term in enumerate(thirds(by_tap)[: z.copies])
        )

    @pl.when(jnp.logical_not(decoder))
    def _():
        weights = dot(proj[...], wt[...], NT)[:8]
        table_out[:8] = weights[:, :LANES]
        table_out[8:16] = weights[:, LANES:] if z.thin > LANES else weights


def back_weights(z, table):
    if z.thin > LANES:
        return jnp.concatenate([table[:8], table[8:16]], axis=1)
    return table[:8]


def first_kernel(z, steps, *refs):
    n = z.sp
    shards, (w_cat, wt, proj, table, rate) = refs[:n], refs[n : n + 5]
    part, hid_cat, slope, inner_out, v = refs[n + 5 : n + 10]
    taps, back, spots_of, thin = refs[n + 10 :]
    decoder = lax.axis_index("sec") == 1
    first = lax.axis_index("sp") == 0
    place_shards(z, steps, shards, v)

    @pl.when(decoder)
    def _():
        zero_ends(z, back)
        by_tap = table[...].astype(BF16)

        def block(r0, rows):
            place = rows_from(r0, rows, z)
            thin[place] = dot(v[place], wt[...], NT)

        in_blocks(z, block)

        def body(r):
            inner = keep_own(z, (later_row(z, thin, r) * rate[r]).astype(BF16).astype(F32))
            inner_out[r] = inner.astype(BF16)
            many = sum(lanes_down(inner, -c * z.own) for c in range(z.copies))
            back[r + 1] = dot(many.astype(BF16), by_tap, NT)

        each_row(z, body)
        block_of, offset = (3 * z.own) // LANES, (3 * z.own) % LANES

        def collect(r):
            lane = lax.broadcasted_iota(jnp.int32, (z.row, LANES), 1)
            value = jnp.where(lane < 24, back[r + 2], jnp.where(lane < 48, back[r + 1], back[r]))
            j = (lane // 8) % 3
            moved = jnp.where(
                j == 0,
                col_move(value, -1, z.cols),
                jnp.where(j == 1, value, col_move(value, 1, z.cols)),
            )
            whole = thin[rows_at(r, z), block_of * LANES : (block_of + 1) * LANES]
            whole = jnp.where(first, lanes_down(whole, offset - 72), 0.0)
            spots_of[rows_at(r, z)] = jnp.where(lane < 72, moved, whole)

        each_row(z, collect)
        turned = spots_of[...].T
        part[...] = sum(turned[8 * g : 8 * g + 8] for g in range(10))

    @pl.when(jnp.logical_not(decoder))
    def _():
        zero_ends(z, taps)

        def block(r0, rows):
            place = rows_from(r0, rows, z)
            taps[pl.ds(r0 + 1, rows)] = dot(v[place], w_cat[...], NN).reshape(
                rows, z.row, z.wide
            )

        in_blocks(z, block)
        activate(z, taps, hid_cat, slope)
        weights = back_weights(z, table)
        whole = dot(proj[...], v[...], NT)[:8]
        part[...] = sum3(dot(stack3(weights), hid_cat[...], NT)) + jnp.where(first, whole, 0.0)


def second_kernel(z, scale, *refs):
    v, w_cat, pos, wt, proj, halves, table, hid_dec, hid_cat, slope, inner_in, total, received = refs[:13]
    big, send, time, part = refs[13:17]
    shifts, inner_cat, thin = refs[17:]
    core = lax.axis_index("dp")
    decoder = lax.axis_index("sec") == 1
    first = lax.axis_index("sp") == 0
    for j in range(3):
        zero_ends(z, shifts.at[j])

    def put_out(kernel_grad, proj_part):
        part[...] = proj_part
        side = z.wide - LANES
        if z.carries:
            pieces = []
            for b in range(2 * z.chans // LANES):
                block = proj_part[:, (b // 2) * LANES : (b // 2 + 1) * LANES]
                pieces.append(block if b % 2 else pltpu.roll(block, LANES // 2, 1))
            carried = jnp.concatenate(pieces, axis=0)
            lane = lax.broadcasted_iota(jnp.int32, carried.shape, 1)
        for j in range(z.sp):
            rows = kernel_grad[j * z.own : (j + 1) * z.own]
            if z.carries:
                tail = jnp.where(lane < LANES // 2, rows[:, side:], carried)
                rows = jnp.concatenate([rows[:, :side], tail], axis=1) if side else tail
            if z.split:
                big[j] = jnp.where(core == 0, rows[: z.half], rows[z.half :])
                send[j] = jnp.where(core == 0, rows[z.half :], rows[: z.half]).astype(BF16)
            else:
                big[j] = rows

    @pl.when(decoder)
    def _():
        def body(r):
            put_shifts(z, inner_in[r].astype(F32), shifts, r)

        each_row(z, body)
        spread(z, shifts, inner_cat)
        half = halves[:8, :1]

        def latent_rows(raw):
            row = lax.broadcasted_iota(jnp.int32, raw.shape, 0)
            return jnp.where(row < z.lat, raw / half - raw[z.lat : z.lat + 1], 0.0)

        short = latent_rows(frame_sum(z, dot(pos[...], inner_cat[...], TN)))
        proj8 = proj[...].astype(F32)[:8]
        proj24 = jnp.concatenate([proj8] * 3, axis=0).astype(BF16)
        kernel_grad = dot(proj24, stack3(short), TN) * scale
        time[...] = dot(hid_dec[...], v[...], TN)[: 3 * z.own] * scale
        whole = latent_rows(frame_sum(z, dot(pos[...], v[...], TN)))
        partial = sum3(dot(stack3(short), w_cat[...], NT))
        put_out(kernel_grad, (partial + jnp.where(first, whole, 0.0)) * scale)

    @pl.when(jnp.logical_not(decoder))
    def _():
        bounded = jnp.tanh(total[...])
        grad = received[...] * (1.0 - bounded * bounded)
        back = back_weights(z, table)
        gh, gm, gl = thirds(grad)
        bh, bm, bl = thirds(back)
        left = jnp.concatenate([gh, gh, gm, gh, gl, gm], axis=0).astype(BF16)
        right = jnp.concatenate([bh, bm, bh, bl, bh, bm], axis=0).astype(BF16)
        thin[...] = dot(left, right, TN)

        def body(r):
            inner = keep_own(z, later_row(z, thin, r) * slope[r])
            put_shifts(z, inner, shifts, r)

        each_row(z, body)
        spread(z, shifts, inner_cat)
        kernel_grad = dot(v[...], inner_cat[...], TN) * scale
        grad3 = jnp.concatenate([gh, gm, gl], axis=0).astype(BF16)
        short = sum3(dot(grad3, hid_cat[...], NN))
        short3 = stack3(short)
        proj8 = proj[...].astype(F32)[:8]
        proj24 = jnp.concatenate([proj8] * 3, axis=0).astype(BF16)
        time[...] = dot(short3, proj24, TN)[: 3 * z.own] * scale
        whole = sum3(dot(grad3, v[...], NN))
        partial = sum3(dot(short3, wt[...], NN))
        put_out(kernel_grad, (partial + jnp.where(first, whole, 0.0)) * scale)


def meet_kernel(mine, other, both):
    both[...] = (mine[...] + other[...].astype(F32)).astype(BF16)


def last_kernel(z, mine, other, time_mine, time_other, space, time, part):
    time[...] = time_mine[...] + time_other[...]
    core = lax.axis_index("dp")
    per = LANES // z.own
    if z.split:
        low = pl.ds(pl.multiple_of(core * z.half, z.half), z.half)
        high = pl.ds(pl.multiple_of((1 - core) * z.half, z.half), z.half)
        sources = ((low, lambda at: mine[at].astype(F32)), (high, lambda at: other[at].astype(F32)))
    else:
        sources = ((slice(0, z.own), lambda at: mine[at].astype(F32) + other[at].astype(F32)),)
    for rows, source in sources:
        for tap, (block, offset) in enumerate(spots(9, z.own)):
            for m in range(z.chans // LANES):
                total = None
                for p in range(per):
                    at = (m * per + p, slice(None), slice(block * LANES, (block + 1) * LANES))
                    value = lanes_down(source(at), offset - p * z.own)
                    if total is None:
                        total = value
                    else:
                        lane = lax.broadcasted_iota(jnp.int32, value.shape, 1)
                        total = jnp.where(lane < p * z.own, total, value)
                space[tap, rows, m * LANES : (m + 1) * LANES] = total
    if z.carries:
        side = slice(z.wide - LANES, z.wide)
        one, two = (
            sum(source[j, :, side].astype(F32) for j in range(z.sp)) for source in (mine, other)
        )
        if z.split:
            carried = jnp.concatenate(
                [jnp.where(core == 0, one, two), jnp.where(core == 0, two, one)], axis=0
            )
        else:
            carried = one + two
        lane = lax.broadcasted_iota(jnp.int32, (8, LANES), 1)
        for m in range(z.chans // LANES):
            low = pltpu.roll(carried[16 * m : 16 * m + 8], LANES // 2, 1)
            high = carried[16 * m + 8 : 16 * m + 16]
            both = jnp.where(lane < LANES // 2, low, high)
            for l in range(z.lat):
                part[l, :, m * LANES : (m + 1) * LANES] = both[l : l + 1]
    else:
        part[...] = jnp.zeros(part.shape, F32)


VM = pl.BlockSpec(memory_space=pltpu.VMEM)


def shaped(shape, dtype):
    return jax.ShapeDtypeStruct(shape, dtype)


def local(block_data, code_index, levels, w_space, w_time, enc_proj, dec_proj):
    frames, cols, chans = block_data.shape[2], block_data.shape[4], block_data.shape[5]
    lat, own = code_index.shape[1], w_space.shape[2]
    z = Sizes(lax.axis_size("sp"), frames, cols, chans, own, lat)
    scale = float(lax.axis_size("dp") * z.count) ** (-0.5)
    decoder = lax.axis_index("sec") == 1
    room = 20 * 1024 * 1024 + 5 * z.count * chans * 4 // 2 * (1 if z.sp > 8 else 0)
    params = pltpu.CompilerParams(vmem_limit_bytes=min(room, 60 * 1024 * 1024))

    codes = code_index.reshape(lat * frames, 1, cols)
    pairs = pl.pallas_call(
        functools.partial(piece_kernel, z),
        out_shape=[shaped((2, z.piece_rows, z.wide), BF16)] * (z.sp // 2),
        in_specs=[VM] * 2,
        out_specs=[VM] * (z.sp // 2),
        compiler_params=params,
        name="pieces",
    )(w_space[0], codes)
    shards, steps = ring_gather(block_data.reshape(z.row, chans))
    pieces = exchange_pieces(pairs, shards)
    proj = jnp.pad(jnp.where(decoder, dec_proj, enc_proj), ((0, 16 - lat), (0, 0)))
    wt = jnp.concatenate([w_time.reshape(3 * own, chans), proj[:8]], axis=0)
    wt = jnp.pad(wt, ((0, z.thin - 3 * own - 8), (0, 0)))
    half = jnp.pad((levels.astype(F32) - 1.0) * 0.5, (0, 16 - lat), constant_values=1.0)
    halves = jnp.broadcast_to(half[:, None], (16, LANES))

    w_cat, pos, hid_dec, rate, table = pl.pallas_call(
        functools.partial(early_kernel, z),
        out_shape=(
            shaped((chans, z.wide), BF16),
            shaped((z.count, LANES), BF16),
            shaped((z.count, z.thin), BF16),
            shaped((z.sp, z.row, LANES), F32),
            shaped((LANES, LANES), F32),
        ),
        in_specs=[VM] * 7,
        out_specs=(VM,) * 5,
        scratch_shapes=[
            pltpu.VMEM((z.sp, z.code_rows, z.wide), BF16),
            pltpu.VMEM((z.sp + 2, z.row, z.wide), F32),
        ],
        compiler_params=params,
        name="early",
    )(*pieces, wt, proj, halves)
    part, hid_cat, slope, inner, v = pl.pallas_call(
        functools.partial(first_kernel, z, steps),
        out_shape=(
            shaped((8, z.count), F32),
            shaped((z.count, z.thin), BF16),
            shaped((z.sp, z.row, LANES), F32),
            shaped((z.sp, z.row, LANES), BF16),
            shaped((z.count, chans), BF16),
        ),
        in_specs=[VM] * (z.sp + 5),
        out_specs=(VM,) * 5,
        scratch_shapes=[
            pltpu.VMEM((z.sp + 2, z.row, z.wide), F32),
            pltpu.VMEM((z.sp + 2, z.row, LANES), F32),
            pltpu.VMEM((z.count, LANES), F32),
            pltpu.VMEM((z.count, z.thin), F32),
        ],
        compiler_params=params,
        name="first",
    )(*shards, w_cat, wt, proj, table, rate)
    total, received = sum_and_cross(part)
    part_rows = (z.sp, z.half if z.split else own, z.wide)
    big, send, time, part = pl.pallas_call(
        functools.partial(second_kernel, z, scale),
        out_shape=(
            shaped(part_rows, F32),
            shaped(part_rows, BF16),
            shaped((3 * own, chans), F32),
            shaped((8, chans), F32),
        ),
        in_specs=[VM] * 13,
        out_specs=(VM,) * 4,
        scratch_shapes=[
            pltpu.VMEM((3, z.sp + 2, z.row, LANES), BF16),
            pltpu.VMEM((z.count, z.wide), BF16),
            pltpu.VMEM((z.count, z.thin), F32),
        ],
        compiler_params=params,
        name="second",
    )(v, w_cat, pos, wt, proj, halves, table, hid_dec, hid_cat, slope, inner, total, received)
    if z.split:
        big = pl.pallas_call(
            meet_kernel,
            out_shape=shaped(part_rows, BF16),
            in_specs=[VM] * 2,
            out_specs=VM,
            compiler_params=params,
            name="meet",
        )(big, swap_core(send))
    big = lax.all_to_all(big.astype(BF16), "sp", 0, 0, tiled=True)
    space, time, carried = pl.pallas_call(
        functools.partial(last_kernel, z),
        out_shape=(
            shaped((9, own, chans), F32),
            shaped((3 * own, chans), F32),
            shaped((lat, 1, chans), F32),
        ),
        in_specs=[VM] * 4,
        out_specs=(VM,) * 3,
        compiler_params=params,
        name="last",
    )(big, swap_core(big), time, swap_core(time))
    if z.carries:
        part = carried.reshape(lat, chans)
    else:
        part = sum_pairs(part, [1 << b for b in range(z.sp.bit_length() - 1)])
        part = (part + swap_core(part))[:lat]
    return space[None], time.reshape(1, 3, own, chans), part[None]


def solution(mesh):
    placed = (
        P("sec", "dp", None, "sp", None, None),
        P("dp", None, None, "sp", None),
        P(),
        P("sec", None, "sp", None),
        P("sec", None, "sp", None),
        P(),
        P(),
    )
    return jax.shard_map(
        local,
        mesh=mesh,
        in_specs=placed,
        out_specs=(P("sec", None, "sp", None), P("sec", None, "sp", None), P("sec", None, None)),
        check_vma=False,
    )
```
